32 devices in a mesh: curve: 8 (over y, x, core), slab: 4 (over z).
Axes of the slice: x: 2, y: 2, z: 4, core: 2. Of those that a mesh axis runs over, the one named last changes fastest.
Arguments:
- start_state: float32 [135, 4096], P(None, ('curve', 'slab')), may hold values from -6 to 6
- right_side: float32 [135, 4096], P(None, ('curve', 'slab')), may hold values from -6 to 6
- block_inverse: float32 [135, 135, 4096], P(None, None, ('curve', 'slab')), as said below
- lifted_flux_jacobian: float32 [6, 135, 45], replicated, may hold values from -0.875 to 0.875
- face_weight: float32 [6, 4096], P(None, ('curve', 'slab')), may hold values from 0.1 to 0.4
- dep_level: int32 [4096], P(('curve', 'slab')), may hold values from 0 to 7
- face_link: int32 [6, 4096], P(None, ('curve', 'slab')), may hold values from -1 to 127, as said below
- send_list: int32 [8, 4096], P(None, ('curve', 'slab')), may hold values from 0 to 768, as said below
- recv_list: int32 [8, 4096], P(None, ('curve', 'slab')), may hold values from 0 to 768, as said below
Outputs:
- forward_state: float32 [135, 4096], P(None, ('curve', 'slab'))
- swept_state: float32 [135, 4096], P(None, ('curve', 'slab'))
The draws below stay inside these ranges and needn't reach their ends.
Inputs may be any that keep to these rules, and one draw needn't show every extreme that they name: `block_inverse`: A dense 135 x 135 matrix for each element. `face_link`: for face d of element k of a device, the index on the same device of the element across that face, or -1 where that element lies on another device or outside the domain; links are mutual. `send_list`: A device's shard holds, for each level, 4 slots for each destination device in order; an entry d * 128 + k names face d of the device's local element k, and 768 marks an empty slot. Non-empty slots go only to devices whose curve index differs from the sender's by at most one. In every draw some device fills all 4 slots to one destination at every level. `recv_list`: A device's shard holds, for each level, 4 slots for each source device in order; slot j from source t names the face index at which t's slot j toward this device arrives, empty (768) exactly where that send slot is empty. Over all levels no face appears twice in one device's shard. Non-empty slots come only from devices whose curve index differs by at most one.
All inputs are finite; a program needn't handle non-finite values.
Results may differ from the reference program's by a relative error of at most 0.0003.
Values sent between devices are 32-bit elements; how exact they have to be, the bound alone decides.
No kernel may reach another device: no remote copies, remote signals or barrier semaphores. Data moves between devices by JAX's collectives and lax.ppermute only.
A program may use at most 64 MiB of HBM per device.

```python
import math
import jax
import jax.numpy as jnp
from jax import lax

VARS = 5
LEVELS = 8
LA = 4
LC = 4
BLOCK = 135
TRACE = 45
EL = 128
CAP = 4
ELEMENTS = 4096
N_CURVE = 8
N_SLAB = 4
DEVICES = 32


def layout(key):
    base = jax.random.fold_in(key, 7)
    shifts = jax.random.randint(jax.random.fold_in(base, 1), (DEVICES, LA, LC), 0, LEVELS).astype(jnp.int32)
    turn_start = jax.random.randint(jax.random.fold_in(base, 2), (1,), 0, N_SLAB).astype(jnp.int32)
    turns = ((jnp.arange(N_CURVE, dtype=jnp.int32) + turn_start) % N_SLAB).astype(jnp.int32)
    scores = jax.random.randint(jax.random.fold_in(base, 3), (DEVICES, EL), 0, 1 << 18).astype(jnp.int32) * EL + jnp.arange(EL, dtype=jnp.int32)[None, :]
    places = jnp.argsort(scores, axis=1).astype(jnp.int32)
    canon = jnp.arange(EL, dtype=jnp.int32)
    coord_b = canon % LEVELS
    coord_a = canon // LEVELS % LA
    coord_c = canon // (LEVELS * LA)
    owners = jnp.arange(DEVICES, dtype=jnp.int32)[:, None]
    levels = jnp.zeros((DEVICES, EL), jnp.int32).at[owners, places].set((coord_b[None, :] + shifts[:, coord_a, coord_c]) % LEVELS)
    coords = (coord_a, coord_b, coord_c)
    extents = (LA, LEVELS, LC)
    strides = (LEVELS, 1, LEVELS * LA)
    link_rows = []
    for face in range(6):
        axis_id = face // 2
        step_dir = 2 * (face % 2) - 1
        moved = coords[axis_id] + step_dir
        inside = (moved >= 0) & (moved < extents[axis_id])
        partner = jnp.clip(canon + step_dir * strides[axis_id], 0, EL - 1)
        target = jnp.where(inside[None, :], places[:, partner], -1).astype(jnp.int32)
        link_rows.append(jnp.full((DEVICES, EL), -1, jnp.int32).at[owners, places].set(target))
    links = jnp.stack(link_rows)
    curve_of = owners[:, 0] // N_SLAB
    slab_of = owners[:, 0] % N_SLAB
    sends = jnp.full((DEVICES, LEVELS, DEVICES * CAP), 6 * EL, jnp.int32)
    recvs = jnp.full((DEVICES, LEVELS, DEVICES * CAP), 6 * EL, jnp.int32)
    source = owners[:, :, None]
    level_axis = jnp.arange(LEVELS, dtype=jnp.int32)[None, :, None]

    def connect(sends, recvs, valid, targets, span, send_a, send_c, recv_a, recv_c, face_send, face_recv):
        slot_indices = jnp.arange(span, dtype=jnp.int32)[None, None, :]
        along_b = (level_axis - shifts[source, send_a[None, None, :], send_c[None, None, :]]) % LEVELS
        sender = places[source, (send_c * LA + send_a)[None, None, :] * LEVELS + along_b]
        dest = jnp.where(valid, targets, DEVICES).astype(jnp.int32)[:, None, None]
        receiver = places[jnp.minimum(dest, DEVICES - 1), (recv_c * LA + recv_a)[None, None, :] * LEVELS + along_b]
        sends = sends.at[source, level_axis, dest * CAP + slot_indices].set(face_send * EL + sender, mode='drop')
        recvs = recvs.at[dest, level_axis, source * CAP + slot_indices].set(face_recv * EL + receiver, mode='drop')
        return (sends, recvs)
    row_a = jnp.arange(LA, dtype=jnp.int32)
    row_c = jnp.arange(LC, dtype=jnp.int32)
    up_curve = (curve_of + 1) * N_SLAB + (slab_of + turns[curve_of]) % N_SLAB
    sends, recvs = connect(sends, recvs, curve_of < N_CURVE - 1, up_curve, LA, row_a, jnp.full((LA,), LC - 1, jnp.int32), row_a, jnp.zeros((LA,), jnp.int32), 5, 4)
    down_curve = (curve_of - 1) * N_SLAB + (slab_of - turns[jnp.maximum(curve_of - 1, 0)]) % N_SLAB
    sends, recvs = connect(sends, recvs, curve_of > 0, down_curve, LA, row_a, jnp.zeros((LA,), jnp.int32), row_a, jnp.full((LA,), LC - 1, jnp.int32), 4, 5)
    sends, recvs = connect(sends, recvs, slab_of < N_SLAB - 1, owners[:, 0] + 1, LC, jnp.full((LC,), LA - 1, jnp.int32), row_c, jnp.zeros((LC,), jnp.int32), row_c, 1, 0)
    sends, recvs = connect(sends, recvs, slab_of > 0, owners[:, 0] - 1, LC, jnp.zeros((LC,), jnp.int32), row_c, jnp.full((LC,), LA - 1, jnp.int32), row_c, 0, 1)
    return (levels, links, sends, recvs)


def draw_block_inverse(key, part):
    base = jax.random.fold_in(key, 21)
    diagonal = jnp.exp(jax.random.uniform(jax.random.fold_in(base, 1), (BLOCK, ELEMENTS), jnp.float32, jnp.log(0.5), jnp.log(1.5)))
    spread = jnp.clip(jax.random.normal(jax.random.fold_in(base, 2), (BLOCK, BLOCK, ELEMENTS), jnp.float32), -4.0, 4.0) * (0.5 / BLOCK ** 0.5)
    eye = jnp.eye(BLOCK, dtype=jnp.float32)[:, :, None]
    return spread + eye * diagonal[:, None, :]


def draw_dep_level(key, part):
    return layout(key)[0].reshape(ELEMENTS)


def draw_face_link(key, part):
    return layout(key)[1].reshape(6, ELEMENTS)


def draw_send_list(key, part):
    return layout(key)[2].transpose(1, 0, 2).reshape(LEVELS, DEVICES * DEVICES * CAP)


def draw_recv_list(key, part):
    return layout(key)[3].transpose(1, 0, 2).reshape(LEVELS, DEVICES * DEVICES * CAP)


def level_of(stream_key, extent, shards, least, high):
    gain = 1.0
    for axis_at, blocks in shards:
        draws = jax.random.uniform(jax.random.fold_in(jax.random.fold_in(stream_key, 6), axis_at), (blocks,), jnp.float32, least / len(shards), high / len(shards))
        gain = gain * jnp.repeat(jnp.exp(draws), extent[axis_at] // blocks).reshape((-1,) + (1,) * (len(extent) - 1 - axis_at))
    return gain


def bell_draw(rng, extent, scale, limit, cuts=(), kind=jnp.bfloat16):
    level = level_of(rng, extent, cuts, -0.22, 0.18) if cuts else 1.0
    values = jax.random.normal(rng, extent, jnp.float32) * scale * level
    return jnp.minimum(jnp.maximum(values, -limit), limit).astype(kind)


def setup_inputs(seed: int = 0) -> dict:
    key_of = jax.random.split(jax.random.key(seed), 10)
    return {
        "start_state": bell_draw(key_of[0], (BLOCK, ELEMENTS), 1.0, 6.0, ((1, 32),), jnp.float32),
        "right_side": bell_draw(key_of[1], (BLOCK, ELEMENTS), 1.0, 6.0, ((1, 32),), jnp.float32),
        "block_inverse": draw_block_inverse(jax.random.fold_in(key_of[9], 71), 0),
        "lifted_flux_jacobian": bell_draw(key_of[3], (6, BLOCK, TRACE), TRACE ** -0.5, 0.875, (), jnp.float32),
        "face_weight": jnp.clip(jnp.exp(math.log(0.4) - 1.3862944 * jax.random.uniform(key_of[4], (6, ELEMENTS), jnp.float32) ** level_of(key_of[4], (6, ELEMENTS), ((1, 32),), -0.2, 0.2)), 0.1, 0.4),
        "dep_level": draw_dep_level(jax.random.fold_in(key_of[9], 71), 0),
        "face_link": draw_face_link(jax.random.fold_in(key_of[9], 71), 0),
        "send_list": draw_send_list(jax.random.fold_in(key_of[9], 71), 0),
        "recv_list": draw_recv_list(jax.random.fold_in(key_of[9], 71), 0),
    }


REVERSE_FACE = (1, 0, 3, 2, 5, 4)


def face_table(values):
    columns = values.shape[-1]
    cube = values.reshape(VARS, 3, 3, 3, columns)
    faces = [cube[:, 0], cube[:, 2], cube[:, :, 0], cube[:, :, 2], cube[:, :, :, 0], cube[:, :, :, 2]]
    joined = jnp.concatenate([piece.reshape(TRACE, columns) for piece in faces], axis=1)
    return jnp.concatenate([joined, jnp.zeros((TRACE, 1), joined.dtype)], axis=1)


def neighbor_index(links):
    columns = links.shape[1]
    offsets = jnp.array(REVERSE_FACE, jnp.int32)[:, None] * columns
    return jnp.where(links >= 0, links + offsets, 6 * columns).astype(jnp.int32).reshape(6 * columns)


def inflow(traces, ghosts, where_from, lifted_flux_jacobian, coupling_weights):
    columns = coupling_weights.shape[1]
    gathered = (traces[:, where_from] + ghosts[:, :6 * columns]).reshape(TRACE, 6, columns)
    weighted_traces = gathered * coupling_weights[None]
    return jnp.einsum("vuh,hvw->uw", lifted_flux_jacobian, weighted_traces, precision=lax.Precision.HIGHEST)


def to_devices(values):
    return values.reshape(BLOCK, DEVICES, EL).transpose(1, 0, 2)


def from_devices(stacked):
    return stacked.transpose(1, 0, 2).reshape(BLOCK, DEVICES * EL)


def deliver_traces(ghosts, traces, sends, recvs, width):
    packed = jax.vmap(lambda one_table, one_send: one_table[:, one_send])(traces, sends)
    packed = packed.reshape(DEVICES, TRACE, DEVICES, width).transpose(2, 1, 0, 3).reshape(DEVICES, TRACE, DEVICES * width)
    return jax.vmap(lambda one_ghost, one_recv, arrived: one_ghost.at[:, one_recv].set(arrived))(ghosts, recvs, packed)


def reference(start_state, right_side, block_inverse, lifted_flux_jacobian, face_weight, dep_level, face_link, send_list, recv_list):
    sends = send_list.reshape(LEVELS, DEVICES, DEVICES * CAP)
    recvs = recv_list.reshape(LEVELS, DEVICES, DEVICES * CAP)
    where_from = jax.vmap(neighbor_index)(face_link.reshape(6, DEVICES, EL).transpose(1, 0, 2))
    coupling_weights = face_weight.reshape(6, DEVICES, EL).transpose(1, 0, 2)
    all_send = sends.reshape(LEVELS, DEVICES, DEVICES, CAP).transpose(1, 2, 0, 3).reshape(DEVICES, DEVICES * LEVELS * CAP)
    all_recv = recvs.reshape(LEVELS, DEVICES, DEVICES, CAP).transpose(1, 2, 0, 3).reshape(DEVICES, DEVICES * LEVELS * CAP)
    ghosts = jnp.zeros((DEVICES, TRACE, 6 * EL + 1), jnp.float32)
    traces = jax.vmap(face_table)(to_devices(start_state))
    ghosts = deliver_traces(ghosts, traces, all_send, all_recv, LEVELS * CAP)

    def advance(current, ghosts, traces, level_now):
        flows = jax.vmap(lambda one_table, one_ghost, one_index, one_weight: inflow(one_table, one_ghost, one_index, lifted_flux_jacobian, one_weight))(traces, ghosts, where_from, coupling_weights)
        update = jnp.einsum("ije,je->ie", block_inverse, right_side - from_devices(flows), precision=lax.Precision.HIGHEST)
        return jnp.where(dep_level[None] == level_now, update, current)

    current = start_state
    for level_now in range(LEVELS):
        current = advance(current, ghosts, traces, level_now)
        traces = jax.vmap(face_table)(to_devices(current))
        ghosts = deliver_traces(ghosts, traces, sends[level_now], recvs[level_now], CAP)
    forward_state = current
    for level_now in range(LEVELS - 1, -1, -1):
        current = advance(current, ghosts, traces, level_now)
        if level_now > 0:
            traces = jax.vmap(face_table)(to_devices(current))
            ghosts = deliver_traces(ghosts, traces, sends[level_now], recvs[level_now], CAP)
    return forward_state, current
```

```python
import functools

import jax
import jax.numpy as jnp
import numpy as np
from jax import lax
from jax.experimental import pallas as pl
from jax.experimental.pallas import tpu as pltpu
from jax.sharding import PartitionSpec as P

VARS = 5
SIDE = 3
FACES = 6
LANES = 128
SUB = 8
GROUPS = 8
F32 = jnp.float32
BF16 = jnp.bfloat16


class Sizes:
    def __init__(self, block, columns, levels, slots, curves, slabs):
        self.block = block
        self.columns = columns
        self.levels = levels
        self.slots = slots
        self.curves = curves
        self.slabs = slabs
        self.devices = curves * slabs
        self.trace = VARS * SIDE * SIDE
        self.width = columns // GROUPS
        self.rows = -(-block // GROUPS)
        self.rows_pad = -(-(self.rows + 1) // SUB) * SUB
        self.state_rows = GROUPS * self.rows_pad
        self.block_pad = -(-block // SUB) * SUB
        self.flag = self.trace
        self.wish = self.trace + 1
        self.trace_pad = -(-(self.trace + 2) // 16) * 16
        self.cuts = self.trace_pad // 16
        self.table_rows = FACES * self.trace_pad
        self.jac_rows = -(-self.block_pad // 16) * 16
        assert columns == LANES and slabs * slots == LANES
        assert (self.cuts + 1) * slots <= LANES and block < self.block_pad


def face_rows():
    nodes = np.arange(VARS * SIDE**3).reshape(VARS, SIDE, SIDE, SIDE)
    last = SIDE - 1
    sides = [
        nodes[:, 0],
        nodes[:, last],
        nodes[:, :, 0],
        nodes[:, :, last],
        nodes[:, :, :, 0],
        nodes[:, :, :, last],
    ]
    return [side.reshape(-1) for side in sides]


def selector(z):
    pick = np.zeros((z.table_rows, z.state_rows), np.float32)
    for face, rows in enumerate(face_rows()):
        for h, i in enumerate(rows):
            pick[face * z.trace_pad + h, i // z.rows * z.rows_pad + i % z.rows] = 1
        pick[face * z.trace_pad + z.flag, z.rows] = 1
    return np.concatenate([pick, pick], axis=1)


def lane_take(values, index):
    index = jnp.broadcast_to(index, values.shape)
    return jnp.take_along_axis(values, index, axis=1, mode="promise_in_bounds")


def lane_iota(rows=SUB):
    return lax.broadcasted_iota(jnp.int32, (rows, LANES), 1)


def halves(values):
    high = values.astype(BF16)
    low = (values - high.astype(F32)).astype(BF16)
    return high, low


def as_column(row):
    return jnp.broadcast_to(row, (LANES, LANES)).T


def dot(a, b):
    return jnp.dot(a, b, preferred_element_type=F32)


def tables_of(state, pick):
    high, low = halves(state)
    return dot(pick, jnp.concatenate([high, low], axis=0))


def fluxes(jac, traces):
    high, low = halves(traces)
    return dot(jac, jnp.concatenate([high, low, high], axis=0))


def pack(z, message, group, curve, open_sends, out_ref):
    lanes = lane_iota(16)
    target = curve + group - 1

    @pl.when((target >= 0) & (target < z.curves))
    def _():
        for slab in range(z.slabs):
            block = jnp.broadcast_to(open_sends, (16, LANES))
            for cut in range(z.cuts):
                part = message[cut * 16 : cut * 16 + 16]
                shift = (cut - slab) * z.slots % LANES
                part = pltpu.roll(part, shift, 1) if shift else part
                block = jnp.where(lanes // z.slots == cut, part, block)
            out_ref[target * z.slabs + slab] = block


def unpack(z, group, curve, in_ref):
    lanes = lane_iota(16)
    source = jnp.clip(curve + group - 1, 0, z.curves - 1)
    blocks = [in_ref[source * z.slabs + slab] for slab in range(z.slabs)]
    parts = []
    for cut in range(z.cuts):
        part = jnp.zeros((16, LANES), F32)
        for slab in range(z.slabs):
            shift = (slab - cut) * z.slots % LANES
            block = pltpu.roll(blocks[slab], shift, 1) if shift else blocks[slab]
            part = jnp.where(lanes // z.slots == slab, block, part)
        parts.append(part)
    return jnp.concatenate(parts, axis=0)


def ghost_take(z, slot_traces, where, face):
    index = jnp.maximum(where[face : face + 1], 0)
    lane = jnp.bitwise_and(index, LANES - 1)
    block = index // LANES
    found = jnp.zeros((z.trace_pad, LANES), F32)
    for group in range(3):
        found = jnp.where(block == group, lane_take(slot_traces[group], lane), found)
    return found


def prepare_kernel(
    z,
    curve_ref,
    start_ref,
    dep_ref,
    link_ref,
    weight_ref,
    send_ref,
    recv_ref,
    level_ref,
    pick_ref,
    ints_ref,
    floats_ref,
    sends_ref,
    span_ref,
    table_ref,
    message_ref,
    state_ref,
):
    n = z.columns
    lanes = lane_iota()
    dep_row = dep_ref[...]
    dep = jnp.broadcast_to(dep_row, (SUB, n))
    key = (dep_row * n + lane_iota(1)).astype(F32)
    earlier = as_column(key) < jnp.broadcast_to(key, (n, n))
    pos_row = jnp.sum(jnp.where(earlier, 1.0, 0.0), axis=0, keepdims=True)
    here = as_column(pos_row) == lane_iota(n).astype(F32)
    element = lax.broadcasted_iota(jnp.int32, (n, n), 0).astype(F32)
    perm_row = jnp.sum(jnp.where(here, element, 0.0), axis=0, keepdims=True)
    pos = jnp.broadcast_to(pos_row.astype(jnp.int32), (SUB, n))
    perm = jnp.broadcast_to(perm_row.astype(jnp.int32), (SUB, n))
    dep_sorted = lane_take(dep, perm)
    for level in range(z.levels):
        before = jnp.sum(jnp.where(dep_row < level, 1.0, 0.0)).astype(jnp.int32)
        upto = jnp.sum(jnp.where(dep_row <= level, 1.0, 0.0)).astype(jnp.int32)
        span_ref[level] = before // z.width
        span_ref[z.levels + level] = jnp.where(upto > before, (upto + z.width - 1) // z.width, before // z.width)

    link = link_ref[...]
    near = jnp.where(link >= 0, lane_take(pos, jnp.maximum(link, 0)), -1)
    near = lane_take(near, perm)
    weight = lane_take(weight_ref[...], perm)
    local = near >= 0
    near = jnp.maximum(near, 0)
    dep_near = lane_take(dep_sorted, near)
    zero = jnp.zeros_like(weight)

    recv = recv_ref[...]
    slot_level = jnp.broadcast_to(level_ref[...], (SUB, n))
    rows = []
    slot_id = lax.broadcasted_iota(jnp.int32, (n, n), 0).astype(F32) + 1.0
    columns = [as_column(recv[group : group + 1].astype(F32)) for group in range(3)]
    for face in range(FACES):
        name = (lane_iota(n) + face * n).astype(F32)
        found = jnp.zeros((1, n), F32)
        for group in range(3):
            hit = jnp.where(columns[group] == name, slot_id + float(group * n), 0.0)
            found = jnp.maximum(found, jnp.max(hit, axis=0, keepdims=True))
        rows.append(found)
    rows.append(jnp.zeros((SUB - FACES, n), F32))
    slot = jnp.concatenate(rows, axis=0).astype(jnp.int32) - 1
    slot = lane_take(slot, perm)
    from_far = slot >= 0
    slot = jnp.maximum(slot, 0)
    far_level = lane_take(slot_level, jnp.bitwise_and(slot, n - 1))

    for at, value in enumerate((pos, perm, dep_sorted, near, slot)):
        ints_ref[at] = value
    floats_ref[0] = jnp.where(local & (dep_near < dep_sorted), weight, zero)
    floats_ref[1] = jnp.where(local & (dep_near > dep_sorted), weight, zero)
    floats_ref[2] = jnp.where(local & (dep_near <= dep_sorted), weight, zero)
    floats_ref[3] = jnp.where(local & (dep_near >= dep_sorted), weight, zero)
    floats_ref[4] = jnp.where(from_far & (far_level < dep_sorted), weight, zero)
    floats_ref[5] = jnp.where(from_far, weight, zero)
    floats_ref[6] = jnp.where(from_far & (far_level >= dep_sorted), weight, zero)

    send = send_ref[...]
    send_element = jnp.bitwise_and(send, n - 1)
    sends_ref[0] = lane_take(pos, send_element)
    sends_ref[1] = send // n
    sends_ref[2] = lane_take(dep, send_element)
    recv_dep = lane_take(dep, jnp.bitwise_and(recv, n - 1))
    wish = jnp.where(slot_level <= recv_dep, 1.0, 0.0)

    state_ref[...] = jnp.zeros_like(state_ref)
    for group in range(GROUPS):
        count = min(z.rows, z.block - group * z.rows)
        state_ref[pl.ds(group * z.rows_pad, count), :] = start_ref[pl.ds(group * z.rows, count), :]
    state_ref[pl.ds(z.rows, 1), :] = jnp.ones((1, n), F32)
    state = lane_take(state_ref[...], perm[0:1])
    table = tables_of(state, pick_ref[...])
    table_ref[...] = table
    message_ref[...] = jnp.zeros_like(message_ref)
    row_id = lax.broadcasted_iota(jnp.int32, (z.trace_pad, n), 0)
    for group in range(3):
        where = sends_ref[0][group : group + 1]
        side = sends_ref[1][group : group + 1]
        message = jnp.zeros((z.trace_pad, n), F32)
        for face in range(FACES):
            piece = table[face * z.trace_pad : (face + 1) * z.trace_pad]
            message = jnp.where(side == face, lane_take(piece, where), message)
        message = jnp.where(row_id == z.wish, wish[group : group + 1], message)
        pack(z, message, group, curve_ref[0], jnp.zeros((1, n), F32), message_ref)


def arrange_kernel(
    z,
    curve_ref,
    inverse_ref,
    right_ref,
    ints_ref,
    floats_ref,
    sends_ref,
    level_ref,
    table_ref,
    arrived_ref,
    jac_ref,
    chunks_ref,
    base_ref,
    right_sorted_ref,
    start_slots_ref,
    kinds_ref,
    stack_ref,
):
    n = z.columns
    perm = ints_ref[1]
    lanes = lane_iota()
    orders = [pltpu.roll(perm, group * z.width, 1) if group else perm for group in range(GROUPS)]
    bits = [jnp.bitwise_and(lanes // (z.width << b), 1) == 1 for b in range(3)]

    def row(ii, carry):
        for tile in range(z.block_pad // SUB):
            count = min(SUB, z.block - tile * SUB)
            spread = []
            for group in range(GROUPS):
                i = jnp.minimum(group * z.rows + ii, z.block - 1)
                block = inverse_ref[i, pl.ds(tile * SUB, count), :]
                if count < SUB:
                    block = jnp.concatenate([block, jnp.zeros((SUB - count, n), F32)], axis=0)
                spread.append(lane_take(block, orders[group]))
            for b in range(3):
                spread = [
                    jnp.where(bits[b], spread[(x + (1 << b)) % GROUPS], spread[x])
                    for x in range(GROUPS)
                ]
            for chunk in range(GROUPS):
                chunks_ref[chunk, ii, pl.ds(tile * SUB, SUB), :] = spread[-chunk % GROUPS]
        return carry

    lax.fori_loop(0, z.rows, row, 0)

    slot_traces = []
    for group in range(3):
        traces = unpack(z, group, curve_ref[0], arrived_ref)
        start_slots_ref[group] = traces
        slot_traces.append(traces)
        wish = traces[z.wish : z.wish + 1] > 0.5
        side = sends_ref[1][group : group + 1]
        dep = sends_ref[2][group : group + 1]
        level = level_ref[...]
        kind = jnp.where(
            wish, jnp.where(dep <= level, 1, 3), jnp.where(dep >= level, 2, 1)
        )
        kinds_ref[pl.ds(group, 1), :] = jnp.where(side < FACES, kind, 0)
    near = ints_ref[3]
    slot = ints_ref[4]
    for face in range(FACES):
        back = face ^ 1
        piece = table_ref[pl.ds(back * z.trace_pad, z.trace_pad), :]
        value = lane_take(piece, near[face : face + 1]) * floats_ref[3][face : face + 1]
        ghost = ghost_take(z, slot_traces, slot, face) * floats_ref[6][face : face + 1]
        stack_ref[pl.ds(face * z.trace_pad, z.trace_pad), :] = value + ghost
    flow = fluxes(jac_ref[...], stack_ref[...])[: z.block_pad]
    right = jnp.concatenate([right_ref[...], jnp.zeros((z.block_pad - z.block, n), F32)], axis=0)
    right = lane_take(right, perm[0:1])
    right_sorted_ref[...] = right
    base_ref[...] = right - flow


def round_kernel(
    z,
    curve_ref,
    span_ref,
    arrived_ref,
    ints_ref,
    floats_ref,
    sends_ref,
    kinds_ref,
    start_slots_ref,
    base_ref,
    right_ref,
    jac_ref,
    pick_ref,
    chunks_ref,
    forward_table_in,
    swept_table_in,
    forward_in,
    swept_in,
    message_ref,
    forward_table_ref,
    swept_table_ref,
    forward_ref,
    swept_ref,
    stack_ref,
    wide_ref,
    forward_base_ref,
    swept_base_ref,
    part_ref,
):
    n = z.columns
    lanes = lane_iota()
    forward_table_ref[...] = forward_table_in[...]
    swept_table_ref[...] = swept_table_in[...]
    forward_ref[...] = forward_in[...]
    swept_ref[...] = swept_in[...]
    near_all = ints_ref[3]
    slot = ints_ref[4]
    dep_all = ints_ref[2]
    row_id = lax.broadcasted_iota(jnp.int32, (z.trace_pad, n), 0)

    slot_traces = []
    for group in range(3):
        traces = unpack(z, group, curve_ref[0], arrived_ref)
        flag = traces[z.flag : z.flag + 1]
        traces = jnp.where((flag > 1.5) & (row_id != z.flag), start_slots_ref[group], traces)
        slot_traces.append(traces)
    missing_forward = jnp.zeros((1, n), F32)
    missing_swept = jnp.zeros((1, n), F32)
    for face in range(FACES):
        ghost = ghost_take(z, slot_traces, slot, face)
        forward_weight = floats_ref[4][face : face + 1]
        swept_weight = floats_ref[5][face : face + 1]
        lost = jnp.where(ghost[z.flag : z.flag + 1] > 0.5, 0.0, 1.0)
        missing_forward += jnp.where(forward_weight > 0, lost, 0.0)
        missing_swept += jnp.where(swept_weight > 0, lost, 0.0)
        at = pl.ds(face * z.trace_pad, z.trace_pad)
        wide_ref[at, pl.ds(0, n)] = ghost * forward_weight
        wide_ref[at, pl.ds(n, n)] = ghost * swept_weight
    flow = fluxes(jac_ref[...], wide_ref[...])
    forward_base_ref[...] = base_ref[...] - flow[: z.block_pad, :n]
    swept_base_ref[...] = right_ref[...] - flow[: z.block_pad, n:]
    forward_base_ref[pl.ds(z.block, 1), :] = missing_forward
    swept_base_ref[pl.ds(z.block, 1), :] = missing_swept
    part_ref[...] = jnp.where(
        lax.broadcasted_iota(jnp.int32, (z.rows_pad, n), 0) == z.rows, 1.0, 0.0
    )
    last = z.block_pad - SUB
    flag_tile = z.flag // SUB * SUB
    flag_row = z.flag % SUB

    def flags_of(table_ref, face, index):
        tile = table_ref[pl.ds(face * z.trace_pad + flag_tile, SUB), :]
        return lane_take(tile, index)[flag_row : flag_row + 1]

    def step(level, chunk, backward):
        own = chunk * z.width + jnp.bitwise_and(lanes, z.width - 1)
        near = lane_take(near_all, own)
        base = swept_base_ref if backward else forward_base_ref
        out_table = swept_table_ref if backward else forward_table_ref
        out_state = swept_ref if backward else forward_ref
        old_weight = lane_take(floats_ref[2 if backward else 0], own)
        new_weight = lane_take(floats_ref[1], own)
        missing = lane_take(base[pl.ds(last, SUB), :], own)[SUB - 1 :]
        for face in range(FACES):
            row = near[face : face + 1]
            flag = flags_of(forward_table_ref, face, row)
            missing += jnp.where(old_weight[face : face + 1] > 0, 1.0 - flag, 0.0)
            if backward:
                flag = flags_of(swept_table_ref, face, row)
                missing += jnp.where(new_weight[face : face + 1] > 0, 1.0 - flag, 0.0)
        mine = lane_take(dep_all, own)[0:1] == level
        ready = mine & (missing < 0.5)
        done = flags_of(out_table, 0, own[0:1])
        fresh = jnp.max(jnp.where(ready, 1.0 - done, 0.0))

        @pl.when(fresh > 0.5)
        def _():
            for face in range(FACES):
                at = pl.ds((face ^ 1) * z.trace_pad, z.trace_pad)
                row = near[face : face + 1]
                value = lane_take(forward_table_ref[at, :], row) * old_weight[face : face + 1]
                if backward:
                    new = lane_take(swept_table_ref[at, :], row)
                    value += new * new_weight[face : face + 1]
                stack_ref[pl.ds(face * z.trace_pad, z.trace_pad), :] = value
            flow = fluxes(jac_ref[...], stack_ref[...])[: z.block_pad]
            rest = lane_take(base[...], own[0:1]) - flow
            for ii in range(z.rows):
                part_ref[pl.ds(ii, 1), :] = jnp.sum(
                    chunks_ref[chunk, ii] * rest, axis=0, keepdims=True
                )
            part = part_ref[...]
            state = jnp.concatenate(
                [pltpu.roll(part, -g * z.width % n, 1) if g else part for g in range(GROUPS)],
                axis=0,
            )
            table = tables_of(state, pick_ref[...])
            keep = ready & (lane_iota(1) // z.width == chunk)
            out_state[...] = jnp.where(keep, state, out_state[...])
            out_table[...] = jnp.where(keep, table, out_table[...])

    def level_steps(backward):
        def run(count, carry):
            level = z.levels - 1 - count if backward else count

            def one(chunk, inner):
                step(level, chunk, backward)
                return inner

            return lax.fori_loop(span_ref[level], span_ref[z.levels + level], one, carry)

        lax.fori_loop(0, z.levels, run, 0)

    level_steps(False)
    level_steps(True)

    messages = []
    still = jnp.zeros((1, n), F32)
    for group in range(3):
        where = sends_ref[0][group : group + 1]
        side = sends_ref[1][group : group + 1]
        kind = kinds_ref[pl.ds(group, 1), :]
        message = jnp.zeros((z.trace_pad, n), F32)
        for face in range(FACES):
            at = pl.ds(face * z.trace_pad, z.trace_pad)
            first = lane_take(forward_table_ref[at, :], where)
            second = lane_take(swept_table_ref[at, :], where)
            picked = jnp.where(kind == 1, first, second)
            message = jnp.where(side == face, picked, message)
        message = jnp.where((kind == 3) & (row_id == z.flag), 2.0, message)
        unsent = (kind > 0) & (message[z.flag : z.flag + 1] < 0.5)
        still = jnp.maximum(still, jnp.where(unsent, 1.0, 0.0))
        messages.append(message)
    still = jnp.broadcast_to(jnp.max(still, axis=1, keepdims=True), (1, n))
    message_ref[...] = jnp.broadcast_to(still[None], message_ref.shape)
    for group in range(3):
        pack(z, messages[group], group, curve_ref[0], still, message_ref)


def output_kernel(z, ints_ref, forward_ref, swept_ref, forward_out, swept_out):
    pos = ints_ref[0][0:1]
    for source, target in ((forward_ref, forward_out), (swept_ref, swept_out)):
        for group in range(GROUPS):
            count = min(z.rows, z.block - group * z.rows)
            block = lane_take(source[pl.ds(group * z.rows_pad, z.rows_pad), :], pos)
            target[pl.ds(group * z.rows, count), :] = block[:count]


def call(kernel, outs, scratch=(), aliases=None, smem_in=(), inputs=0, smem_out=()):
    vmem, smem = pl.BlockSpec(memory_space=pltpu.VMEM), pl.BlockSpec(memory_space=pltpu.SMEM)
    return pl.pallas_call(
        kernel,
        out_shape=outs,
        in_specs=[smem if at in smem_in else vmem for at in range(inputs)],
        out_specs=[smem if at in smem_out else vmem for at in range(len(outs))],
        scratch_shapes=list(scratch),
        input_output_aliases=aliases or {},
        compiler_params=pltpu.CompilerParams(vmem_limit_bytes=48 << 20),
    )


def shape(*dims, kind=F32):
    return jax.ShapeDtypeStruct(dims, kind)


def body(
    start_state,
    right_side,
    block_inverse,
    lifted_flux_jacobian,
    face_weight,
    dep_level,
    face_link,
    send_list,
    recv_list,
):
    curves, slabs = lax.axis_size("curve"), lax.axis_size("slab")
    levels = send_list.shape[0]
    cap = send_list.shape[1] // (curves * slabs)
    slots = levels * cap
    block, n = start_state.shape
    z = Sizes(block, n, levels, slots, curves, slabs)
    own = lax.axis_index("curve").astype(jnp.int32)
    curve = own.reshape(1)

    def nearby(lists):
        grid = lists.reshape(levels, curves, slabs, cap).transpose(1, 2, 0, 3)
        grid = grid.reshape(curves, slabs * slots)
        grid = jnp.pad(grid, ((1, 1), (0, 0)), constant_values=FACES * n)
        picked = lax.dynamic_slice_in_dim(grid, own, 3, axis=0)
        return jnp.pad(picked, ((0, SUB - 3), (0, 0)), constant_values=FACES * n)

    send, recv = nearby(send_list), nearby(recv_list)
    link = jnp.pad(face_link, ((0, SUB - FACES), (0, 0)), constant_values=-1)
    weight = jnp.pad(face_weight, ((0, SUB - FACES), (0, 0)))
    slot_level = jnp.asarray(
        np.tile(np.repeat(np.arange(levels), cap), slabs).reshape(1, n), jnp.int32
    )
    pick = jnp.asarray(selector(z), BF16)
    jac = jnp.pad(
        lifted_flux_jacobian, ((0, 0), (0, z.jac_rows - block), (0, z.trace_pad - z.trace))
    )
    jac = jac.transpose(1, 0, 2).reshape(z.jac_rows, z.table_rows)
    rounded = lax.reduce_precision(jac, 8, 7)
    high, low = rounded.astype(BF16), (jac - rounded).astype(BF16)
    jac = jnp.concatenate([high, high, low], axis=1)

    ints, floats, sends, span, start_table, message = call(
        functools.partial(prepare_kernel, z),
        [
            shape(5, SUB, n, kind=jnp.int32),
            shape(7, SUB, n),
            shape(3, SUB, n, kind=jnp.int32),
            shape(2 * levels, kind=jnp.int32),
            shape(z.table_rows, n),
            shape(z.devices, 16, n),
        ],
        scratch=[pltpu.VMEM((z.state_rows, n), F32)],
        smem_in=(0,),
        inputs=9,
        smem_out=(3,),
    )(curve, start_state, dep_level.reshape(1, n), link, weight, send, recv, slot_level, pick)

    def exchange(message):
        return lax.all_to_all(message, ("curve", "slab"), 0, 0, tiled=True)

    arrived = exchange(message)
    chunks, base, right, start_slots, kinds = call(
        functools.partial(arrange_kernel, z),
        [
            shape(GROUPS, z.rows, z.block_pad, n),
            shape(z.block_pad, n),
            shape(z.block_pad, n),
            shape(3, z.trace_pad, n),
            shape(3, n, kind=jnp.int32),
        ],
        scratch=[pltpu.VMEM((z.table_rows, n), F32)],
        smem_in=(0,),
        inputs=10,
    )(curve, block_inverse, right_side, ints, floats, sends, slot_level, start_table, arrived, jac)

    round_call = call(
        functools.partial(round_kernel, z),
        [
            shape(z.devices, 16, n),
            shape(z.table_rows, n),
            shape(z.table_rows, n),
            shape(z.state_rows, n),
            shape(z.state_rows, n),
        ],
        scratch=[
            pltpu.VMEM((z.table_rows, n), F32),
            pltpu.VMEM((z.table_rows, 2 * n), F32),
            pltpu.VMEM((z.block_pad, n), F32),
            pltpu.VMEM((z.block_pad, n), F32),
            pltpu.VMEM((z.rows_pad, n), F32),
        ],
        aliases={13: 1, 14: 2, 15: 3, 16: 4},
        smem_in=(0, 1),
        inputs=17,
    )

    def run(arrived, tables):
        return round_call(
            curve, span, arrived, ints, floats, sends, kinds, start_slots, base, right, jac, pick, chunks, *tables
        )

    def more(carry):
        return carry[0]

    def one_round(carry):
        _, message, tables = carry
        arrived = exchange(message)
        message, *tables = run(arrived, tables)
        return jnp.max(arrived[:, 0, n - 1]) > 0.5, message, tuple(tables)

    empty = (
        jnp.zeros((z.table_rows, n), F32),
        jnp.zeros((z.table_rows, n), F32),
        jnp.zeros((z.state_rows, n), F32),
        jnp.zeros((z.state_rows, n), F32),
    )
    message, *tables = run(jnp.zeros_like(message), empty)
    _, _, tables = lax.while_loop(more, one_round, (jnp.array(True), message, tuple(tables)))
    return tuple(
        call(functools.partial(output_kernel, z), [shape(block, n), shape(block, n)], inputs=3)(
            ints, tables[2], tables[3]
        )
    )


def solution(mesh):
    split = ("curve", "slab")
    return jax.shard_map(
        body,
        mesh=mesh,
        in_specs=(
            P(None, split),
            P(None, split),
            P(None, None, split),
            P(),
            P(None, split),
            P(split),
            P(None, split),
            P(None, split),
            P(None, split),
        ),
        out_specs=(P(None, split), P(None, split)),
        check_vma=False,
    )
```

```python
import functools

import jax
import jax.numpy as jnp
import numpy as np
from jax import lax
from jax.experimental import pallas as pl
from jax.experimental.pallas import tpu as pltpu
from jax.sharding import PartitionSpec as P

VARS = 5
SIDE = 3
FACES = 6
LANES = 128
SUB = 8
GROUPS = 8
F32 = jnp.float32
BF16 = jnp.bfloat16


class Sizes:
    def __init__(self, block, columns, levels, slots, curves, slabs):
        self.block = block
        self.columns = columns
        self.levels = levels
        self.slots = slots
        self.curves = curves
        self.slabs = slabs
        self.devices = curves * slabs
        self.trace = VARS * SIDE * SIDE
        self.width = columns // GROUPS
        self.rows = -(-block // GROUPS)
        self.rows_pad = -(-(self.rows + 1) // SUB) * SUB
        self.state_rows = GROUPS * self.rows_pad
        self.block_pad = -(-block // SUB) * SUB
        self.flag = self.trace
        self.wish = self.trace + 1
        self.trace_pad = -(-(self.trace + 2) // 16) * 16
        self.cuts = self.trace_pad // 16
        self.table_rows = FACES * self.trace_pad
        self.jac_rows = -(-self.block_pad // 16) * 16
        assert columns == LANES and slabs * slots == LANES
        assert (self.cuts + 1) * slots <= LANES and block < self.block_pad


def face_rows():
    nodes = np.arange(VARS * SIDE**3).reshape(VARS, SIDE, SIDE, SIDE)
    last = SIDE - 1
    sides = [
        nodes[:, 0],
        nodes[:, last],
        nodes[:, :, 0],
        nodes[:, :, last],
        nodes[:, :, :, 0],
        nodes[:, :, :, last],
    ]
    return [side.reshape(-1) for side in sides]


def selector(z):
    pick = np.zeros((z.table_rows, z.state_rows), np.float32)
    for face, rows in enumerate(face_rows()):
        for h, i in enumerate(rows):
            pick[face * z.trace_pad + h, i // z.rows * z.rows_pad + i % z.rows] = 1
        pick[face * z.trace_pad + z.flag, z.rows] = 1
    return np.concatenate([pick, pick], axis=1)


def lane_take(values, index):
    index = jnp.broadcast_to(index, values.shape)
    return jnp.take_along_axis(values, index, axis=1, mode="promise_in_bounds")


def lane_iota(rows=SUB):
    return lax.broadcasted_iota(jnp.int32, (rows, LANES), 1)


def halves(values):
    high = values.astype(BF16)
    low = (values - high.astype(F32)).astype(BF16)
    return high, low


def as_column(row):
    return jnp.broadcast_to(row, (LANES, LANES)).T


def dot(a, b):
    return jnp.dot(a, b, preferred_element_type=F32)


def tables_of(state, pick):
    high, low = halves(state)
    return dot(pick, jnp.concatenate([high, low], axis=0))


def fluxes(jac, traces):
    high, low = halves(traces)
    return dot(jac, jnp.concatenate([high, low, high], axis=0))


def pack(z, message, group, curve, open_sends, out_ref):
    lanes = lane_iota(16)
    target = curve + group - 1

    @pl.when((target >= 0) & (target < z.curves))
    def _():
        for slab in range(z.slabs):
            block = jnp.broadcast_to(open_sends, (16, LANES))
            for cut in range(z.cuts):
                part = message[cut * 16 : cut * 16 + 16]
                shift = (cut - slab) * z.slots % LANES
                part = pltpu.roll(part, shift, 1) if shift else part
                block = jnp.where(lanes // z.slots == cut, part, block)
            out_ref[target * z.slabs + slab] = block


def unpack(z, group, curve, in_ref):
    lanes = lane_iota(16)
    source = jnp.clip(curve + group - 1, 0, z.curves - 1)
    blocks = [in_ref[source * z.slabs + slab] for slab in range(z.slabs)]
    parts = []
    for cut in range(z.cuts):
        part = jnp.zeros((16, LANES), F32)
        for slab in range(z.slabs):
            shift = (slab - cut) * z.slots % LANES
            block = pltpu.roll(blocks[slab], shift, 1) if shift else blocks[slab]
            part = jnp.where(lanes // z.slots == slab, block, part)
        parts.append(part)
    return jnp.concatenate(parts, axis=0)


def ghost_take(z, slot_traces, where, face):
    index = jnp.maximum(where[face : face + 1], 0)
    lane = jnp.bitwise_and(index, LANES - 1)
    block = index // LANES
    found = jnp.zeros((z.trace_pad, LANES), F32)
    for group in range(3):
        found = jnp.where(block == group, lane_take(slot_traces[group], lane), found)
    return found


def prepare_kernel(
    z,
    curve_ref,
    start_ref,
    dep_ref,
    link_ref,
    weight_ref,
    send_ref,
    recv_ref,
    level_ref,
    pick_ref,
    ints_ref,
    floats_ref,
    sends_ref,
    span_ref,
    table_ref,
    message_ref,
    state_ref,
):
    n = z.columns
    lanes = lane_iota()
    dep_row = dep_ref[...]
    dep = jnp.broadcast_to(dep_row, (SUB, n))
    key = (dep_row * n + lane_iota(1)).astype(F32)
    earlier = as_column(key) < jnp.broadcast_to(key, (n, n))
    pos_row = jnp.sum(jnp.where(earlier, 1.0, 0.0), axis=0, keepdims=True)
    here = as_column(pos_row) == lane_iota(n).astype(F32)
    element = lax.broadcasted_iota(jnp.int32, (n, n), 0).astype(F32)
    perm_row = jnp.sum(jnp.where(here, element, 0.0), axis=0, keepdims=True)
    pos = jnp.broadcast_to(pos_row.astype(jnp.int32), (SUB, n))
    perm = jnp.broadcast_to(perm_row.astype(jnp.int32), (SUB, n))
    dep_sorted = lane_take(dep, perm)
    for level in range(z.levels):
        before = jnp.sum(jnp.where(dep_row < level, 1.0, 0.0)).astype(jnp.int32)
        upto = jnp.sum(jnp.where(dep_row <= level, 1.0, 0.0)).astype(jnp.int32)
        span_ref[level] = before // z.width
        span_ref[z.levels + level] = jnp.where(upto > before, (upto + z.width - 1) // z.width, before // z.width)

    link = link_ref[...]
    near = jnp.where(link >= 0, lane_take(pos, jnp.maximum(link, 0)), -1)
    near = lane_take(near, perm)
    weight = lane_take(weight_ref[...], perm)
    local = near >= 0
    near = jnp.maximum(near, 0)
    dep_near = lane_take(dep_sorted, near)
    zero = jnp.zeros_like(weight)

    recv = recv_ref[...]
    slot_level = jnp.broadcast_to(level_ref[...], (SUB, n))
    rows = []
    slot_id = lax.broadcasted_iota(jnp.int32, (n, n), 0).astype(F32) + 1.0
    columns = [as_column(recv[group : group + 1].astype(F32)) for group in range(3)]
    for face in range(FACES):
        name = (lane_iota(n) + face * n).astype(F32)
        found = jnp.zeros((1, n), F32)
        for group in range(3):
            hit = jnp.where(columns[group] == name, slot_id + float(group * n), 0.0)
            found = jnp.maximum(found, jnp.max(hit, axis=0, keepdims=True))
        rows.append(found)
    rows.append(jnp.zeros((SUB - FACES, n), F32))
    slot = jnp.concatenate(rows, axis=0).astype(jnp.int32) - 1
    slot = lane_take(slot, perm)
    from_far = slot >= 0
    slot = jnp.maximum(slot, 0)
    far_level = lane_take(slot_level, jnp.bitwise_and(slot, n - 1))

    for at, value in enumerate((pos, perm, dep_sorted, near, slot)):
        ints_ref[at] = value
    floats_ref[0] = jnp.where(local & (dep_near < dep_sorted), weight, zero)
    floats_ref[1] = jnp.where(local & (dep_near > dep_sorted), weight, zero)
    floats_ref[2] = jnp.where(local & (dep_near <= dep_sorted), weight, zero)
    floats_ref[3] = jnp.where(local & (dep_near >= dep_sorted), weight, zero)
    floats_ref[4] = jnp.where(from_far & (far_level < dep_sorted), weight, zero)
    floats_ref[5] = jnp.where(from_far, weight, zero)
    floats_ref[6] = jnp.where(from_far & (far_level >= dep_sorted), weight, zero)

    send = send_ref[...]
    send_element = jnp.bitwise_and(send, n - 1)
    sends_ref[0] = lane_take(pos, send_element)
    sends_ref[1] = send // n
    sends_ref[2] = lane_take(dep, send_element)
    recv_dep = lane_take(dep, jnp.bitwise_and(recv, n - 1))
    wish = jnp.where(slot_level <= recv_dep, 1.0, 0.0)

    state_ref[...] = jnp.zeros_like(state_ref)
    for group in range(GROUPS):
        count = min(z.rows, z.block - group * z.rows)
        state_ref[pl.ds(group * z.rows_pad, count), :] = start_ref[pl.ds(group * z.rows, count), :]
    state_ref[pl.ds(z.rows, 1), :] = jnp.ones((1, n), F32)
    state = lane_take(state_ref[...], perm[0:1])
    table = tables_of(state, pick_ref[...])
    table_ref[...] = table
    message_ref[...] = jnp.zeros_like(message_ref)
    row_id = lax.broadcasted_iota(jnp.int32, (z.trace_pad, n), 0)
    for group in range(3):
        where = sends_ref[0][group : group + 1]
        side = sends_ref[1][group : group + 1]
        message = jnp.zeros((z.trace_pad, n), F32)
        for face in range(FACES):
            piece = table[face * z.trace_pad : (face + 1) * z.trace_pad]
            message = jnp.where(side == face, lane_take(piece, where), message)
        message = jnp.where(row_id == z.wish, wish[group : group + 1], message)
        pack(z, message, group, curve_ref[0], jnp.zeros((1, n), F32), message_ref)


def blocks_kernel(z, inverse_ref, ints_ref, floats_ref, chunks_ref, near_ref, weights_ref, buffer_ref, sems):
    n = z.columns
    perm = ints_ref[1]
    lanes = lane_iota()
    depth = buffer_ref.shape[0]
    orders = [pltpu.roll(perm, group * z.width, 1) if group else perm for group in range(GROUPS)]
    bits = [jnp.bitwise_and(lanes // (z.width << b), 1) == 1 for b in range(3)]
    buffer_ref[:, :, z.block :, :] = jnp.zeros((depth, GROUPS, z.block_pad - z.block, n), F32)

    def copies(ii):
        for group in range(GROUPS):
            i = jnp.minimum(group * z.rows + ii, z.block - 1)
            slot = lax.rem(ii, depth)
            yield pltpu.make_async_copy(
                inverse_ref.at[i], buffer_ref.at[slot, group, pl.ds(0, z.block)], sems.at[slot, group]
            )

    for first in range(depth - 1):
        for copy in copies(first):
            copy.start()
    for chunk in range(GROUPS):
        own = chunk * z.width + jnp.bitwise_and(lanes, z.width - 1)
        near_ref[chunk] = lane_take(ints_ref[3], own)
        for at in range(3):
            weights_ref[chunk, at] = lane_take(floats_ref[at], own)

    def row(ii, carry):
        @pl.when(ii + depth - 1 < z.rows)
        def _():
            for copy in copies(ii + depth - 1):
                copy.start()

        for copy in copies(ii):
            copy.wait()
        slot = lax.rem(ii, depth)
        for tile in range(z.block_pad // SUB):
            at = pl.ds(tile * SUB, SUB)
            spread = [lane_take(buffer_ref[slot, group, at, :], orders[group]) for group in range(GROUPS)]
            for b in range(3):
                spread = [
                    jnp.where(bits[b], spread[(x + (1 << b)) % GROUPS], spread[x])
                    for x in range(GROUPS)
                ]
            for chunk in range(GROUPS):
                chunks_ref[chunk, ii, at, :] = spread[-chunk % GROUPS]
        return carry

    lax.fori_loop(0, z.rows, row, 0)


def first_base(z, traces, start_table_ref, ints_ref, floats_ref, right_ref, jac_ref, stack_ref, right_sorted_ref, base_ref):
    n = z.columns
    near = ints_ref[3]
    slot = ints_ref[4]
    for face in range(FACES):
        piece = start_table_ref[pl.ds((face ^ 1) * z.trace_pad, z.trace_pad), :]
        value = lane_take(piece, near[face : face + 1]) * floats_ref[3][face : face + 1]
        ghost = ghost_take(z, traces, slot, face) * floats_ref[6][face : face + 1]
        stack_ref[pl.ds(face * z.trace_pad, z.trace_pad), :] = value + ghost
    flow = fluxes(jac_ref[...], stack_ref[...])[: z.block_pad]
    right = jnp.concatenate([right_ref[...], jnp.zeros((z.block_pad - z.block, n), F32)], axis=0)
    right = lane_take(right, ints_ref[1][0:1])
    right_sorted_ref[...] = right
    base_ref[...] = right - flow


def send_kinds(z, traces, sends_ref, level_ref, kinds_ref):
    for group in range(3):
        wish = traces[group][z.wish : z.wish + 1] > 0.5
        side = sends_ref[1][group : group + 1]
        dep = sends_ref[2][group : group + 1]
        level = level_ref[...]
        kind = jnp.where(wish, jnp.where(dep <= level, 1, 3), jnp.where(dep >= level, 2, 1))
        kinds_ref[pl.ds(group, 1), :] = jnp.where(side < FACES, kind, 0)


def later_bases(z, traces, ints_ref, floats_ref, base_ref, right_ref, jac_ref, wide_ref, forward_base_ref, swept_base_ref):
    n = z.columns
    slot = ints_ref[4]
    missing_forward = jnp.zeros((1, n), F32)
    missing_swept = jnp.zeros((1, n), F32)
    for face in range(FACES):
        ghost = ghost_take(z, traces, slot, face)
        forward_weight = floats_ref[4][face : face + 1]
        swept_weight = floats_ref[5][face : face + 1]
        lost = jnp.where(ghost[z.flag : z.flag + 1] > 0.5, 0.0, 1.0)
        missing_forward += jnp.where(forward_weight > 0, lost, 0.0)
        missing_swept += jnp.where(swept_weight > 0, lost, 0.0)
        at = pl.ds(face * z.trace_pad, z.trace_pad)
        wide_ref[at, pl.ds(0, n)] = ghost * forward_weight
        wide_ref[at, pl.ds(n, n)] = ghost * swept_weight
    flow = fluxes(jac_ref[...], wide_ref[...])
    forward_base_ref[...] = base_ref[...] - flow[: z.block_pad, :n]
    swept_base_ref[...] = right_ref[...] - flow[: z.block_pad, n:]
    return missing_forward, missing_swept


def steps(
    z,
    span_ref,
    missing_forward,
    missing_swept,
    ints_ref,
    floats_ref,
    near_ref,
    weights_ref,
    jac_ref,
    pick_ref,
    chunks_ref,
    forward_table_ref,
    swept_table_ref,
    forward_ref,
    swept_ref,
    forward_base,
    swept_base,
    stack_ref,
    part_ref,
    fresh_ref,
):
    n = z.columns
    near = ints_ref[3]
    dep = ints_ref[2]
    chunk_of = lane_iota(1) // z.width
    per_sum = GROUPS // 2
    part_ref[...] = jnp.where(
        lax.broadcasted_iota(jnp.int32, (z.rows_pad, n), 0) == z.rows, 1.0, 0.0
    )

    def spread(row):
        return jnp.broadcast_to(row, (SUB, n))

    def absent(flags, weights):
        lost = jnp.where(weights > 0, 1.0 - lane_take(flags, near), 0.0)
        return jnp.sum(lost, axis=0, keepdims=True)

    old_forward = spread(forward_table_ref[pl.ds(z.flag, 1), :])
    old_swept = spread(swept_table_ref[pl.ds(z.flag, 1), :])
    forward, swept = old_forward, old_swept
    for level in range(z.levels):
        missing = absent(forward, floats_ref[0]) + missing_forward
        forward = jnp.where((dep == level) & spread(missing < 0.5), 1.0, forward)
    settled = absent(forward, floats_ref[2]) + missing_swept
    for level in range(z.levels - 1, -1, -1):
        missing = absent(swept, floats_ref[1]) + settled
        swept = jnp.where((dep == level) & spread(missing < 0.5), 1.0, swept)
    counts = []
    for at, fresh in enumerate((forward - old_forward, swept - old_swept)):
        fresh = fresh[0:1]
        fresh_ref[pl.ds(at, 1), :] = fresh
        for half in range(2):
            scale = jnp.zeros((1, n), F32)
            for at_chunk in range(per_sum):
                scale = jnp.where(chunk_of == half * per_sum + at_chunk, float((2 * z.width) ** at_chunk), scale)
            counts.append(jnp.sum(fresh * scale).astype(jnp.int32))

    def step(level, chunk, backward):
        old = forward_table_ref
        new = swept_table_ref
        base = swept_base if backward else forward_base
        rows = near_ref[chunk]
        old_weight = weights_ref[chunk, 2 if backward else 0]
        new_weight = weights_ref[chunk, 1]
        own = chunk * z.width + jnp.bitwise_and(lane_iota(1), z.width - 1)
        for face in range(FACES):
            at = pl.ds((face ^ 1) * z.trace_pad, z.trace_pad)
            row = rows[face : face + 1]
            value = lane_take(old[at, :], row) * old_weight[face : face + 1]
            if backward:
                value += lane_take(new[at, :], row) * new_weight[face : face + 1]
            stack_ref[pl.ds(face * z.trace_pad, z.trace_pad), :] = value
        flow = fluxes(jac_ref[...], stack_ref[...])[: z.block_pad]
        rest = lane_take(base[...], own) - flow
        for ii in range(z.rows):
            part_ref[pl.ds(ii, 1), :] = jnp.sum(chunks_ref[chunk, ii] * rest, axis=0, keepdims=True)
        part = part_ref[...]
        state = jnp.concatenate(
            [pltpu.roll(part, -g * z.width % n, 1) if g else part for g in range(GROUPS)], axis=0
        )
        table = tables_of(state, pick_ref[...])
        fresh = fresh_ref[pl.ds(1 if backward else 0, 1), :] > 0.5
        keep = fresh & (chunk_of == chunk) & (dep[0:1] == level)
        out_state = swept_ref if backward else forward_ref
        out_table = swept_table_ref if backward else forward_table_ref
        out_state[...] = jnp.where(keep, state, out_state[...])
        out_table[...] = jnp.where(keep, table, out_table[...])

    for backward in (False, True):
        low, high = counts[2 * backward], counts[2 * backward + 1]

        def run(count, carry, backward=backward, low=low, high=high):
            level = z.levels - 1 - count if backward else count

            def one(chunk, inner):
                bits = jnp.where(chunk >= per_sum, high, low)
                shift = (2 * z.width).bit_length() - 1
                bits = lax.shift_right_logical(bits, lax.rem(chunk, per_sum) * shift)

                @pl.when(jnp.bitwise_and(bits, 2 * z.width - 1) > 0)
                def _():
                    step(level, chunk, backward)

                return inner

            return lax.fori_loop(span_ref[level], span_ref[z.levels + level], one, carry)

        lax.fori_loop(0, z.levels, run, 0)


def send_messages(z, curve, sends_ref, kinds_ref, forward_table_ref, swept_table_ref, message_ref):
    n = z.columns
    row_id = lax.broadcasted_iota(jnp.int32, (z.trace_pad, n), 0)
    messages = []
    still = jnp.zeros((1, n), F32)
    for group in range(3):
        where = sends_ref[0][group : group + 1]
        side = sends_ref[1][group : group + 1]
        kind = kinds_ref[pl.ds(group, 1), :]
        message = jnp.zeros((z.trace_pad, n), F32)
        for face in range(FACES):
            at = pl.ds(face * z.trace_pad, z.trace_pad)
            first = lane_take(forward_table_ref[at, :], where)
            second = lane_take(swept_table_ref[at, :], where)
            picked = jnp.where(kind == 1, first, second)
            message = jnp.where(side == face, picked, message)
        message = jnp.where((kind == 3) & (row_id == z.flag), 2.0, message)
        unsent = (kind > 0) & (message[z.flag : z.flag + 1] < 0.5)
        still = jnp.maximum(still, jnp.where(unsent, 1.0, 0.0))
        messages.append(message)
    still = jnp.broadcast_to(jnp.max(still, axis=1, keepdims=True), (1, n))
    message_ref[...] = jnp.broadcast_to(still[None], message_ref.shape)
    for group in range(3):
        pack(z, messages[group], group, curve, still, message_ref)


def first_kernel(
    z,
    curve_ref,
    span_ref,
    right_ref,
    level_ref,
    start_table_ref,
    arrived_ref,
    ints_ref,
    floats_ref,
    sends_ref,
    near_ref,
    weights_ref,
    jac_ref,
    pick_ref,
    chunks_ref,
    message_ref,
    base_ref,
    right_sorted_ref,
    start_slots_ref,
    kinds_ref,
    forward_table_ref,
    swept_table_ref,
    forward_ref,
    swept_ref,
    stack_ref,
    part_ref,
    fresh_ref,
):
    n = z.columns
    curve = curve_ref[0]
    traces = [unpack(z, group, curve, arrived_ref) for group in range(3)]
    for group in range(3):
        start_slots_ref[group] = traces[group]
    send_kinds(z, traces, sends_ref, level_ref, kinds_ref)
    first_base(
        z, traces, start_table_ref, ints_ref, floats_ref, right_ref, jac_ref, stack_ref, right_sorted_ref, base_ref
    )
    forward_table_ref[...] = jnp.zeros_like(forward_table_ref)
    swept_table_ref[...] = jnp.zeros_like(swept_table_ref)
    forward_ref[...] = jnp.zeros_like(forward_ref)
    swept_ref[...] = jnp.zeros_like(swept_ref)
    missing_forward = jnp.sum(jnp.where(floats_ref[4] > 0, 1.0, 0.0), axis=0, keepdims=True)
    missing_swept = jnp.sum(jnp.where(floats_ref[5] > 0, 1.0, 0.0), axis=0, keepdims=True)
    steps(
        z,
        span_ref,
        missing_forward,
        missing_swept,
        ints_ref,
        floats_ref,
        near_ref,
        weights_ref,
        jac_ref,
        pick_ref,
        chunks_ref,
        forward_table_ref,
        swept_table_ref,
        forward_ref,
        swept_ref,
        base_ref,
        right_sorted_ref,
        stack_ref,
        part_ref,
        fresh_ref,
    )
    send_messages(z, curve, sends_ref, kinds_ref, forward_table_ref, swept_table_ref, message_ref)


def round_kernel(
    z,
    curve_ref,
    span_ref,
    arrived_ref,
    ints_ref,
    floats_ref,
    sends_ref,
    near_ref,
    weights_ref,
    jac_ref,
    pick_ref,
    chunks_ref,
    base_ref,
    right_ref,
    start_slots_ref,
    kinds_ref,
    forward_table_in,
    swept_table_in,
    forward_in,
    swept_in,
    message_ref,
    more_ref,
    forward_table_ref,
    swept_table_ref,
    forward_ref,
    swept_ref,
    stack_ref,
    part_ref,
    fresh_ref,
    wide_ref,
    forward_base_ref,
    swept_base_ref,
):
    n = z.columns
    curve = curve_ref[0]
    forward_table_ref[...] = forward_table_in[...]
    swept_table_ref[...] = swept_table_in[...]
    forward_ref[...] = forward_in[...]
    swept_ref[...] = swept_in[...]
    row_id = lax.broadcasted_iota(jnp.int32, (z.trace_pad, n), 0)
    still = jnp.max(arrived_ref[:, 0:1, :], axis=0)
    still = jnp.where(lane_iota(1) == n - 1, still, 0.0)
    more_ref[0] = jnp.max(still).astype(jnp.int32)
    traces = []
    for group in range(3):
        arrived = unpack(z, group, curve, arrived_ref)
        flag = arrived[z.flag : z.flag + 1]
        traces.append(jnp.where((flag > 1.5) & (row_id != z.flag), start_slots_ref[group], arrived))
    missing_forward, missing_swept = later_bases(
        z, traces, ints_ref, floats_ref, base_ref, right_ref, jac_ref, wide_ref, forward_base_ref, swept_base_ref
    )
    steps(
        z,
        span_ref,
        missing_forward,
        missing_swept,
        ints_ref,
        floats_ref,
        near_ref,
        weights_ref,
        jac_ref,
        pick_ref,
        chunks_ref,
        forward_table_ref,
        swept_table_ref,
        forward_ref,
        swept_ref,
        forward_base_ref,
        swept_base_ref,
        stack_ref,
        part_ref,
        fresh_ref,
    )
    send_messages(z, curve, sends_ref, kinds_ref, forward_table_ref, swept_table_ref, message_ref)


def output_kernel(z, ints_ref, forward_ref, swept_ref, forward_out, swept_out):
    pos = ints_ref[0][0:1]
    for source, target in ((forward_ref, forward_out), (swept_ref, swept_out)):
        for group in range(GROUPS):
            count = min(z.rows, z.block - group * z.rows)
            block = lane_take(source[pl.ds(group * z.rows_pad, z.rows_pad), :], pos)
            target[pl.ds(group * z.rows, count), :] = block[:count]


def call(kernel, outs, inputs, scratch=(), aliases=None, smem_in=(), smem_out=(), hbm_in=()):
    vmem, smem = pl.BlockSpec(memory_space=pltpu.VMEM), pl.BlockSpec(memory_space=pltpu.SMEM)
    hbm = pl.BlockSpec(memory_space=pltpu.HBM)
    return pl.pallas_call(
        kernel,
        out_shape=outs,
        in_specs=[smem if at in smem_in else hbm if at in hbm_in else vmem for at in range(inputs)],
        out_specs=[smem if at in smem_out else vmem for at in range(len(outs))],
        scratch_shapes=list(scratch),
        input_output_aliases=aliases or {},
        compiler_params=pltpu.CompilerParams(vmem_limit_bytes=24 << 20),
    )


def shape(*dims, kind=F32):
    return jax.ShapeDtypeStruct(dims, kind)


def kept(*dims, kind=F32):
    return pltpu.VMEM(dims, kind)


def body(
    start_state,
    right_side,
    block_inverse,
    lifted_flux_jacobian,
    face_weight,
    dep_level,
    face_link,
    send_list,
    recv_list,
):
    curves, slabs = lax.axis_size("curve"), lax.axis_size("slab")
    levels = send_list.shape[0]
    cap = send_list.shape[1] // (curves * slabs)
    slots = levels * cap
    block, n = start_state.shape
    z = Sizes(block, n, levels, slots, curves, slabs)
    own = lax.axis_index("curve").astype(jnp.int32)
    curve = own.reshape(1)

    def nearby(lists):
        grid = lists.reshape(levels, curves, slabs, cap).transpose(1, 2, 0, 3)
        grid = grid.reshape(curves, slabs * slots)
        grid = jnp.pad(grid, ((1, 1), (0, 0)), constant_values=FACES * n)
        picked = lax.dynamic_slice_in_dim(grid, own, 3, axis=0)
        return jnp.pad(picked, ((0, SUB - 3), (0, 0)), constant_values=FACES * n)

    send, recv = nearby(send_list), nearby(recv_list)
    link = jnp.pad(face_link, ((0, SUB - FACES), (0, 0)), constant_values=-1)
    weight = jnp.pad(face_weight, ((0, SUB - FACES), (0, 0)))
    slot_level = jnp.asarray(
        np.tile(np.repeat(np.arange(levels), cap), slabs).reshape(1, n), jnp.int32
    )
    pick = jnp.asarray(selector(z), BF16)
    jac = jnp.pad(
        lifted_flux_jacobian, ((0, 0), (0, z.jac_rows - block), (0, z.trace_pad - z.trace))
    )
    jac = jac.transpose(1, 0, 2).reshape(z.jac_rows, z.table_rows)
    rounded = lax.reduce_precision(jac, 8, 7)
    high, low = rounded.astype(BF16), (jac - rounded).astype(BF16)
    jac = jnp.concatenate([high, high, low], axis=1)

    ints, floats, sends, span, start_table, message = call(
        functools.partial(prepare_kernel, z),
        [
            kept(5, SUB, n, kind=jnp.int32),
            kept(7, SUB, n),
            kept(3, SUB, n, kind=jnp.int32),
            shape(2 * levels, kind=jnp.int32),
            kept(z.table_rows, n),
            shape(z.devices, 16, n),
        ],
        9,
        scratch=[pltpu.VMEM((z.state_rows, n), F32)],
        smem_in=(0,),
        smem_out=(3,),
    )(curve, start_state, dep_level.reshape(1, n), link, weight, send, recv, slot_level, pick)

    def exchange(message):
        return lax.all_to_all(message, ("curve", "slab"), 0, 0, tiled=True)

    arrived = exchange(message)
    depth = 4
    chunks, near, weights = call(
        functools.partial(blocks_kernel, z),
        [
            kept(GROUPS, z.rows, z.block_pad, n),
            kept(GROUPS, SUB, n, kind=jnp.int32),
            kept(GROUPS, 3, SUB, n),
        ],
        3,
        scratch=[
            pltpu.VMEM((depth, GROUPS, z.block_pad, n), F32),
            pltpu.SemaphoreType.DMA((depth, GROUPS)),
        ],
        hbm_in=(0,),
    )(block_inverse, ints, floats)

    tables = [
        kept(z.table_rows, n),
        kept(z.table_rows, n),
        kept(z.state_rows, n),
        kept(z.state_rows, n),
    ]
    scratch = [
        pltpu.VMEM((z.table_rows, n), F32),
        pltpu.VMEM((z.rows_pad, n), F32),
        pltpu.VMEM((SUB, n), F32),
    ]
    message, base, right, start_slots, kinds, *state = call(
        functools.partial(first_kernel, z),
        [
            shape(z.devices, 16, n),
            kept(z.block_pad, n),
            kept(z.block_pad, n),
            kept(3, z.trace_pad, n),
            kept(3, n, kind=jnp.int32),
        ]
        + tables,
        14,
        scratch=scratch,
        smem_in=(0, 1),
    )(
        curve,
        span,
        right_side,
        slot_level,
        start_table,
        arrived,
        ints,
        floats,
        sends,
        near,
        weights,
        jac,
        pick,
        chunks,
    )

    round_call = call(
        functools.partial(round_kernel, z),
        [shape(z.devices, 16, n), shape(1, kind=jnp.int32)] + tables,
        19,
        scratch=scratch
        + [
            pltpu.VMEM((z.table_rows, 2 * n), F32),
            pltpu.VMEM((z.block_pad, n), F32),
            pltpu.VMEM((z.block_pad, n), F32),
        ],
        aliases={15: 2, 16: 3, 17: 4, 18: 5},
        smem_in=(0, 1),
        smem_out=(1,),
    )

    def one_round(carry):
        _, message, state = carry
        message, more, *state = round_call(
            curve,
            span,
            exchange(message),
            ints,
            floats,
            sends,
            near,
            weights,
            jac,
            pick,
            chunks,
            base,
            right,
            start_slots,
            kinds,
            *state,
        )
        return more[0], message, tuple(state)

    start = (jnp.array(1, jnp.int32), message, tuple(state))
    _, _, state = lax.while_loop(lambda carry: carry[0] > 0, one_round, start)
    return tuple(
        call(functools.partial(output_kernel, z), [shape(block, n), shape(block, n)], 3)(
            ints, state[2], state[3]
        )
    )


def solution(mesh):
    split = ("curve", "slab")
    return jax.shard_map(
        body,
        mesh=mesh,
        in_specs=(
            P(None, split),
            P(None, split),
            P(None, None, split),
            P(),
            P(None, split),
            P(split),
            P(None, split),
            P(None, split),
            P(None, split),
        ),
        out_specs=(P(None, split), P(None, split)),
        check_vma=False,
    )
```

```python
import functools

import jax
import jax.numpy as jnp
import numpy as np
from jax import lax
from jax.experimental import pallas as pl
from jax.experimental.pallas import tpu as pltpu
from jax.sharding import PartitionSpec as P

VARS = 5
SIDE = 3
FACES = 6
LANES = 128
SUB = 8
GROUPS = 8
F32 = jnp.float32
BF16 = jnp.bfloat16


class Sizes:
    def __init__(self, block, columns, levels, slots, curves, slabs):
        self.block = block
        self.columns = columns
        self.levels = levels
        self.slots = slots
        self.curves = curves
        self.slabs = slabs
        self.devices = curves * slabs
        self.trace = VARS * SIDE * SIDE
        self.width = columns // GROUPS
        self.rows = -(-block // GROUPS)
        self.rows_pad = -(-(self.rows + 1) // SUB) * SUB
        self.state_rows = GROUPS * self.rows_pad
        self.block_pad = -(-block // SUB) * SUB
        self.flag = self.trace
        self.wish = self.trace + 1
        self.trace_pad = -(-(self.trace + 2) // 16) * 16
        self.cuts = self.trace_pad // 16
        self.table_rows = FACES * self.trace_pad
        self.jac_rows = -(-self.block_pad // 16) * 16
        assert columns == LANES and slabs * slots == LANES
        assert (self.cuts + 1) * slots <= LANES and block < self.block_pad


def face_rows():
    nodes = np.arange(VARS * SIDE**3).reshape(VARS, SIDE, SIDE, SIDE)
    last = SIDE - 1
    sides = [
        nodes[:, 0],
        nodes[:, last],
        nodes[:, :, 0],
        nodes[:, :, last],
        nodes[:, :, :, 0],
        nodes[:, :, :, last],
    ]
    return [side.reshape(-1) for side in sides]


def selector(z):
    pick = np.zeros((z.table_rows, z.state_rows), np.float32)
    for face, rows in enumerate(face_rows()):
        for h, i in enumerate(rows):
            pick[face * z.trace_pad + h, i // z.rows * z.rows_pad + i % z.rows] = 1
        pick[face * z.trace_pad + z.flag, z.rows] = 1
    return np.concatenate([pick, pick], axis=1)


def lane_take(values, index):
    index = jnp.broadcast_to(index, values.shape)
    return jnp.take_along_axis(values, index, axis=1, mode="promise_in_bounds")


def lane_iota(rows=SUB):
    return lax.broadcasted_iota(jnp.int32, (rows, LANES), 1)


def halves(values):
    high = values.astype(BF16)
    low = (values - high.astype(F32)).astype(BF16)
    return high, low


def as_column(row):
    return jnp.broadcast_to(row, (LANES, LANES)).T


def dot(a, b):
    return jnp.dot(a, b, preferred_element_type=F32)


def tables_of(state, pick):
    high, low = halves(state)
    return dot(pick, jnp.concatenate([high, low], axis=0))


def fluxes(jac, traces):
    high, low = halves(traces)
    return dot(jac, jnp.concatenate([high, low, high], axis=0))


def pack(z, message, group, curve, open_sends, out_ref):
    lanes = lane_iota(16)
    target = curve + group - 1

    @pl.when((target >= 0) & (target < z.curves))
    def _():
        for slab in range(z.slabs):
            block = jnp.broadcast_to(open_sends, (16, LANES))
            for cut in range(z.cuts):
                part = message[cut * 16 : cut * 16 + 16]
                shift = (cut - slab) * z.slots % LANES
                part = pltpu.roll(part, shift, 1) if shift else part
                block = jnp.where(lanes // z.slots == cut, part, block)
            out_ref[target * z.slabs + slab] = block


def unpack(z, group, curve, in_ref):
    lanes = lane_iota(16)
    source = jnp.clip(curve + group - 1, 0, z.curves - 1)
    blocks = [in_ref[source * z.slabs + slab] for slab in range(z.slabs)]
    parts = []
    for cut in range(z.cuts):
        part = jnp.zeros((16, LANES), F32)
        for slab in range(z.slabs):
            shift = (slab - cut) * z.slots % LANES
            block = pltpu.roll(blocks[slab], shift, 1) if shift else blocks[slab]
            part = jnp.where(lanes // z.slots == slab, block, part)
        parts.append(part)
    return jnp.concatenate(parts, axis=0)


def ghost_take(z, slot_traces, where, face):
    index = jnp.maximum(where[face : face + 1], 0)
    lane = jnp.bitwise_and(index, LANES - 1)
    block = index // LANES
    found = jnp.zeros((z.trace_pad, LANES), F32)
    for group in range(3):
        found = jnp.where(block == group, lane_take(slot_traces[group], lane), found)
    return found


def prepare_kernel(
    z,
    curve_ref,
    start_ref,
    dep_ref,
    link_ref,
    weight_ref,
    send_ref,
    recv_ref,
    level_ref,
    pick_ref,
    ints_ref,
    floats_ref,
    sends_ref,
    span_ref,
    table_ref,
    message_ref,
    state_ref,
):
    n = z.columns
    lanes = lane_iota()
    dep_row = dep_ref[...]
    dep = jnp.broadcast_to(dep_row, (SUB, n))
    key = (dep_row * n + lane_iota(1)).astype(F32)
    earlier = as_column(key) < jnp.broadcast_to(key, (n, n))
    pos_row = jnp.sum(jnp.where(earlier, 1.0, 0.0), axis=0, keepdims=True)
    here = as_column(pos_row) == lane_iota(n).astype(F32)
    element = lax.broadcasted_iota(jnp.int32, (n, n), 0).astype(F32)
    perm_row = jnp.sum(jnp.where(here, element, 0.0), axis=0, keepdims=True)
    pos = jnp.broadcast_to(pos_row.astype(jnp.int32), (SUB, n))
    perm = jnp.broadcast_to(perm_row.astype(jnp.int32), (SUB, n))
    dep_sorted = lane_take(dep, perm)
    for level in range(z.levels):
        before = jnp.sum(jnp.where(dep_row < level, 1.0, 0.0)).astype(jnp.int32)
        upto = jnp.sum(jnp.where(dep_row <= level, 1.0, 0.0)).astype(jnp.int32)
        span_ref[level] = before // z.width
        span_ref[z.levels + level] = jnp.where(upto > before, (upto + z.width - 1) // z.width, before // z.width)

    link = link_ref[...]
    near = jnp.where(link >= 0, lane_take(pos, jnp.maximum(link, 0)), -1)
    near = lane_take(near, perm)
    weight = lane_take(weight_ref[...], perm)
    local = near >= 0
    near = jnp.maximum(near, 0)
    dep_near = lane_take(dep_sorted, near)
    zero = jnp.zeros_like(weight)

    recv = recv_ref[...]
    slot_level = jnp.broadcast_to(level_ref[...], (SUB, n))
    rows = []
    slot_id = lax.broadcasted_iota(jnp.int32, (n, n), 0).astype(F32) + 1.0
    columns = [as_column(recv[group : group + 1].astype(F32)) for group in range(3)]
    for face in range(FACES):
        name = (lane_iota(n) + face * n).astype(F32)
        found = jnp.zeros((1, n), F32)
        for group in range(3):
            hit = jnp.where(columns[group] == name, slot_id + float(group * n), 0.0)
            found = jnp.maximum(found, jnp.max(hit, axis=0, keepdims=True))
        rows.append(found)
    rows.append(jnp.zeros((SUB - FACES, n), F32))
    slot = jnp.concatenate(rows, axis=0).astype(jnp.int32) - 1
    slot = lane_take(slot, perm)
    from_far = slot >= 0
    slot = jnp.maximum(slot, 0)
    far_level = lane_take(slot_level, jnp.bitwise_and(slot, n - 1))

    for at, value in enumerate((pos, perm, dep_sorted, near, slot)):
        ints_ref[at] = value
    floats_ref[0] = jnp.where(local & (dep_near < dep_sorted), weight, zero)
    floats_ref[1] = jnp.where(local & (dep_near > dep_sorted), weight, zero)
    floats_ref[2] = jnp.where(local & (dep_near <= dep_sorted), weight, zero)
    floats_ref[3] = jnp.where(local & (dep_near >= dep_sorted), weight, zero)
    floats_ref[4] = jnp.where(from_far & (far_level < dep_sorted), weight, zero)
    floats_ref[5] = jnp.where(from_far, weight, zero)
    floats_ref[6] = jnp.where(from_far & (far_level >= dep_sorted), weight, zero)

    send = send_ref[...]
    send_element = jnp.bitwise_and(send, n - 1)
    sends_ref[0] = lane_take(pos, send_element)
    sends_ref[1] = send // n
    sends_ref[2] = lane_take(dep, send_element)
    recv_dep = lane_take(dep, jnp.bitwise_and(recv, n - 1))
    wish = jnp.where(slot_level <= recv_dep, 1.0, 0.0)

    state_ref[...] = jnp.zeros_like(state_ref)
    for group in range(GROUPS):
        count = min(z.rows, z.block - group * z.rows)
        state_ref[pl.ds(group * z.rows_pad, count), :] = start_ref[pl.ds(group * z.rows, count), :]
    state_ref[pl.ds(z.rows, 1), :] = jnp.ones((1, n), F32)
    state = lane_take(state_ref[...], perm[0:1])
    table = tables_of(state, pick_ref[...])
    table_ref[...] = table
    message_ref[...] = jnp.zeros_like(message_ref)
    row_id = lax.broadcasted_iota(jnp.int32, (z.trace_pad, n), 0)
    for group in range(3):
        where = sends_ref[0][group : group + 1]
        side = sends_ref[1][group : group + 1]
        message = jnp.zeros((z.trace_pad, n), F32)
        for face in range(FACES):
            piece = table[face * z.trace_pad : (face + 1) * z.trace_pad]
            message = jnp.where(side == face, lane_take(piece, where), message)
        message = jnp.where(row_id == z.wish, wish[group : group + 1], message)
        pack(z, message, group, curve_ref[0], jnp.zeros((1, n), F32), message_ref)


def block_copies(z, ii, inverse_ref, buffer_ref, sems):
    slot = lax.rem(ii, buffer_ref.shape[0])
    for group in range(GROUPS):
        i = jnp.minimum(group * z.rows + ii, z.block - 1)
        yield pltpu.make_async_copy(
            inverse_ref.at[i], buffer_ref.at[slot, group, pl.ds(0, z.block)], sems.at[slot, group]
        )


def chunk_tables(z, ints_ref, floats_ref, near_ref, weights_ref):
    for chunk in range(GROUPS):
        own = chunk * z.width + jnp.bitwise_and(lane_iota(), z.width - 1)
        near_ref[chunk] = lane_take(ints_ref[3], own)
        for at in range(3):
            weights_ref[chunk, at] = lane_take(floats_ref[at], own)


def arrange_blocks(z, inverse_ref, ints_ref, chunks_ref, buffer_ref, sems):
    n = z.columns
    perm = ints_ref[1]
    depth = buffer_ref.shape[0]
    orders = [pltpu.roll(perm, group * z.width, 1) if group else perm for group in range(GROUPS)]
    bits = [jnp.bitwise_and(lane_iota() // (z.width << b), 1) == 1 for b in range(3)]

    def row(ii, carry):
        @pl.when(ii + depth - 1 < z.rows)
        def _():
            for copy in block_copies(z, ii + depth - 1, inverse_ref, buffer_ref, sems):
                copy.start()

        for copy in block_copies(z, ii, inverse_ref, buffer_ref, sems):
            copy.wait()
        slot = lax.rem(ii, depth)
        for tile in range(z.block_pad // SUB):
            at = pl.ds(tile * SUB, SUB)
            spread = [lane_take(buffer_ref[slot, group, at, :], orders[group]) for group in range(GROUPS)]
            for b in range(3):
                spread = [
                    jnp.where(bits[b], spread[(x + (1 << b)) % GROUPS], spread[x])
                    for x in range(GROUPS)
                ]
            for chunk in range(GROUPS):
                chunks_ref[chunk, ii, at, :] = spread[-chunk % GROUPS]
        return carry

    lax.fori_loop(0, z.rows, row, 0)


def first_base(z, traces, start_table_ref, ints_ref, floats_ref, right_ref, jac_ref, stack_ref, right_sorted_ref, base_ref):
    n = z.columns
    near = ints_ref[3]
    slot = ints_ref[4]
    for face in range(FACES):
        piece = start_table_ref[pl.ds((face ^ 1) * z.trace_pad, z.trace_pad), :]
        value = lane_take(piece, near[face : face + 1]) * floats_ref[3][face : face + 1]
        ghost = ghost_take(z, traces, slot, face) * floats_ref[6][face : face + 1]
        stack_ref[pl.ds(face * z.trace_pad, z.trace_pad), :] = value + ghost
    flow = fluxes(jac_ref[...], stack_ref[...])[: z.block_pad]
    right = jnp.concatenate([right_ref[...], jnp.zeros((z.block_pad - z.block, n), F32)], axis=0)
    right = lane_take(right, ints_ref[1][0:1])
    right_sorted_ref[...] = right
    base_ref[...] = right - flow


def send_kinds(z, traces, sends_ref, level_ref, kinds_ref):
    for group in range(3):
        wish = traces[group][z.wish : z.wish + 1] > 0.5
        side = sends_ref[1][group : group + 1]
        dep = sends_ref[2][group : group + 1]
        level = level_ref[...]
        kind = jnp.where(wish, jnp.where(dep <= level, 1, 3), jnp.where(dep >= level, 2, 1))
        kinds_ref[pl.ds(group, 1), :] = jnp.where(side < FACES, kind, 0)


def later_bases(z, traces, ints_ref, floats_ref, base_ref, right_ref, jac_ref, wide_ref, forward_base_ref, swept_base_ref):
    n = z.columns
    slot = ints_ref[4]
    missing_forward = jnp.zeros((1, n), F32)
    missing_swept = jnp.zeros((1, n), F32)
    for face in range(FACES):
        ghost = ghost_take(z, traces, slot, face)
        forward_weight = floats_ref[4][face : face + 1]
        swept_weight = floats_ref[5][face : face + 1]
        lost = jnp.where(ghost[z.flag : z.flag + 1] > 0.5, 0.0, 1.0)
        missing_forward += jnp.where(forward_weight > 0, lost, 0.0)
        missing_swept += jnp.where(swept_weight > 0, lost, 0.0)
        at = pl.ds(face * z.trace_pad, z.trace_pad)
        wide_ref[at, pl.ds(0, n)] = ghost * forward_weight
        wide_ref[at, pl.ds(n, n)] = ghost * swept_weight
    flow = fluxes(jac_ref[...], wide_ref[...])
    forward_base_ref[...] = base_ref[...] - flow[: z.block_pad, :n]
    swept_base_ref[...] = right_ref[...] - flow[: z.block_pad, n:]
    return missing_forward, missing_swept


def steps(
    z,
    span_ref,
    missing_forward,
    missing_swept,
    ints_ref,
    floats_ref,
    near_ref,
    weights_ref,
    jac_ref,
    pick_ref,
    chunks_ref,
    forward_table_ref,
    swept_table_ref,
    forward_ref,
    swept_ref,
    forward_base,
    swept_base,
    stack_ref,
    part_ref,
    fresh_ref,
):
    n = z.columns
    near = ints_ref[3]
    dep = ints_ref[2]
    chunk_of = lane_iota(1) // z.width
    per_sum = GROUPS // 2
    part_ref[...] = jnp.where(
        lax.broadcasted_iota(jnp.int32, (z.rows_pad, n), 0) == z.rows, 1.0, 0.0
    )

    def spread(row):
        return jnp.broadcast_to(row, (SUB, n))

    def absent(flags, weights):
        lost = jnp.where(weights > 0, 1.0 - lane_take(flags, near), 0.0)
        return jnp.sum(lost, axis=0, keepdims=True)

    old_forward = spread(forward_table_ref[pl.ds(z.flag, 1), :])
    old_swept = spread(swept_table_ref[pl.ds(z.flag, 1), :])
    forward, swept = old_forward, old_swept
    for level in range(z.levels):
        missing = absent(forward, floats_ref[0]) + missing_forward
        forward = jnp.where((dep == level) & spread(missing < 0.5), 1.0, forward)
    settled = absent(forward, floats_ref[2]) + missing_swept
    for level in range(z.levels - 1, -1, -1):
        missing = absent(swept, floats_ref[1]) + settled
        swept = jnp.where((dep == level) & spread(missing < 0.5), 1.0, swept)
    counts = []
    for at, fresh in enumerate((forward - old_forward, swept - old_swept)):
        fresh = fresh[0:1]
        fresh_ref[pl.ds(at, 1), :] = fresh
        for half in range(2):
            scale = jnp.zeros((1, n), F32)
            for at_chunk in range(per_sum):
                scale = jnp.where(chunk_of == half * per_sum + at_chunk, float((2 * z.width) ** at_chunk), scale)
            counts.append(jnp.sum(fresh * scale).astype(jnp.int32))

    def step(level, chunk, backward):
        old = forward_table_ref
        new = swept_table_ref
        base = swept_base if backward else forward_base
        rows = near_ref[chunk]
        old_weight = weights_ref[chunk, 2 if backward else 0]
        new_weight = weights_ref[chunk, 1]
        own = chunk * z.width + jnp.bitwise_and(lane_iota(1), z.width - 1)
        for face in range(FACES):
            at = pl.ds((face ^ 1) * z.trace_pad, z.trace_pad)
            row = rows[face : face + 1]
            value = lane_take(old[at, :], row) * old_weight[face : face + 1]
            if backward:
                value += lane_take(new[at, :], row) * new_weight[face : face + 1]
            stack_ref[pl.ds(face * z.trace_pad, z.trace_pad), :] = value
        flow = fluxes(jac_ref[...], stack_ref[...])[: z.block_pad]
        rest = lane_take(base[...], own) - flow
        for ii in range(z.rows):
            part_ref[pl.ds(ii, 1), :] = jnp.sum(chunks_ref[chunk, ii] * rest, axis=0, keepdims=True)
        part = part_ref[...]
        state = jnp.concatenate(
            [pltpu.roll(part, -g * z.width % n, 1) if g else part for g in range(GROUPS)], axis=0
        )
        table = tables_of(state, pick_ref[...])
        fresh = fresh_ref[pl.ds(1 if backward else 0, 1), :] > 0.5
        keep = fresh & (chunk_of == chunk) & (dep[0:1] == level)
        out_state = swept_ref if backward else forward_ref
        out_table = swept_table_ref if backward else forward_table_ref
        out_state[...] = jnp.where(keep, state, out_state[...])
        out_table[...] = jnp.where(keep, table, out_table[...])

    for backward in (False, True):
        low, high = counts[2 * backward], counts[2 * backward + 1]

        def run(count, carry, backward=backward, low=low, high=high):
            level = z.levels - 1 - count if backward else count

            def one(chunk, inner):
                bits = jnp.where(chunk >= per_sum, high, low)
                shift = (2 * z.width).bit_length() - 1
                bits = lax.shift_right_logical(bits, lax.rem(chunk, per_sum) * shift)

                @pl.when(jnp.bitwise_and(bits, 2 * z.width - 1) > 0)
                def _():
                    step(level, chunk, backward)

                return inner

            return lax.fori_loop(span_ref[level], span_ref[z.levels + level], one, carry)

        lax.fori_loop(0, z.levels, run, 0)


def send_messages(z, curve, sends_ref, kinds_ref, forward_table_ref, swept_table_ref, message_ref):
    n = z.columns
    row_id = lax.broadcasted_iota(jnp.int32, (z.trace_pad, n), 0)
    messages = []
    still = jnp.zeros((1, n), F32)
    for group in range(3):
        where = sends_ref[0][group : group + 1]
        side = sends_ref[1][group : group + 1]
        kind = kinds_ref[pl.ds(group, 1), :]
        message = jnp.zeros((z.trace_pad, n), F32)
        for face in range(FACES):
            at = pl.ds(face * z.trace_pad, z.trace_pad)
            first = lane_take(forward_table_ref[at, :], where)
            second = lane_take(swept_table_ref[at, :], where)
            picked = jnp.where(kind == 1, first, second)
            message = jnp.where(side == face, picked, message)
        message = jnp.where((kind == 3) & (row_id == z.flag), 2.0, message)
        unsent = (kind > 0) & (message[z.flag : z.flag + 1] < 0.5)
        still = jnp.maximum(still, jnp.where(unsent, 1.0, 0.0))
        messages.append(message)
    still = jnp.broadcast_to(jnp.max(still, axis=1, keepdims=True), (1, n))
    message_ref[...] = jnp.broadcast_to(still[None], message_ref.shape)
    for group in range(3):
        pack(z, messages[group], group, curve, still, message_ref)


def first_kernel(
    z,
    curve_ref,
    span_ref,
    right_ref,
    level_ref,
    start_table_ref,
    arrived_ref,
    ints_ref,
    floats_ref,
    sends_ref,
    jac_ref,
    pick_ref,
    inverse_ref,
    message_ref,
    base_ref,
    right_sorted_ref,
    start_slots_ref,
    kinds_ref,
    chunks_ref,
    near_ref,
    weights_ref,
    forward_table_ref,
    swept_table_ref,
    forward_ref,
    swept_ref,
    stack_ref,
    part_ref,
    fresh_ref,
    buffer_ref,
    sems,
):
    n = z.columns
    curve = curve_ref[0]
    depth = buffer_ref.shape[0]
    buffer_ref[:, :, z.block :, :] = jnp.zeros((depth, GROUPS, z.block_pad - z.block, n), F32)
    for first in range(depth - 1):
        for copy in block_copies(z, first, inverse_ref, buffer_ref, sems):
            copy.start()
    chunk_tables(z, ints_ref, floats_ref, near_ref, weights_ref)
    traces = [unpack(z, group, curve, arrived_ref) for group in range(3)]
    for group in range(3):
        start_slots_ref[group] = traces[group]
    send_kinds(z, traces, sends_ref, level_ref, kinds_ref)
    first_base(
        z, traces, start_table_ref, ints_ref, floats_ref, right_ref, jac_ref, stack_ref, right_sorted_ref, base_ref
    )
    forward_table_ref[...] = jnp.zeros_like(forward_table_ref)
    swept_table_ref[...] = jnp.zeros_like(swept_table_ref)
    forward_ref[...] = jnp.zeros_like(forward_ref)
    swept_ref[...] = jnp.zeros_like(swept_ref)
    arrange_blocks(z, inverse_ref, ints_ref, chunks_ref, buffer_ref, sems)
    missing_forward = jnp.sum(jnp.where(floats_ref[4] > 0, 1.0, 0.0), axis=0, keepdims=True)
    missing_swept = jnp.sum(jnp.where(floats_ref[5] > 0, 1.0, 0.0), axis=0, keepdims=True)
    steps(
        z,
        span_ref,
        missing_forward,
        missing_swept,
        ints_ref,
        floats_ref,
        near_ref,
        weights_ref,
        jac_ref,
        pick_ref,
        chunks_ref,
        forward_table_ref,
        swept_table_ref,
        forward_ref,
        swept_ref,
        base_ref,
        right_sorted_ref,
        stack_ref,
        part_ref,
        fresh_ref,
    )
    send_messages(z, curve, sends_ref, kinds_ref, forward_table_ref, swept_table_ref, message_ref)


def round_kernel(
    z,
    curve_ref,
    span_ref,
    arrived_ref,
    ints_ref,
    floats_ref,
    sends_ref,
    near_ref,
    weights_ref,
    jac_ref,
    pick_ref,
    chunks_ref,
    base_ref,
    right_ref,
    start_slots_ref,
    kinds_ref,
    forward_table_in,
    swept_table_in,
    forward_in,
    swept_in,
    message_ref,
    more_ref,
    forward_table_ref,
    swept_table_ref,
    forward_ref,
    swept_ref,
    stack_ref,
    part_ref,
    fresh_ref,
    wide_ref,
    forward_base_ref,
    swept_base_ref,
):
    n = z.columns
    curve = curve_ref[0]
    forward_table_ref[...] = forward_table_in[...]
    swept_table_ref[...] = swept_table_in[...]
    forward_ref[...] = forward_in[...]
    swept_ref[...] = swept_in[...]
    row_id = lax.broadcasted_iota(jnp.int32, (z.trace_pad, n), 0)
    still = jnp.max(arrived_ref[:, 0:1, :], axis=0)
    still = jnp.where(lane_iota(1) == n - 1, still, 0.0)
    more_ref[0] = jnp.max(still).astype(jnp.int32)
    traces = []
    for group in range(3):
        arrived = unpack(z, group, curve, arrived_ref)
        flag = arrived[z.flag : z.flag + 1]
        traces.append(jnp.where((flag > 1.5) & (row_id != z.flag), start_slots_ref[group], arrived))
    missing_forward, missing_swept = later_bases(
        z, traces, ints_ref, floats_ref, base_ref, right_ref, jac_ref, wide_ref, forward_base_ref, swept_base_ref
    )
    steps(
        z,
        span_ref,
        missing_forward,
        missing_swept,
        ints_ref,
        floats_ref,
        near_ref,
        weights_ref,
        jac_ref,
        pick_ref,
        chunks_ref,
        forward_table_ref,
        swept_table_ref,
        forward_ref,
        swept_ref,
        forward_base_ref,
        swept_base_ref,
        stack_ref,
        part_ref,
        fresh_ref,
    )
    send_messages(z, curve, sends_ref, kinds_ref, forward_table_ref, swept_table_ref, message_ref)


def output_kernel(z, ints_ref, forward_ref, swept_ref, forward_out, swept_out):
    pos = ints_ref[0][0:1]
    for source, target in ((forward_ref, forward_out), (swept_ref, swept_out)):
        for group in range(GROUPS):
            count = min(z.rows, z.block - group * z.rows)
            block = lane_take(source[pl.ds(group * z.rows_pad, z.rows_pad), :], pos)
            target[pl.ds(group * z.rows, count), :] = block[:count]


def call(kernel, outs, inputs, scratch=(), aliases=None, smem_in=(), smem_out=(), hbm_in=(), vmem=24):
    whole, smem = pl.BlockSpec(memory_space=pltpu.VMEM), pl.BlockSpec(memory_space=pltpu.SMEM)
    hbm = pl.BlockSpec(memory_space=pltpu.HBM)
    return pl.pallas_call(
        kernel,
        out_shape=outs,
        in_specs=[smem if at in smem_in else hbm if at in hbm_in else whole for at in range(inputs)],
        out_specs=[smem if at in smem_out else whole for at in range(len(outs))],
        scratch_shapes=list(scratch),
        input_output_aliases=aliases or {},
        compiler_params=pltpu.CompilerParams(vmem_limit_bytes=vmem << 20),
    )


def shape(*dims, kind=F32):
    return jax.ShapeDtypeStruct(dims, kind)


def kept(*dims, kind=F32):
    return pltpu.VMEM(dims, kind)


def body(
    start_state,
    right_side,
    block_inverse,
    lifted_flux_jacobian,
    face_weight,
    dep_level,
    face_link,
    send_list,
    recv_list,
):
    curves, slabs = lax.axis_size("curve"), lax.axis_size("slab")
    levels = send_list.shape[0]
    cap = send_list.shape[1] // (curves * slabs)
    slots = levels * cap
    block, n = start_state.shape
    z = Sizes(block, n, levels, slots, curves, slabs)
    own = lax.axis_index("curve").astype(jnp.int32)
    curve = own.reshape(1)

    def nearby(lists):
        grid = lists.reshape(levels, curves, slabs, cap).transpose(1, 2, 0, 3)
        grid = grid.reshape(curves, slabs * slots)
        grid = jnp.pad(grid, ((1, 1), (0, 0)), constant_values=FACES * n)
        picked = lax.dynamic_slice_in_dim(grid, own, 3, axis=0)
        return jnp.pad(picked, ((0, SUB - 3), (0, 0)), constant_values=FACES * n)

    send, recv = nearby(send_list), nearby(recv_list)
    link = jnp.pad(face_link, ((0, SUB - FACES), (0, 0)), constant_values=-1)
    weight = jnp.pad(face_weight, ((0, SUB - FACES), (0, 0)))
    slot_level = jnp.asarray(
        np.tile(np.repeat(np.arange(levels), cap), slabs).reshape(1, n), jnp.int32
    )
    pick = jnp.asarray(selector(z), BF16)
    jac = jnp.pad(
        lifted_flux_jacobian, ((0, 0), (0, z.jac_rows - block), (0, z.trace_pad - z.trace))
    )
    jac = jac.transpose(1, 0, 2).reshape(z.jac_rows, z.table_rows)
    rounded = lax.reduce_precision(jac, 8, 7)
    high, low = rounded.astype(BF16), (jac - rounded).astype(BF16)
    jac = jnp.concatenate([high, high, low], axis=1)

    ints, floats, sends, span, start_table, message = call(
        functools.partial(prepare_kernel, z),
        [
            kept(5, SUB, n, kind=jnp.int32),
            kept(7, SUB, n),
            kept(3, SUB, n, kind=jnp.int32),
            shape(2 * levels, kind=jnp.int32),
            kept(z.table_rows, n),
            shape(z.devices, 16, n),
        ],
        9,
        scratch=[pltpu.VMEM((z.state_rows, n), F32)],
        smem_in=(0,),
        smem_out=(3,),
    )(curve, start_state, dep_level.reshape(1, n), link, weight, send, recv, slot_level, pick)

    def exchange(message):
        return lax.all_to_all(message, ("curve", "slab"), 0, 0, tiled=True)

    arrived = exchange(message)
    tables = [
        kept(z.table_rows, n),
        kept(z.table_rows, n),
        kept(z.state_rows, n),
        kept(z.state_rows, n),
    ]
    scratch = [
        pltpu.VMEM((z.table_rows, n), F32),
        pltpu.VMEM((z.rows_pad, n), F32),
        pltpu.VMEM((SUB, n), F32),
    ]
    depth = 6
    message, base, right, start_slots, kinds, chunks, near, weights, *state = call(
        functools.partial(first_kernel, z),
        [
            shape(z.devices, 16, n),
            kept(z.block_pad, n),
            kept(z.block_pad, n),
            kept(3, z.trace_pad, n),
            kept(3, n, kind=jnp.int32),
            kept(GROUPS, z.rows, z.block_pad, n),
            kept(GROUPS, SUB, n, kind=jnp.int32),
            kept(GROUPS, 3, SUB, n),
        ]
        + tables,
        12,
        scratch=scratch
        + [
            pltpu.VMEM((depth, GROUPS, z.block_pad, n), F32),
            pltpu.SemaphoreType.DMA((depth, GROUPS)),
        ],
        smem_in=(0, 1),
        hbm_in=(11,),
        vmem=48,
    )(
        curve,
        span,
        right_side,
        slot_level,
        start_table,
        arrived,
        ints,
        floats,
        sends,
        jac,
        pick,
        block_inverse,
    )

    round_call = call(
        functools.partial(round_kernel, z),
        [shape(z.devices, 16, n), shape(1, kind=jnp.int32)] + tables,
        19,
        scratch=scratch
        + [
            pltpu.VMEM((z.table_rows, 2 * n), F32),
            pltpu.VMEM((z.block_pad, n), F32),
            pltpu.VMEM((z.block_pad, n), F32),
        ],
        aliases={15: 2, 16: 3, 17: 4, 18: 5},
        smem_in=(0, 1),
        smem_out=(1,),
    )

    def one_round(carry):
        _, message, state = carry
        message, more, *state = round_call(
            curve,
            span,
            exchange(message),
            ints,
            floats,
            sends,
            near,
            weights,
            jac,
            pick,
            chunks,
            base,
            right,
            start_slots,
            kinds,
            *state,
        )
        return more[0], message, tuple(state)

    start = (jnp.array(1, jnp.int32), message, tuple(state))
    _, _, state = lax.while_loop(lambda carry: carry[0] > 0, one_round, start)
    return tuple(
        call(functools.partial(output_kernel, z), [shape(block, n), shape(block, n)], 3)(
            ints, state[2], state[3]
        )
    )


def solution(mesh):
    split = ("curve", "slab")
    return jax.shard_map(
        body,
        mesh=mesh,
        in_specs=(
            P(None, split),
            P(None, split),
            P(None, None, split),
            P(),
            P(None, split),
            P(split),
            P(None, split),
            P(None, split),
            P(None, split),
        ),
        out_specs=(P(None, split), P(None, split)),
        check_vma=False,
    )
```

```python
import functools

import jax
import jax.numpy as jnp
import numpy as np
from jax import lax
from jax.experimental import pallas as pl
from jax.experimental.pallas import tpu as pltpu
from jax.sharding import PartitionSpec as P

VARS = 5
SIDE = 3
FACES = 6
LANES = 128
SUB = 8
GROUPS = 8
F32 = jnp.float32
BF16 = jnp.bfloat16


class Sizes:
    def __init__(self, block, columns, levels, slots, curves, slabs):
        self.block = block
        self.columns = columns
        self.levels = levels
        self.slots = slots
        self.curves = curves
        self.slabs = slabs
        self.devices = curves * slabs
        self.trace = VARS * SIDE * SIDE
        self.width = columns // GROUPS
        self.rows = -(-block // GROUPS)
        self.rows_pad = -(-(self.rows + 1) // SUB) * SUB
        self.state_rows = GROUPS * self.rows_pad
        self.block_pad = -(-block // SUB) * SUB
        self.flag = self.trace
        self.wish = self.trace + 1
        self.trace_pad = -(-(self.trace + 2) // 16) * 16
        self.cuts = self.trace_pad // 16
        self.table_rows = FACES * self.trace_pad
        self.jac_rows = -(-self.block_pad // 16) * 16
        assert columns == LANES and slabs * slots == LANES
        assert (self.cuts + 1) * slots <= LANES and block < self.block_pad


def face_rows():
    nodes = np.arange(VARS * SIDE**3).reshape(VARS, SIDE, SIDE, SIDE)
    last = SIDE - 1
    sides = [
        nodes[:, 0],
        nodes[:, last],
        nodes[:, :, 0],
        nodes[:, :, last],
        nodes[:, :, :, 0],
        nodes[:, :, :, last],
    ]
    return [side.reshape(-1) for side in sides]


def selector(z):
    pick = np.zeros((z.table_rows, z.state_rows), np.float32)
    for face, rows in enumerate(face_rows()):
        for h, i in enumerate(rows):
            pick[face * z.trace_pad + h, i // z.rows * z.rows_pad + i % z.rows] = 1
        pick[face * z.trace_pad + z.flag, z.rows] = 1
    return np.concatenate([pick, pick], axis=1)


def lane_take(values, index):
    index = jnp.broadcast_to(index, values.shape)
    return jnp.take_along_axis(values, index, axis=1, mode="promise_in_bounds")


def lane_iota(rows=SUB):
    return lax.broadcasted_iota(jnp.int32, (rows, LANES), 1)


def halves(values):
    high = values.astype(BF16)
    low = (values - high.astype(F32)).astype(BF16)
    return high, low


def as_column(row):
    return jnp.broadcast_to(row, (LANES, LANES)).T


def dot(a, b):
    return jnp.dot(a, b, preferred_element_type=F32)


def tables_of(state, pick):
    high, low = halves(state)
    return dot(pick, jnp.concatenate([high, low], axis=0))


def fluxes(jac, traces):
    high, low = halves(traces)
    return dot(jac, jnp.concatenate([high, low, high], axis=0))


def pack(z, message, group, curve, open_sends, out_ref):
    lanes = lane_iota(16)
    target = curve + group - 1

    @pl.when((target >= 0) & (target < z.curves))
    def _():
        for slab in range(z.slabs):
            block = jnp.broadcast_to(open_sends, (16, LANES))
            for cut in range(z.cuts):
                part = message[cut * 16 : cut * 16 + 16]
                shift = (cut - slab) * z.slots % LANES
                part = pltpu.roll(part, shift, 1) if shift else part
                block = jnp.where(lanes // z.slots == cut, part, block)
            out_ref[target * z.slabs + slab] = block


def unpack(z, group, curve, in_ref):
    lanes = lane_iota(16)
    source = jnp.clip(curve + group - 1, 0, z.curves - 1)
    blocks = [in_ref[source * z.slabs + slab] for slab in range(z.slabs)]
    parts = []
    for cut in range(z.cuts):
        part = jnp.zeros((16, LANES), F32)
        for slab in range(z.slabs):
            shift = (slab - cut) * z.slots % LANES
            block = pltpu.roll(blocks[slab], shift, 1) if shift else blocks[slab]
            part = jnp.where(lanes // z.slots == slab, block, part)
        parts.append(part)
    return jnp.concatenate(parts, axis=0)


def ghost_take(z, slot_traces, where, face):
    index = jnp.maximum(where[face : face + 1], 0)
    lane = jnp.bitwise_and(index, LANES - 1)
    block = index // LANES
    found = jnp.zeros((z.trace_pad, LANES), F32)
    for group in range(3):
        found = jnp.where(block == group, lane_take(slot_traces[group], lane), found)
    return found


def regroup(z, lists_ref, level_ref):
    n = z.columns
    cap = z.slots // z.levels
    lane = lane_iota(1)
    source = lane // z.slots * cap + jnp.bitwise_and(lane, cap - 1)
    row_id = lax.broadcasted_iota(jnp.int32, (z.levels, n), 0)
    own_row = row_id == level_ref[...]
    both = []
    for at in range(2):
        lists = lists_ref[pl.ds(at * z.levels, z.levels), :]
        rows = []
        for group in range(3):
            taken = lane_take(lists, source + group * z.slabs * cap)
            rows.append(jnp.sum(jnp.where(own_row, taken, 0).astype(F32), axis=0, keepdims=True))
        rows.append(jnp.full((SUB - 3, n), float(FACES * n), F32))
        both.append(jnp.concatenate(rows, axis=0).astype(jnp.int32))
    return both


def prepare_kernel(
    z,
    curve_ref,
    start_ref,
    dep_ref,
    link_ref,
    weight_ref,
    lists_ref,
    level_ref,
    pick_ref,
    ints_ref,
    floats_ref,
    sends_ref,
    span_ref,
    table_ref,
    message_ref,
    state_ref,
):
    n = z.columns
    lanes = lane_iota()
    dep_row = dep_ref[...]
    dep = jnp.broadcast_to(dep_row, (SUB, n))
    key = (dep_row * n + lane_iota(1)).astype(F32)
    earlier = as_column(key) < jnp.broadcast_to(key, (n, n))
    pos_row = jnp.sum(jnp.where(earlier, 1.0, 0.0), axis=0, keepdims=True)
    here = as_column(pos_row) == lane_iota(n).astype(F32)
    element = lax.broadcasted_iota(jnp.int32, (n, n), 0).astype(F32)
    perm_row = jnp.sum(jnp.where(here, element, 0.0), axis=0, keepdims=True)
    pos = jnp.broadcast_to(pos_row.astype(jnp.int32), (SUB, n))
    perm = jnp.broadcast_to(perm_row.astype(jnp.int32), (SUB, n))
    dep_sorted = lane_take(dep, perm)
    for level in range(z.levels):
        before = jnp.sum(jnp.where(dep_row < level, 1.0, 0.0)).astype(jnp.int32)
        upto = jnp.sum(jnp.where(dep_row <= level, 1.0, 0.0)).astype(jnp.int32)
        span_ref[level] = before // z.width
        span_ref[z.levels + level] = jnp.where(upto > before, (upto + z.width - 1) // z.width, before // z.width)

    link = jnp.concatenate([link_ref[...], jnp.full((SUB - FACES, n), -1, jnp.int32)], axis=0)
    near = jnp.where(link >= 0, lane_take(pos, jnp.maximum(link, 0)), -1)
    near = lane_take(near, perm)
    weight = jnp.concatenate([weight_ref[...], jnp.zeros((SUB - FACES, n), F32)], axis=0)
    weight = lane_take(weight, perm)
    local = near >= 0
    near = jnp.maximum(near, 0)
    dep_near = lane_take(dep_sorted, near)
    zero = jnp.zeros_like(weight)

    send, recv = regroup(z, lists_ref, level_ref)
    slot_level = jnp.broadcast_to(level_ref[...], (SUB, n))
    rows = []
    slot_id = lax.broadcasted_iota(jnp.int32, (n, n), 0).astype(F32) + 1.0
    columns = [as_column(recv[group : group + 1].astype(F32)) for group in range(3)]
    for face in range(FACES):
        name = (lane_iota(n) + face * n).astype(F32)
        found = jnp.zeros((1, n), F32)
        for group in range(3):
            hit = jnp.where(columns[group] == name, slot_id + float(group * n), 0.0)
            found = jnp.maximum(found, jnp.max(hit, axis=0, keepdims=True))
        rows.append(found)
    rows.append(jnp.zeros((SUB - FACES, n), F32))
    slot = jnp.concatenate(rows, axis=0).astype(jnp.int32) - 1
    slot = lane_take(slot, perm)
    from_far = slot >= 0
    slot = jnp.maximum(slot, 0)
    far_level = lane_take(slot_level, jnp.bitwise_and(slot, n - 1))

    for at, value in enumerate((pos, perm, dep_sorted, near, slot)):
        ints_ref[at] = value
    floats_ref[0] = jnp.where(local & (dep_near < dep_sorted), weight, zero)
    floats_ref[1] = jnp.where(local & (dep_near > dep_sorted), weight, zero)
    floats_ref[2] = jnp.where(local & (dep_near <= dep_sorted), weight, zero)
    floats_ref[3] = jnp.where(local & (dep_near >= dep_sorted), weight, zero)
    floats_ref[4] = jnp.where(from_far & (far_level < dep_sorted), weight, zero)
    floats_ref[5] = jnp.where(from_far, weight, zero)
    floats_ref[6] = jnp.where(from_far & (far_level >= dep_sorted), weight, zero)

    send_element = jnp.bitwise_and(send, n - 1)
    sends_ref[0] = lane_take(pos, send_element)
    sends_ref[1] = send // n
    sends_ref[2] = lane_take(dep, send_element)
    recv_dep = lane_take(dep, jnp.bitwise_and(recv, n - 1))
    wish = jnp.where(slot_level <= recv_dep, 1.0, 0.0)

    state_ref[...] = jnp.zeros_like(state_ref)
    for group in range(GROUPS):
        count = min(z.rows, z.block - group * z.rows)
        state_ref[pl.ds(group * z.rows_pad, count), :] = start_ref[pl.ds(group * z.rows, count), :]
    state_ref[pl.ds(z.rows, 1), :] = jnp.ones((1, n), F32)
    state = lane_take(state_ref[...], perm[0:1])
    table = tables_of(state, pick_ref[...])
    table_ref[...] = table
    message_ref[...] = jnp.zeros_like(message_ref)
    row_id = lax.broadcasted_iota(jnp.int32, (z.trace_pad, n), 0)
    for group in range(3):
        where = sends_ref[0][group : group + 1]
        side = sends_ref[1][group : group + 1]
        message = jnp.zeros((z.trace_pad, n), F32)
        for face in range(FACES):
            piece = table[face * z.trace_pad : (face + 1) * z.trace_pad]
            message = jnp.where(side == face, lane_take(piece, where), message)
        message = jnp.where(row_id == z.wish, wish[group : group + 1], message)
        pack(z, message, group, curve_ref[0], jnp.zeros((1, n), F32), message_ref)


def block_copies(z, ii, inverse_ref, buffer_ref, sems):
    slot = lax.rem(ii, buffer_ref.shape[0])
    for group in range(GROUPS):
        i = jnp.minimum(group * z.rows + ii, z.block - 1)
        yield pltpu.make_async_copy(
            inverse_ref.at[i], buffer_ref.at[slot, group, pl.ds(0, z.block)], sems.at[slot, group]
        )


def chunk_tables(z, ints_ref, floats_ref, near_ref, weights_ref):
    for chunk in range(GROUPS):
        own = chunk * z.width + jnp.bitwise_and(lane_iota(), z.width - 1)
        near_ref[chunk] = lane_take(ints_ref[3], own)
        for at in range(3):
            weights_ref[chunk, at] = lane_take(floats_ref[at], own)


def chunk_copy(ii, chunks_ref, out_ref, sems):
    return pltpu.make_async_copy(chunks_ref.at[:, ii], out_ref.at[:, ii], sems.at[ii])


def arrange_blocks(z, inverse_ref, ints_ref, chunks_ref, out_ref, buffer_ref, sems, out_sems):
    n = z.columns
    perm = ints_ref[1]
    depth = buffer_ref.shape[0]
    orders = [pltpu.roll(perm, group * z.width, 1) if group else perm for group in range(GROUPS)]
    bits = [jnp.bitwise_and(lane_iota() // (z.width << b), 1) == 1 for b in range(3)]

    def row(ii, carry):
        @pl.when(ii + depth - 1 < z.rows)
        def _():
            for copy in block_copies(z, ii + depth - 1, inverse_ref, buffer_ref, sems):
                copy.start()

        for copy in block_copies(z, ii, inverse_ref, buffer_ref, sems):
            copy.wait()
        slot = lax.rem(ii, depth)
        for tile in range(z.block_pad // SUB):
            at = pl.ds(tile * SUB, SUB)
            spread = [lane_take(buffer_ref[slot, group, at, :], orders[group]) for group in range(GROUPS)]
            for b in range(3):
                spread = [
                    jnp.where(bits[b], spread[(x + (1 << b)) % GROUPS], spread[x])
                    for x in range(GROUPS)
                ]
            for chunk in range(GROUPS):
                chunks_ref[chunk, ii, at, :] = spread[-chunk % GROUPS]
        chunk_copy(ii, chunks_ref, out_ref, out_sems).start()
        return carry

    lax.fori_loop(0, z.rows, row, 0)


def first_base(z, traces, start_table_ref, ints_ref, floats_ref, right_ref, jac_ref, stack_ref, right_sorted_ref, base_ref):
    n = z.columns
    near = ints_ref[3]
    slot = ints_ref[4]
    for face in range(FACES):
        piece = start_table_ref[pl.ds((face ^ 1) * z.trace_pad, z.trace_pad), :]
        value = lane_take(piece, near[face : face + 1]) * floats_ref[3][face : face + 1]
        ghost = ghost_take(z, traces, slot, face) * floats_ref[6][face : face + 1]
        stack_ref[pl.ds(face * z.trace_pad, z.trace_pad), :] = value + ghost
    flow = fluxes(jac_ref[...], stack_ref[...])[: z.block_pad]
    right = jnp.concatenate([right_ref[...], jnp.zeros((z.block_pad - z.block, n), F32)], axis=0)
    right = lane_take(right, ints_ref[1][0:1])
    right_sorted_ref[...] = right
    base_ref[...] = right - flow


def send_kinds(z, traces, sends_ref, level_ref, kinds_ref):
    for group in range(3):
        wish = traces[group][z.wish : z.wish + 1] > 0.5
        side = sends_ref[1][group : group + 1]
        dep = sends_ref[2][group : group + 1]
        level = level_ref[...]
        kind = jnp.where(wish, jnp.where(dep <= level, 1, 3), jnp.where(dep >= level, 2, 1))
        kinds_ref[pl.ds(group, 1), :] = jnp.where(side < FACES, kind, 0)


def later_bases(z, traces, ints_ref, floats_ref, base_ref, right_ref, jac_ref, wide_ref, forward_base_ref, swept_base_ref):
    n = z.columns
    slot = ints_ref[4]
    missing_forward = jnp.zeros((1, n), F32)
    missing_swept = jnp.zeros((1, n), F32)
    for face in range(FACES):
        ghost = ghost_take(z, traces, slot, face)
        forward_weight = floats_ref[4][face : face + 1]
        swept_weight = floats_ref[5][face : face + 1]
        lost = jnp.where(ghost[z.flag : z.flag + 1] > 0.5, 0.0, 1.0)
        missing_forward += jnp.where(forward_weight > 0, lost, 0.0)
        missing_swept += jnp.where(swept_weight > 0, lost, 0.0)
        at = pl.ds(face * z.trace_pad, z.trace_pad)
        wide_ref[at, pl.ds(0, n)] = ghost * forward_weight
        wide_ref[at, pl.ds(n, n)] = ghost * swept_weight
    flow = fluxes(jac_ref[...], wide_ref[...])
    forward_base_ref[...] = base_ref[...] - flow[: z.block_pad, :n]
    swept_base_ref[...] = right_ref[...] - flow[: z.block_pad, n:]
    return missing_forward, missing_swept


def steps(
    z,
    span_ref,
    missing_forward,
    missing_swept,
    ints_ref,
    floats_ref,
    near_ref,
    weights_ref,
    jac_ref,
    pick_ref,
    chunks_ref,
    forward_table_ref,
    swept_table_ref,
    forward_ref,
    swept_ref,
    forward_base,
    swept_base,
    stack_ref,
    part_ref,
    fresh_ref,
    fetches,
):
    n = z.columns
    near = ints_ref[3]
    dep = ints_ref[2]
    chunk_of = lane_iota(1) // z.width
    per_sum = GROUPS // 2
    part_ref[...] = jnp.where(
        lax.broadcasted_iota(jnp.int32, (z.rows_pad, n), 0) == z.rows, 1.0, 0.0
    )

    def spread(row):
        return jnp.broadcast_to(row, (SUB, n))

    def absent(flags, weights):
        lost = jnp.where(weights > 0, 1.0 - lane_take(flags, near), 0.0)
        return jnp.sum(lost, axis=0, keepdims=True)

    old_forward = spread(forward_table_ref[pl.ds(z.flag, 1), :])
    old_swept = spread(swept_table_ref[pl.ds(z.flag, 1), :])
    forward, swept = old_forward, old_swept
    for level in range(z.levels):
        missing = absent(forward, floats_ref[0]) + missing_forward
        forward = jnp.where((dep == level) & spread(missing < 0.5), 1.0, forward)
    settled = absent(forward, floats_ref[2]) + missing_swept
    for level in range(z.levels - 1, -1, -1):
        missing = absent(swept, floats_ref[1]) + settled
        swept = jnp.where((dep == level) & spread(missing < 0.5), 1.0, swept)
    counts = []
    for at, fresh in enumerate((forward - old_forward, swept - old_swept)):
        fresh = fresh[0:1]
        fresh_ref[pl.ds(at, 1), :] = fresh
        for half in range(2):
            scale = jnp.zeros((1, n), F32)
            for at_chunk in range(per_sum):
                scale = jnp.where(chunk_of == half * per_sum + at_chunk, float((2 * z.width) ** at_chunk), scale)
            counts.append(jnp.sum(fresh * scale).astype(jnp.int32))

    for fetch in fetches:
        fetch.wait()

    def step(level, chunk, backward):
        old = forward_table_ref
        new = swept_table_ref
        base = swept_base if backward else forward_base
        rows = near_ref[chunk]
        old_weight = weights_ref[chunk, 2 if backward else 0]
        new_weight = weights_ref[chunk, 1]
        own = chunk * z.width + jnp.bitwise_and(lane_iota(1), z.width - 1)
        for face in range(FACES):
            at = pl.ds((face ^ 1) * z.trace_pad, z.trace_pad)
            row = rows[face : face + 1]
            value = lane_take(old[at, :], row) * old_weight[face : face + 1]
            if backward:
                value += lane_take(new[at, :], row) * new_weight[face : face + 1]
            stack_ref[pl.ds(face * z.trace_pad, z.trace_pad), :] = value
        flow = fluxes(jac_ref[...], stack_ref[...])[: z.block_pad]
        rest = lane_take(base[...], own) - flow
        for ii in range(z.rows):
            part_ref[pl.ds(ii, 1), :] = jnp.sum(chunks_ref[chunk, ii] * rest, axis=0, keepdims=True)
        part = part_ref[...]
        state = jnp.concatenate(
            [pltpu.roll(part, -g * z.width % n, 1) if g else part for g in range(GROUPS)], axis=0
        )
        table = tables_of(state, pick_ref[...])
        fresh = fresh_ref[pl.ds(1 if backward else 0, 1), :] > 0.5
        keep = fresh & (chunk_of == chunk) & (dep[0:1] == level)
        out_state = swept_ref if backward else forward_ref
        out_table = swept_table_ref if backward else forward_table_ref
        out_state[...] = jnp.where(keep, state, out_state[...])
        out_table[...] = jnp.where(keep, table, out_table[...])

    for backward in (False, True):
        low, high = counts[2 * backward], counts[2 * backward + 1]

        def run(count, carry, backward=backward, low=low, high=high):
            level = z.levels - 1 - count if backward else count

            def one(chunk, inner):
                bits = jnp.where(chunk >= per_sum, high, low)
                shift = (2 * z.width).bit_length() - 1
                bits = lax.shift_right_logical(bits, lax.rem(chunk, per_sum) * shift)

                @pl.when(jnp.bitwise_and(bits, 2 * z.width - 1) > 0)
                def _():
                    step(level, chunk, backward)

                return inner

            return lax.fori_loop(span_ref[level], span_ref[z.levels + level], one, carry)

        lax.fori_loop(0, z.levels, run, 0)


def send_messages(z, curve, sends_ref, kinds_ref, forward_table_ref, swept_table_ref, message_ref):
    n = z.columns
    row_id = lax.broadcasted_iota(jnp.int32, (z.trace_pad, n), 0)
    messages = []
    still = jnp.zeros((1, n), F32)
    for group in range(3):
        where = sends_ref[0][group : group + 1]
        side = sends_ref[1][group : group + 1]
        kind = kinds_ref[pl.ds(group, 1), :]
        message = jnp.zeros((z.trace_pad, n), F32)
        for face in range(FACES):
            at = pl.ds(face * z.trace_pad, z.trace_pad)
            first = lane_take(forward_table_ref[at, :], where)
            second = lane_take(swept_table_ref[at, :], where)
            picked = jnp.where(kind == 1, first, second)
            message = jnp.where(side == face, picked, message)
        message = jnp.where((kind == 3) & (row_id == z.flag), 2.0, message)
        unsent = (kind > 0) & (message[z.flag : z.flag + 1] < 0.5)
        still = jnp.maximum(still, jnp.where(unsent, 1.0, 0.0))
        messages.append(message)
    still = jnp.broadcast_to(jnp.max(still, axis=1, keepdims=True), (1, n))
    message_ref[...] = jnp.broadcast_to(still[None], message_ref.shape)
    for group in range(3):
        pack(z, messages[group], group, curve, still, message_ref)


def first_kernel(
    z,
    curve_ref,
    span_ref,
    right_ref,
    level_ref,
    start_table_ref,
    arrived_ref,
    ints_ref,
    floats_ref,
    sends_ref,
    jac_ref,
    pick_ref,
    inverse_ref,
    message_ref,
    base_ref,
    right_sorted_ref,
    start_slots_ref,
    kinds_ref,
    chunks_out,
    near_ref,
    weights_ref,
    forward_table_ref,
    swept_table_ref,
    forward_ref,
    swept_ref,
    stack_ref,
    part_ref,
    fresh_ref,
    buffer_ref,
    chunks_ref,
    sems,
    out_sems,
):
    n = z.columns
    curve = curve_ref[0]
    depth = buffer_ref.shape[0]
    buffer_ref[:, :, z.block :, :] = jnp.zeros((depth, GROUPS, z.block_pad - z.block, n), F32)
    for first in range(depth - 1):
        for copy in block_copies(z, first, inverse_ref, buffer_ref, sems):
            copy.start()
    chunk_tables(z, ints_ref, floats_ref, near_ref, weights_ref)
    traces = [unpack(z, group, curve, arrived_ref) for group in range(3)]
    for group in range(3):
        start_slots_ref[group] = traces[group]
    send_kinds(z, traces, sends_ref, level_ref, kinds_ref)
    first_base(
        z, traces, start_table_ref, ints_ref, floats_ref, right_ref, jac_ref, stack_ref, right_sorted_ref, base_ref
    )
    forward_table_ref[...] = jnp.zeros_like(forward_table_ref)
    swept_table_ref[...] = jnp.zeros_like(swept_table_ref)
    forward_ref[...] = jnp.zeros_like(forward_ref)
    swept_ref[...] = jnp.zeros_like(swept_ref)
    arrange_blocks(z, inverse_ref, ints_ref, chunks_ref, chunks_out, buffer_ref, sems, out_sems)
    missing_forward = jnp.sum(jnp.where(floats_ref[4] > 0, 1.0, 0.0), axis=0, keepdims=True)
    missing_swept = jnp.sum(jnp.where(floats_ref[5] > 0, 1.0, 0.0), axis=0, keepdims=True)
    steps(
        z,
        span_ref,
        missing_forward,
        missing_swept,
        ints_ref,
        floats_ref,
        near_ref,
        weights_ref,
        jac_ref,
        pick_ref,
        chunks_ref,
        forward_table_ref,
        swept_table_ref,
        forward_ref,
        swept_ref,
        base_ref,
        right_sorted_ref,
        stack_ref,
        part_ref,
        fresh_ref,
        (),
    )
    send_messages(z, curve, sends_ref, kinds_ref, forward_table_ref, swept_table_ref, message_ref)
    for ii in range(z.rows):
        chunk_copy(ii, chunks_ref, chunks_out, out_sems).wait()


def round_kernel(
    z,
    curve_ref,
    span_ref,
    arrived_ref,
    ints_ref,
    floats_ref,
    sends_ref,
    near_ref,
    weights_ref,
    jac_ref,
    pick_ref,
    chunks_in,
    base_ref,
    right_ref,
    start_slots_ref,
    kinds_ref,
    forward_table_in,
    swept_table_in,
    forward_in,
    swept_in,
    message_ref,
    more_ref,
    forward_table_ref,
    swept_table_ref,
    forward_ref,
    swept_ref,
    stack_ref,
    part_ref,
    fresh_ref,
    wide_ref,
    forward_base_ref,
    swept_base_ref,
    chunks_ref,
    sems,
):
    n = z.columns
    curve = curve_ref[0]
    fetches = [
        pltpu.make_async_copy(chunks_in.at[chunk], chunks_ref.at[chunk], sems.at[chunk]) for chunk in range(GROUPS)
    ]
    for fetch in fetches:
        fetch.start()
    forward_table_ref[...] = forward_table_in[...]
    swept_table_ref[...] = swept_table_in[...]
    forward_ref[...] = forward_in[...]
    swept_ref[...] = swept_in[...]
    row_id = lax.broadcasted_iota(jnp.int32, (z.trace_pad, n), 0)
    still = jnp.max(arrived_ref[:, 0:1, :], axis=0)
    still = jnp.where(lane_iota(1) == n - 1, still, 0.0)
    more_ref[0] = jnp.max(still).astype(jnp.int32)
    traces = []
    for group in range(3):
        arrived = unpack(z, group, curve, arrived_ref)
        flag = arrived[z.flag : z.flag + 1]
        traces.append(jnp.where((flag > 1.5) & (row_id != z.flag), start_slots_ref[group], arrived))
    missing_forward, missing_swept = later_bases(
        z, traces, ints_ref, floats_ref, base_ref, right_ref, jac_ref, wide_ref, forward_base_ref, swept_base_ref
    )
    steps(
        z,
        span_ref,
        missing_forward,
        missing_swept,
        ints_ref,
        floats_ref,
        near_ref,
        weights_ref,
        jac_ref,
        pick_ref,
        chunks_ref,
        forward_table_ref,
        swept_table_ref,
        forward_ref,
        swept_ref,
        forward_base_ref,
        swept_base_ref,
        stack_ref,
        part_ref,
        fresh_ref,
        fetches,
    )
    send_messages(z, curve, sends_ref, kinds_ref, forward_table_ref, swept_table_ref, message_ref)


def output_kernel(z, ints_ref, forward_ref, swept_ref, forward_out, swept_out):
    pos = ints_ref[0][0:1]
    for source, target in ((forward_ref, forward_out), (swept_ref, swept_out)):
        for group in range(GROUPS):
            count = min(z.rows, z.block - group * z.rows)
            block = lane_take(source[pl.ds(group * z.rows_pad, z.rows_pad), :], pos)
            target[pl.ds(group * z.rows, count), :] = block[:count]


def call(kernel, outs, inputs, scratch=(), aliases=None, smem_in=(), smem_out=(), hbm_in=(), hbm_out=(), vmem=24):
    whole, smem = pl.BlockSpec(memory_space=pltpu.VMEM), pl.BlockSpec(memory_space=pltpu.SMEM)
    hbm = pl.BlockSpec(memory_space=pltpu.HBM)
    return pl.pallas_call(
        kernel,
        out_shape=outs,
        in_specs=[smem if at in smem_in else hbm if at in hbm_in else whole for at in range(inputs)],
        out_specs=[smem if at in smem_out else hbm if at in hbm_out else whole for at in range(len(outs))],
        scratch_shapes=list(scratch),
        input_output_aliases=aliases or {},
        compiler_params=pltpu.CompilerParams(vmem_limit_bytes=vmem << 20),
    )


def shape(*dims, kind=F32):
    return jax.ShapeDtypeStruct(dims, kind)


def kept(*dims, kind=F32):
    return pltpu.VMEM(dims, kind)


def body(
    start_state,
    right_side,
    block_inverse,
    lifted_flux_jacobian,
    face_weight,
    dep_level,
    face_link,
    send_list,
    recv_list,
):
    curves, slabs = lax.axis_size("curve"), lax.axis_size("slab")
    levels = send_list.shape[0]
    cap = send_list.shape[1] // (curves * slabs)
    slots = levels * cap
    block, n = start_state.shape
    z = Sizes(block, n, levels, slots, curves, slabs)
    own = lax.axis_index("curve").astype(jnp.int32)
    curve = own.reshape(1)

    stride = slabs * cap
    lists = jnp.concatenate([send_list, recv_list], axis=0)
    lists = jnp.pad(lists, ((0, 0), (stride, n)), constant_values=FACES * n)
    lists = lax.dynamic_slice_in_dim(lists, own * stride, n, axis=1)
    slot_level = jnp.asarray(
        np.tile(np.repeat(np.arange(levels), cap), slabs).reshape(1, n), jnp.int32
    )
    pick = jnp.asarray(selector(z), BF16)
    jac = jnp.pad(
        lifted_flux_jacobian, ((0, 0), (0, z.jac_rows - block), (0, z.trace_pad - z.trace))
    )
    jac = jac.transpose(1, 0, 2).reshape(z.jac_rows, z.table_rows)
    rounded = lax.reduce_precision(jac, 8, 7)
    high, low = rounded.astype(BF16), (jac - rounded).astype(BF16)
    jac = jnp.concatenate([high, high, low], axis=1)

    ints, floats, sends, span, start_table, message = call(
        functools.partial(prepare_kernel, z),
        [
            kept(5, SUB, n, kind=jnp.int32),
            kept(7, SUB, n),
            kept(3, SUB, n, kind=jnp.int32),
            shape(2 * levels, kind=jnp.int32),
            kept(z.table_rows, n),
            shape(z.devices, 16, n),
        ],
        8,
        scratch=[pltpu.VMEM((z.state_rows, n), F32)],
        smem_in=(0,),
        smem_out=(3,),
        vmem=60,
    )(curve, start_state, dep_level.reshape(1, n), face_link, face_weight, lists, slot_level, pick)
    message, jac = lax.optimization_barrier((message, jac))

    def exchange(message):
        return lax.all_to_all(message, ("curve", "slab"), 0, 0, tiled=True)

    arrived = exchange(message)
    tables = [
        kept(z.table_rows, n),
        kept(z.table_rows, n),
        kept(z.state_rows, n),
        kept(z.state_rows, n),
    ]
    scratch = [
        pltpu.VMEM((z.table_rows, n), F32),
        pltpu.VMEM((z.rows_pad, n), F32),
        pltpu.VMEM((SUB, n), F32),
    ]
    depth = 6
    message, base, right, start_slots, kinds, chunks, near, weights, *state = call(
        functools.partial(first_kernel, z),
        [
            shape(z.devices, 16, n),
            kept(z.block_pad, n),
            kept(z.block_pad, n),
            kept(3, z.trace_pad, n),
            kept(3, n, kind=jnp.int32),
            shape(GROUPS, z.rows, z.block_pad, n),
            kept(GROUPS, SUB, n, kind=jnp.int32),
            kept(GROUPS, 3, SUB, n),
        ]
        + tables,
        12,
        scratch=scratch
        + [
            pltpu.VMEM((depth, GROUPS, z.block_pad, n), F32),
            pltpu.VMEM((GROUPS, z.rows, z.block_pad, n), F32),
            pltpu.SemaphoreType.DMA((depth, GROUPS)),
            pltpu.SemaphoreType.DMA((z.rows,)),
        ],
        smem_in=(0, 1),
        hbm_in=(11,),
        hbm_out=(5,),
        vmem=56,
    )(
        curve,
        span,
        right_side,
        slot_level,
        start_table,
        arrived,
        ints,
        floats,
        sends,
        jac,
        pick,
        block_inverse,
    )

    round_call = call(
        functools.partial(round_kernel, z),
        [shape(z.devices, 16, n), shape(1, kind=jnp.int32)] + tables,
        19,
        scratch=scratch
        + [
            pltpu.VMEM((z.table_rows, 2 * n), F32),
            pltpu.VMEM((z.block_pad, n), F32),
            pltpu.VMEM((z.block_pad, n), F32),
            pltpu.VMEM((GROUPS, z.rows, z.block_pad, n), F32),
            pltpu.SemaphoreType.DMA((GROUPS,)),
        ],
        hbm_in=(10,),
        vmem=56,
        aliases={15: 2, 16: 3, 17: 4, 18: 5},
        smem_in=(0, 1),
        smem_out=(1,),
    )

    def one_round(carry):
        _, message, state = carry
        message, more, *state = round_call(
            curve,
            span,
            exchange(message),
            ints,
            floats,
            sends,
            near,
            weights,
            jac,
            pick,
            chunks,
            base,
            right,
            start_slots,
            kinds,
            *state,
        )
        return more[0], message, tuple(state)

    start = (jnp.array(1, jnp.int32), message, tuple(state))
    _, _, state = lax.while_loop(lambda carry: carry[0] > 0, one_round, start)
    return tuple(
        call(functools.partial(output_kernel, z), [shape(block, n), shape(block, n)], 3)(
            ints, state[2], state[3]
        )
    )


def solution(mesh):
    split = ("curve", "slab")
    return jax.shard_map(
        body,
        mesh=mesh,
        in_specs=(
            P(None, split),
            P(None, split),
            P(None, None, split),
            P(),
            P(None, split),
            P(split),
            P(None, split),
            P(None, split),
            P(None, split),
        ),
        out_specs=(P(None, split), P(None, split)),
        check_vma=False,
    )
```

```python
import functools

import jax
import jax.numpy as jnp
import numpy as np
from jax import lax
from jax.experimental import pallas as pl
from jax.experimental.pallas import tpu as pltpu
from jax.sharding import PartitionSpec as P

VARS = 5
SIDE = 3
FACES = 6
LANES = 128
SUB = 8
GROUPS = 8
F32 = jnp.float32
BF16 = jnp.bfloat16


class Sizes:
    def __init__(self, block, columns, levels, slots, curves, slabs):
        self.block = block
        self.columns = columns
        self.levels = levels
        self.slots = slots
        self.curves = curves
        self.slabs = slabs
        self.devices = curves * slabs
        self.trace = VARS * SIDE * SIDE
        self.width = columns // GROUPS
        self.rows = -(-block // GROUPS)
        self.rows_pad = -(-(self.rows + 1) // SUB) * SUB
        self.state_rows = GROUPS * self.rows_pad
        self.block_pad = -(-block // SUB) * SUB
        self.flag = self.trace
        self.wish = self.trace + 1
        self.trace_pad = -(-(self.trace + 2) // 16) * 16
        self.cuts = self.trace_pad // 16
        self.table_rows = FACES * self.trace_pad
        self.jac_rows = -(-self.block_pad // 16) * 16
        assert columns == LANES and slabs * slots == LANES
        assert (self.cuts + 1) * slots <= LANES and block < self.block_pad


def face_rows():
    nodes = np.arange(VARS * SIDE**3).reshape(VARS, SIDE, SIDE, SIDE)
    last = SIDE - 1
    sides = [
        nodes[:, 0],
        nodes[:, last],
        nodes[:, :, 0],
        nodes[:, :, last],
        nodes[:, :, :, 0],
        nodes[:, :, :, last],
    ]
    return [side.reshape(-1) for side in sides]


def selector(z):
    pick = np.zeros((z.table_rows, z.state_rows), np.float32)
    for face, rows in enumerate(face_rows()):
        for h, i in enumerate(rows):
            pick[face * z.trace_pad + h, i // z.rows * z.rows_pad + i % z.rows] = 1
        pick[face * z.trace_pad + z.flag, z.rows] = 1
    return np.concatenate([pick, pick], axis=1)


def lane_take(values, index):
    index = jnp.broadcast_to(index, values.shape)
    return jnp.take_along_axis(values, index, axis=1, mode="promise_in_bounds")


def lane_iota(rows=SUB):
    return lax.broadcasted_iota(jnp.int32, (rows, LANES), 1)


def halves(values):
    high = values.astype(BF16)
    low = (values - high.astype(F32)).astype(BF16)
    return high, low


def as_column(row):
    return jnp.broadcast_to(row, (LANES, LANES)).T


def dot(a, b):
    return jnp.dot(a, b, preferred_element_type=F32)


def tables_of(state, pick):
    high, low = halves(state)
    return dot(pick, jnp.concatenate([high, low], axis=0))


def fluxes(jac, traces):
    high, low = halves(traces)
    return dot(jac, jnp.concatenate([high, low, high], axis=0))


def pack(z, message, group, curve, open_sends, out_ref):
    lanes = lane_iota(16)
    target = curve + group - 1

    @pl.when((target >= 0) & (target < z.curves))
    def _():
        for slab in range(z.slabs):
            block = jnp.broadcast_to(open_sends, (16, LANES))
            for cut in range(z.cuts):
                part = message[cut * 16 : cut * 16 + 16]
                shift = (cut - slab) * z.slots % LANES
                part = pltpu.roll(part, shift, 1) if shift else part
                block = jnp.where(lanes // z.slots == cut, part, block)
            out_ref[target * z.slabs + slab] = block


def unpack(z, group, curve, in_ref):
    lanes = lane_iota(16)
    source = jnp.clip(curve + group - 1, 0, z.curves - 1)
    blocks = [in_ref[source * z.slabs + slab] for slab in range(z.slabs)]
    parts = []
    for cut in range(z.cuts):
        part = jnp.zeros((16, LANES), F32)
        for slab in range(z.slabs):
            shift = (slab - cut) * z.slots % LANES
            block = pltpu.roll(blocks[slab], shift, 1) if shift else blocks[slab]
            part = jnp.where(lanes // z.slots == slab, block, part)
        parts.append(part)
    return jnp.concatenate(parts, axis=0)


def ghost_take(z, slot_traces, where, face):
    index = jnp.maximum(where[face : face + 1], 0)
    lane = jnp.bitwise_and(index, LANES - 1)
    block = index // LANES
    found = jnp.zeros((z.trace_pad, LANES), F32)
    for group in range(3):
        found = jnp.where(block == group, lane_take(slot_traces[group], lane), found)
    return found


def regroup(z, lists_ref, level_ref):
    n = z.columns
    cap = z.slots // z.levels
    lane = lane_iota(1)
    source = lane // z.slots * cap + jnp.bitwise_and(lane, cap - 1)
    row_id = lax.broadcasted_iota(jnp.int32, (z.levels, n), 0)
    own_row = row_id == level_ref[...]
    both = []
    for at in range(2):
        lists = lists_ref[pl.ds(at * z.levels, z.levels), :]
        rows = []
        for group in range(3):
            taken = lane_take(lists, source + group * z.slabs * cap)
            rows.append(jnp.sum(jnp.where(own_row, taken, 0).astype(F32), axis=0, keepdims=True))
        rows.append(jnp.full((SUB - 3, n), float(FACES * n), F32))
        both.append(jnp.concatenate(rows, axis=0).astype(jnp.int32))
    return both


def prepare_kernel(
    z,
    curve_ref,
    start_ref,
    dep_ref,
    link_ref,
    weight_ref,
    lists_ref,
    level_ref,
    pick_ref,
    ints_ref,
    floats_ref,
    sends_ref,
    span_ref,
    table_ref,
    message_ref,
    state_ref,
):
    n = z.columns
    lanes = lane_iota()
    dep_row = dep_ref[...]
    dep = jnp.broadcast_to(dep_row, (SUB, n))
    key = (dep_row * n + lane_iota(1)).astype(F32)
    earlier = as_column(key) < jnp.broadcast_to(key, (n, n))
    pos_row = jnp.sum(jnp.where(earlier, 1.0, 0.0), axis=0, keepdims=True)
    here = as_column(pos_row) == lane_iota(n).astype(F32)
    element = lax.broadcasted_iota(jnp.int32, (n, n), 0).astype(F32)
    perm_row = jnp.sum(jnp.where(here, element, 0.0), axis=0, keepdims=True)
    pos = jnp.broadcast_to(pos_row.astype(jnp.int32), (SUB, n))
    perm = jnp.broadcast_to(perm_row.astype(jnp.int32), (SUB, n))
    dep_sorted = lane_take(dep, perm)
    for level in range(z.levels):
        before = jnp.sum(jnp.where(dep_row < level, 1.0, 0.0)).astype(jnp.int32)
        upto = jnp.sum(jnp.where(dep_row <= level, 1.0, 0.0)).astype(jnp.int32)
        span_ref[level] = before // z.width
        span_ref[z.levels + level] = jnp.where(upto > before, (upto + z.width - 1) // z.width, before // z.width)

    span_ref[2 * z.levels] = 1

    link = jnp.concatenate([link_ref[...], jnp.full((SUB - FACES, n), -1, jnp.int32)], axis=0)
    near = jnp.where(link >= 0, lane_take(pos, jnp.maximum(link, 0)), -1)
    near = lane_take(near, perm)
    weight = jnp.concatenate([weight_ref[...], jnp.zeros((SUB - FACES, n), F32)], axis=0)
    weight = lane_take(weight, perm)
    local = near >= 0
    near = jnp.maximum(near, 0)
    dep_near = lane_take(dep_sorted, near)
    zero = jnp.zeros_like(weight)

    send, recv = regroup(z, lists_ref, level_ref)
    slot_level = jnp.broadcast_to(level_ref[...], (SUB, n))
    rows = []
    slot_id = lax.broadcasted_iota(jnp.int32, (n, n), 0).astype(F32) + 1.0
    columns = [as_column(recv[group : group + 1].astype(F32)) for group in range(3)]
    for face in range(FACES):
        name = (lane_iota(n) + face * n).astype(F32)
        found = jnp.zeros((1, n), F32)
        for group in range(3):
            hit = jnp.where(columns[group] == name, slot_id + float(group * n), 0.0)
            found = jnp.maximum(found, jnp.max(hit, axis=0, keepdims=True))
        rows.append(found)
    rows.append(jnp.zeros((SUB - FACES, n), F32))
    slot = jnp.concatenate(rows, axis=0).astype(jnp.int32) - 1
    slot = lane_take(slot, perm)
    from_far = slot >= 0
    slot = jnp.maximum(slot, 0)
    far_level = lane_take(slot_level, jnp.bitwise_and(slot, n - 1))

    for at, value in enumerate((pos, perm, dep_sorted, near, slot)):
        ints_ref[at] = value
    floats_ref[0] = jnp.where(local & (dep_near < dep_sorted), weight, zero)
    floats_ref[1] = jnp.where(local & (dep_near > dep_sorted), weight, zero)
    floats_ref[2] = jnp.where(local & (dep_near <= dep_sorted), weight, zero)
    floats_ref[3] = jnp.where(local & (dep_near >= dep_sorted), weight, zero)
    floats_ref[4] = jnp.where(from_far & (far_level < dep_sorted), weight, zero)
    floats_ref[5] = jnp.where(from_far, weight, zero)
    floats_ref[6] = jnp.where(from_far & (far_level >= dep_sorted), weight, zero)

    send_element = jnp.bitwise_and(send, n - 1)
    sends_ref[0] = lane_take(pos, send_element)
    sends_ref[1] = send // n
    sends_ref[2] = lane_take(dep, send_element)
    recv_dep = lane_take(dep, jnp.bitwise_and(recv, n - 1))
    wish = jnp.where(slot_level <= recv_dep, 1.0, 0.0)

    state_ref[...] = jnp.zeros_like(state_ref)
    for group in range(GROUPS):
        count = min(z.rows, z.block - group * z.rows)
        state_ref[pl.ds(group * z.rows_pad, count), :] = start_ref[pl.ds(group * z.rows, count), :]
    state_ref[pl.ds(z.rows, 1), :] = jnp.ones((1, n), F32)
    state = lane_take(state_ref[...], perm[0:1])
    table = tables_of(state, pick_ref[...])
    table_ref[...] = table
    message_ref[...] = jnp.zeros_like(message_ref)
    row_id = lax.broadcasted_iota(jnp.int32, (z.trace_pad, n), 0)
    for group in range(3):
        where = sends_ref[0][group : group + 1]
        side = sends_ref[1][group : group + 1]
        message = jnp.zeros((z.trace_pad, n), F32)
        for face in range(FACES):
            piece = table[face * z.trace_pad : (face + 1) * z.trace_pad]
            message = jnp.where(side == face, lane_take(piece, where), message)
        message = jnp.where(row_id == z.wish, wish[group : group + 1], message)
        pack(z, message, group, curve_ref[0], jnp.zeros((1, n), F32), message_ref)


def block_copies(z, ii, inverse_ref, buffer_ref, sems):
    slot = lax.rem(ii, buffer_ref.shape[0])
    for group in range(GROUPS):
        i = jnp.minimum(group * z.rows + ii, z.block - 1)
        yield pltpu.make_async_copy(
            inverse_ref.at[i], buffer_ref.at[slot, group, pl.ds(0, z.block)], sems.at[slot, group]
        )


def chunk_tables(z, ints_ref, floats_ref, near_ref, weights_ref):
    for chunk in range(GROUPS):
        own = chunk * z.width + jnp.bitwise_and(lane_iota(), z.width - 1)
        near_ref[chunk] = lane_take(ints_ref[3], own)
        for at in range(3):
            weights_ref[chunk, at] = lane_take(floats_ref[at], own)


def chunk_copy(ii, chunks_ref, out_ref, sems):
    return pltpu.make_async_copy(chunks_ref.at[:, ii], out_ref.at[:, ii], sems.at[ii])


def arrange_blocks(z, inverse_ref, ints_ref, chunks_ref, out_ref, buffer_ref, sems, out_sems):
    n = z.columns
    perm = ints_ref[1]
    depth = buffer_ref.shape[0]
    orders = [pltpu.roll(perm, group * z.width, 1) if group else perm for group in range(GROUPS)]
    bits = [jnp.bitwise_and(lane_iota() // (z.width << b), 1) == 1 for b in range(3)]

    def row(ii, carry):
        @pl.when(ii + depth - 1 < z.rows)
        def _():
            for copy in block_copies(z, ii + depth - 1, inverse_ref, buffer_ref, sems):
                copy.start()

        for copy in block_copies(z, ii, inverse_ref, buffer_ref, sems):
            copy.wait()
        slot = lax.rem(ii, depth)
        for tile in range(z.block_pad // SUB):
            at = pl.ds(tile * SUB, SUB)
            spread = [lane_take(buffer_ref[slot, group, at, :], orders[group]) for group in range(GROUPS)]
            for b in range(3):
                spread = [
                    jnp.where(bits[b], spread[(x + (1 << b)) % GROUPS], spread[x])
                    for x in range(GROUPS)
                ]
            for chunk in range(GROUPS):
                chunks_ref[chunk, ii, at, :] = spread[-chunk % GROUPS]
        chunk_copy(ii, chunks_ref, out_ref, out_sems).start()
        return carry

    lax.fori_loop(0, z.rows, row, 0)


def first_base(z, traces, start_table_ref, ints_ref, floats_ref, right_ref, jac_ref, stack_ref, right_sorted_ref, base_ref):
    n = z.columns
    near = ints_ref[3]
    slot = ints_ref[4]
    for face in range(FACES):
        piece = start_table_ref[pl.ds((face ^ 1) * z.trace_pad, z.trace_pad), :]
        value = lane_take(piece, near[face : face + 1]) * floats_ref[3][face : face + 1]
        ghost = ghost_take(z, traces, slot, face) * floats_ref[6][face : face + 1]
        stack_ref[pl.ds(face * z.trace_pad, z.trace_pad), :] = value + ghost
    flow = fluxes(jac_ref[...], stack_ref[...])[: z.block_pad]
    right = jnp.concatenate([right_ref[...], jnp.zeros((z.block_pad - z.block, n), F32)], axis=0)
    right = lane_take(right, ints_ref[1][0:1])
    right_sorted_ref[...] = right
    base_ref[...] = right - flow


def send_kinds(z, traces, sends_ref, level_ref, kinds_ref):
    for group in range(3):
        wish = traces[group][z.wish : z.wish + 1] > 0.5
        side = sends_ref[1][group : group + 1]
        dep = sends_ref[2][group : group + 1]
        level = level_ref[...]
        kind = jnp.where(wish, jnp.where(dep <= level, 1, 3), jnp.where(dep >= level, 2, 1))
        kinds_ref[pl.ds(group, 1), :] = jnp.where(side < FACES, kind, 0)


def later_bases(z, traces, ints_ref, floats_ref, base_ref, right_ref, jac_ref, wide_ref, forward_base_ref, swept_base_ref):
    n = z.columns
    slot = ints_ref[4]
    missing_forward = jnp.zeros((1, n), F32)
    missing_swept = jnp.zeros((1, n), F32)
    for face in range(FACES):
        ghost = ghost_take(z, traces, slot, face)
        forward_weight = floats_ref[4][face : face + 1]
        swept_weight = floats_ref[5][face : face + 1]
        lost = jnp.where(ghost[z.flag : z.flag + 1] > 0.5, 0.0, 1.0)
        missing_forward += jnp.where(forward_weight > 0, lost, 0.0)
        missing_swept += jnp.where(swept_weight > 0, lost, 0.0)
        at = pl.ds(face * z.trace_pad, z.trace_pad)
        wide_ref[at, pl.ds(0, n)] = ghost * forward_weight
        wide_ref[at, pl.ds(n, n)] = ghost * swept_weight
    flow = fluxes(jac_ref[...], wide_ref[...])
    forward_base_ref[...] = base_ref[...] - flow[: z.block_pad, :n]
    swept_base_ref[...] = right_ref[...] - flow[: z.block_pad, n:]
    return missing_forward, missing_swept


def steps(
    z,
    span_ref,
    missing_forward,
    missing_swept,
    ints_ref,
    floats_ref,
    near_ref,
    weights_ref,
    jac_ref,
    pick_ref,
    chunks_ref,
    forward_table_ref,
    swept_table_ref,
    forward_ref,
    swept_ref,
    forward_base,
    swept_base,
    stack_ref,
    part_ref,
    fresh_ref,
    fetch=None,
    open_ref=None,
):
    n = z.columns
    near = ints_ref[3]
    dep = ints_ref[2]
    chunk_of = lane_iota(1) // z.width
    per_sum = GROUPS // 2
    part_ref[...] = jnp.where(
        lax.broadcasted_iota(jnp.int32, (z.rows_pad, n), 0) == z.rows, 1.0, 0.0
    )

    def spread(row):
        return jnp.broadcast_to(row, (SUB, n))

    def absent(flags, weights):
        lost = jnp.where(weights > 0, 1.0 - lane_take(flags, near), 0.0)
        return jnp.sum(lost, axis=0, keepdims=True)

    old_forward = spread(forward_table_ref[pl.ds(z.flag, 1), :])
    old_swept = spread(swept_table_ref[pl.ds(z.flag, 1), :])
    forward, swept = old_forward, old_swept
    for level in range(z.levels):
        missing = absent(forward, floats_ref[0]) + missing_forward
        forward = jnp.where((dep == level) & spread(missing < 0.5), 1.0, forward)
    settled = absent(forward, floats_ref[2]) + missing_swept
    for level in range(z.levels - 1, -1, -1):
        missing = absent(swept, floats_ref[1]) + settled
        swept = jnp.where((dep == level) & spread(missing < 0.5), 1.0, swept)
    counts = []
    for at, fresh in enumerate((forward - old_forward, swept - old_swept)):
        fresh = fresh[0:1]
        fresh_ref[pl.ds(at, 1), :] = fresh
        for half in range(2):
            scale = jnp.zeros((1, n), F32)
            for at_chunk in range(per_sum):
                scale = jnp.where(chunk_of == half * per_sum + at_chunk, float((2 * z.width) ** at_chunk), scale)
            counts.append(jnp.sum(fresh * scale).astype(jnp.int32))

    shift = (2 * z.width).bit_length() - 1

    def count_of(chunk, backward):
        low, high = counts[2 * backward], counts[2 * backward + 1]
        bits = jnp.where(chunk >= per_sum, high, low)
        bits = lax.shift_right_logical(bits, lax.rem(chunk, per_sum) * shift)
        return jnp.bitwise_and(bits, 2 * z.width - 1)

    def fetch_for(chunk, backward):
        needed = count_of(chunk, backward) > 0
        if backward:
            needed &= open_ref[chunk] == 0

        @pl.when(needed)
        def _():
            fetch(chunk).start()
            open_ref[chunk] = 1

    if fetch is not None:
        for chunk in range(GROUPS):
            open_ref[chunk] = 0
        for chunk in range(GROUPS):
            fetch_for(jnp.int32(chunk), False)
        for chunk in reversed(range(GROUPS)):
            fetch_for(jnp.int32(chunk), True)

    def step(level, chunk, backward):
        if fetch is not None:

            @pl.when(open_ref[chunk] == 1)
            def _():
                fetch(chunk).wait()
                open_ref[chunk] = 2

        old = forward_table_ref
        new = swept_table_ref
        base = swept_base if backward else forward_base
        rows = near_ref[chunk]
        old_weight = weights_ref[chunk, 2 if backward else 0]
        new_weight = weights_ref[chunk, 1]
        own = chunk * z.width + jnp.bitwise_and(lane_iota(1), z.width - 1)
        for face in range(FACES):
            at = pl.ds((face ^ 1) * z.trace_pad, z.trace_pad)
            row = rows[face : face + 1]
            value = lane_take(old[at, :], row) * old_weight[face : face + 1]
            if backward:
                value += lane_take(new[at, :], row) * new_weight[face : face + 1]
            stack_ref[pl.ds(face * z.trace_pad, z.trace_pad), :] = value
        flow = fluxes(jac_ref[...], stack_ref[...])[: z.block_pad]
        rest = lane_take(base[...], own) - flow
        for ii in range(z.rows):
            part_ref[pl.ds(ii, 1), :] = jnp.sum(chunks_ref[chunk, ii] * rest, axis=0, keepdims=True)
        part = part_ref[...]
        state = jnp.concatenate(
            [pltpu.roll(part, -g * z.width % n, 1) if g else part for g in range(GROUPS)], axis=0
        )
        table = tables_of(state, pick_ref[...])
        fresh = fresh_ref[pl.ds(1 if backward else 0, 1), :] > 0.5
        keep = fresh & (chunk_of == chunk) & (dep[0:1] == level)
        out_state = swept_ref if backward else forward_ref
        out_table = swept_table_ref if backward else forward_table_ref
        out_state[...] = jnp.where(keep, state, out_state[...])
        out_table[...] = jnp.where(keep, table, out_table[...])

    for backward in (False, True):

        def run(count, carry, backward=backward):
            level = z.levels - 1 - count if backward else count

            def one(chunk, inner):
                @pl.when(count_of(chunk, backward) > 0)
                def _():
                    step(level, chunk, backward)

                return inner

            return lax.fori_loop(span_ref[level], span_ref[z.levels + level], one, carry)

        lax.fori_loop(0, z.levels, run, 0)


def send_messages(z, curve, sends_ref, kinds_ref, forward_table_ref, swept_table_ref, message_ref):
    n = z.columns
    row_id = lax.broadcasted_iota(jnp.int32, (z.trace_pad, n), 0)
    messages = []
    still = jnp.zeros((1, n), F32)
    for group in range(3):
        where = sends_ref[0][group : group + 1]
        side = sends_ref[1][group : group + 1]
        kind = kinds_ref[pl.ds(group, 1), :]
        message = jnp.zeros((z.trace_pad, n), F32)
        for face in range(FACES):
            at = pl.ds(face * z.trace_pad, z.trace_pad)
            first = lane_take(forward_table_ref[at, :], where)
            second = lane_take(swept_table_ref[at, :], where)
            picked = jnp.where(kind == 1, first, second)
            message = jnp.where(side == face, picked, message)
        message = jnp.where((kind == 3) & (row_id == z.flag), 2.0, message)
        unsent = (kind > 0) & (message[z.flag : z.flag + 1] < 0.5)
        still = jnp.maximum(still, jnp.where(unsent, 1.0, 0.0))
        messages.append(message)
    still = jnp.broadcast_to(jnp.max(still, axis=1, keepdims=True), (1, n))
    message_ref[...] = jnp.broadcast_to(still[None], message_ref.shape)
    for group in range(3):
        pack(z, messages[group], group, curve, still, message_ref)


def first_kernel(
    z,
    curve_ref,
    span_ref,
    right_ref,
    level_ref,
    start_table_ref,
    arrived_ref,
    ints_ref,
    floats_ref,
    sends_ref,
    jac_ref,
    pick_ref,
    inverse_ref,
    message_ref,
    base_ref,
    right_sorted_ref,
    start_slots_ref,
    kinds_ref,
    chunks_out,
    near_ref,
    weights_ref,
    forward_table_ref,
    swept_table_ref,
    forward_ref,
    swept_ref,
    stack_ref,
    part_ref,
    fresh_ref,
    buffer_ref,
    chunks_ref,
    sems,
    out_sems,
):
    n = z.columns
    curve = curve_ref[0]
    depth = buffer_ref.shape[0]
    buffer_ref[:, :, z.block :, :] = jnp.zeros((depth, GROUPS, z.block_pad - z.block, n), F32)
    for first in range(depth - 1):
        for copy in block_copies(z, first, inverse_ref, buffer_ref, sems):
            copy.start()
    chunk_tables(z, ints_ref, floats_ref, near_ref, weights_ref)
    traces = [unpack(z, group, curve, arrived_ref) for group in range(3)]
    for group in range(3):
        start_slots_ref[group] = traces[group]
    send_kinds(z, traces, sends_ref, level_ref, kinds_ref)
    first_base(
        z, traces, start_table_ref, ints_ref, floats_ref, right_ref, jac_ref, stack_ref, right_sorted_ref, base_ref
    )
    forward_table_ref[...] = jnp.zeros_like(forward_table_ref)
    swept_table_ref[...] = jnp.zeros_like(swept_table_ref)
    forward_ref[...] = jnp.zeros_like(forward_ref)
    swept_ref[...] = jnp.zeros_like(swept_ref)
    arrange_blocks(z, inverse_ref, ints_ref, chunks_ref, chunks_out, buffer_ref, sems, out_sems)
    missing_forward = jnp.sum(jnp.where(floats_ref[4] > 0, 1.0, 0.0), axis=0, keepdims=True)
    missing_swept = jnp.sum(jnp.where(floats_ref[5] > 0, 1.0, 0.0), axis=0, keepdims=True)
    steps(
        z,
        span_ref,
        missing_forward,
        missing_swept,
        ints_ref,
        floats_ref,
        near_ref,
        weights_ref,
        jac_ref,
        pick_ref,
        chunks_ref,
        forward_table_ref,
        swept_table_ref,
        forward_ref,
        swept_ref,
        base_ref,
        right_sorted_ref,
        stack_ref,
        part_ref,
        fresh_ref,
    )
    send_messages(z, curve, sends_ref, kinds_ref, forward_table_ref, swept_table_ref, message_ref)
    for ii in range(z.rows):
        chunk_copy(ii, chunks_ref, chunks_out, out_sems).wait()


def round_kernel(
    z,
    curve_ref,
    span_ref,
    arrived_ref,
    ints_ref,
    floats_ref,
    sends_ref,
    near_ref,
    weights_ref,
    jac_ref,
    pick_ref,
    chunks_in,
    base_ref,
    right_ref,
    start_slots_ref,
    kinds_ref,
    forward_table_in,
    swept_table_in,
    forward_in,
    swept_in,
    message_ref,
    more_ref,
    forward_table_ref,
    swept_table_ref,
    forward_ref,
    swept_ref,
    stack_ref,
    part_ref,
    fresh_ref,
    wide_ref,
    forward_base_ref,
    swept_base_ref,
    chunks_ref,
    sems,
    open_ref,
):
    n = z.columns
    curve = curve_ref[0]

    def fetch(chunk):
        return pltpu.make_async_copy(chunks_in.at[chunk], chunks_ref.at[chunk], sems.at[chunk])

    forward_table_ref[...] = forward_table_in[...]
    swept_table_ref[...] = swept_table_in[...]
    forward_ref[...] = forward_in[...]
    swept_ref[...] = swept_in[...]
    row_id = lax.broadcasted_iota(jnp.int32, (z.trace_pad, n), 0)
    still = jnp.max(arrived_ref[:, 0:1, :], axis=0)
    still = jnp.where(lane_iota(1) == n - 1, still, 0.0)
    more_ref[0] = jnp.max(still).astype(jnp.int32)
    traces = []
    for group in range(3):
        arrived = unpack(z, group, curve, arrived_ref)
        flag = arrived[z.flag : z.flag + 1]
        traces.append(jnp.where((flag > 1.5) & (row_id != z.flag), start_slots_ref[group], arrived))
    missing_forward, missing_swept = later_bases(
        z, traces, ints_ref, floats_ref, base_ref, right_ref, jac_ref, wide_ref, forward_base_ref, swept_base_ref
    )
    steps(
        z,
        span_ref,
        missing_forward,
        missing_swept,
        ints_ref,
        floats_ref,
        near_ref,
        weights_ref,
        jac_ref,
        pick_ref,
        chunks_ref,
        forward_table_ref,
        swept_table_ref,
        forward_ref,
        swept_ref,
        forward_base_ref,
        swept_base_ref,
        stack_ref,
        part_ref,
        fresh_ref,
        fetch,
        open_ref,
    )
    send_messages(z, curve, sends_ref, kinds_ref, forward_table_ref, swept_table_ref, message_ref)


def output_kernel(z, ints_ref, forward_ref, swept_ref, forward_out, swept_out):
    pos = ints_ref[0][0:1]
    for source, target in ((forward_ref, forward_out), (swept_ref, swept_out)):
        for group in range(GROUPS):
            count = min(z.rows, z.block - group * z.rows)
            block = lane_take(source[pl.ds(group * z.rows_pad, z.rows_pad), :], pos)
            target[pl.ds(group * z.rows, count), :] = block[:count]


def call(kernel, outs, inputs, scratch=(), aliases=None, smem_in=(), smem_out=(), hbm_in=(), hbm_out=(), vmem=24):
    whole, smem = pl.BlockSpec(memory_space=pltpu.VMEM), pl.BlockSpec(memory_space=pltpu.SMEM)
    hbm = pl.BlockSpec(memory_space=pltpu.HBM)
    return pl.pallas_call(
        kernel,
        out_shape=outs,
        in_specs=[smem if at in smem_in else hbm if at in hbm_in else whole for at in range(inputs)],
        out_specs=[smem if at in smem_out else hbm if at in hbm_out else whole for at in range(len(outs))],
        scratch_shapes=list(scratch),
        input_output_aliases=aliases or {},
        compiler_params=pltpu.CompilerParams(vmem_limit_bytes=vmem << 20),
    )


def shape(*dims, kind=F32):
    return jax.ShapeDtypeStruct(dims, kind)


def kept(*dims, kind=F32):
    return pltpu.VMEM(dims, kind)


def body(
    start_state,
    right_side,
    block_inverse,
    lifted_flux_jacobian,
    face_weight,
    dep_level,
    face_link,
    send_list,
    recv_list,
):
    curves, slabs = lax.axis_size("curve"), lax.axis_size("slab")
    levels = send_list.shape[0]
    cap = send_list.shape[1] // (curves * slabs)
    slots = levels * cap
    block, n = start_state.shape
    z = Sizes(block, n, levels, slots, curves, slabs)
    own = lax.axis_index("curve").astype(jnp.int32)
    curve = own.reshape(1)

    stride = slabs * cap
    lists = jnp.concatenate([send_list, recv_list], axis=0)
    lists = jnp.pad(lists, ((0, 0), (stride, n)), constant_values=FACES * n)
    lists = lax.dynamic_slice_in_dim(lists, own * stride, n, axis=1)
    slot_level = jnp.asarray(
        np.tile(np.repeat(np.arange(levels), cap), slabs).reshape(1, n), jnp.int32
    )
    pick = jnp.asarray(selector(z), BF16)
    jac = jnp.pad(
        lifted_flux_jacobian, ((0, 0), (0, z.jac_rows - block), (0, z.trace_pad - z.trace))
    )
    jac = jac.transpose(1, 0, 2).reshape(z.jac_rows, z.table_rows)
    rounded = lax.reduce_precision(jac, 8, 7)
    high, low = rounded.astype(BF16), (jac - rounded).astype(BF16)
    jac = jnp.concatenate([high, high, low], axis=1)

    ints, floats, sends, span, start_table, message = call(
        functools.partial(prepare_kernel, z),
        [
            kept(5, SUB, n, kind=jnp.int32),
            kept(7, SUB, n),
            kept(3, SUB, n, kind=jnp.int32),
            shape(2 * levels + 1, kind=jnp.int32),
            kept(z.table_rows, n),
            shape(z.devices, 16, n),
        ],
        8,
        scratch=[pltpu.VMEM((z.state_rows, n), F32)],
        smem_in=(0,),
        smem_out=(3,),
        vmem=60,
    )(curve, start_state, dep_level.reshape(1, n), face_link, face_weight, lists, slot_level, pick)
    message, jac = lax.optimization_barrier((message, jac))

    def exchange(message):
        return lax.all_to_all(message, ("curve", "slab"), 0, 0, tiled=True)

    arrived = exchange(message)
    tables = [
        kept(z.table_rows, n),
        kept(z.table_rows, n),
        kept(z.state_rows, n),
        kept(z.state_rows, n),
    ]
    scratch = [
        pltpu.VMEM((z.table_rows, n), F32),
        pltpu.VMEM((z.rows_pad, n), F32),
        pltpu.VMEM((SUB, n), F32),
    ]
    depth = 6
    message, base, right, start_slots, kinds, chunks, near, weights, *state = call(
        functools.partial(first_kernel, z),
        [
            shape(z.devices, 16, n),
            kept(z.block_pad, n),
            kept(z.block_pad, n),
            kept(3, z.trace_pad, n),
            kept(3, n, kind=jnp.int32),
            shape(GROUPS, z.rows, z.block_pad, n),
            kept(GROUPS, SUB, n, kind=jnp.int32),
            kept(GROUPS, 3, SUB, n),
        ]
        + tables,
        12,
        scratch=scratch
        + [
            pltpu.VMEM((depth, GROUPS, z.block_pad, n), F32),
            pltpu.VMEM((GROUPS, z.rows, z.block_pad, n), F32),
            pltpu.SemaphoreType.DMA((depth, GROUPS)),
            pltpu.SemaphoreType.DMA((z.rows,)),
        ],
        smem_in=(0, 1),
        hbm_in=(11,),
        hbm_out=(5,),
        vmem=48,
    )(
        curve,
        span,
        right_side,
        slot_level,
        start_table,
        arrived,
        ints,
        floats,
        sends,
        jac,
        pick,
        block_inverse,
    )

    round_call = call(
        functools.partial(round_kernel, z),
        [shape(z.devices, 16, n), shape(1, kind=jnp.int32)] + tables,
        19,
        scratch=scratch
        + [
            pltpu.VMEM((z.table_rows, 2 * n), F32),
            pltpu.VMEM((z.block_pad, n), F32),
            pltpu.VMEM((z.block_pad, n), F32),
            pltpu.VMEM((GROUPS, z.rows, z.block_pad, n), F32),
            pltpu.SemaphoreType.DMA((GROUPS,)),
            pltpu.SMEM((GROUPS,), jnp.int32),
        ],
        hbm_in=(10,),
        vmem=16,
        aliases={15: 2, 16: 3, 17: 4, 18: 5},
        smem_in=(0, 1),
        smem_out=(1,),
    )

    def one_round(carry):
        _, message, state = carry
        message, more, *state = round_call(
            curve,
            span,
            exchange(message),
            ints,
            floats,
            sends,
            near,
            weights,
            jac,
            pick,
            chunks,
            base,
            right,
            start_slots,
            kinds,
            *state,
        )
        return more[0], message, tuple(state)

    start = (jnp.array(1, jnp.int32), message, tuple(state))
    _, _, state = lax.while_loop(lambda carry: carry[0] > 0, one_round, start)
    return tuple(
        call(functools.partial(output_kernel, z), [shape(block, n), shape(block, n)], 3)(
            ints, state[2], state[3]
        )
    )


def solution(mesh):
    split = ("curve", "slab")
    return jax.shard_map(
        body,
        mesh=mesh,
        in_specs=(
            P(None, split),
            P(None, split),
            P(None, None, split),
            P(),
            P(None, split),
            P(split),
            P(None, split),
            P(None, split),
            P(None, split),
        ),
        out_specs=(P(None, split), P(None, split)),
        check_vma=False,
    )
```

```python
import functools

import jax
import jax.numpy as jnp
import numpy as np
from jax import lax
from jax.experimental import pallas as pl
from jax.experimental.pallas import tpu as pltpu
from jax.sharding import PartitionSpec as P

VARS = 5
SIDE = 3
FACES = 6
LANES = 128
SUB = 8
GROUPS = 8
F32 = jnp.float32
BF16 = jnp.bfloat16


class Sizes:
    def __init__(self, block, columns, levels, slots, curves, slabs):
        self.block = block
        self.columns = columns
        self.levels = levels
        self.slots = slots
        self.curves = curves
        self.slabs = slabs
        self.devices = curves * slabs
        self.trace = VARS * SIDE * SIDE
        self.width = columns // GROUPS
        self.rows = -(-block // GROUPS)
        self.rows_pad = -(-(self.rows + 1) // SUB) * SUB
        self.state_rows = GROUPS * self.rows_pad
        self.block_pad = -(-block // SUB) * SUB
        self.flag = self.trace
        self.wish = self.trace + 1
        self.trace_pad = -(-(self.trace + 2) // 16) * 16
        self.cuts = self.trace_pad // 16
        self.table_rows = FACES * self.trace_pad
        self.jac_rows = -(-self.block_pad // 16) * 16
        assert columns == LANES and slabs * slots == LANES
        assert (self.cuts + 1) * slots <= LANES and block < self.block_pad


def face_rows():
    nodes = np.arange(VARS * SIDE**3).reshape(VARS, SIDE, SIDE, SIDE)
    last = SIDE - 1
    sides = [
        nodes[:, 0],
        nodes[:, last],
        nodes[:, :, 0],
        nodes[:, :, last],
        nodes[:, :, :, 0],
        nodes[:, :, :, last],
    ]
    return [side.reshape(-1) for side in sides]


def selector(z):
    pick = np.zeros((z.table_rows, z.state_rows), np.float32)
    for face, rows in enumerate(face_rows()):
        for h, i in enumerate(rows):
            pick[face * z.trace_pad + h, i // z.rows * z.rows_pad + i % z.rows] = 1
        pick[face * z.trace_pad + z.flag, z.rows] = 1
    return np.concatenate([pick, pick], axis=1)


def lane_take(values, index):
    index = jnp.broadcast_to(index, values.shape)
    return jnp.take_along_axis(values, index, axis=1, mode="promise_in_bounds")


def lane_iota(rows=SUB):
    return lax.broadcasted_iota(jnp.int32, (rows, LANES), 1)


def halves(values):
    high = values.astype(BF16)
    low = (values - high.astype(F32)).astype(BF16)
    return high, low


def as_column(row):
    return jnp.broadcast_to(row, (LANES, LANES)).T


def dot(a, b):
    return jnp.dot(a, b, preferred_element_type=F32)


def tables_of(state, pick):
    high, low = halves(state)
    return dot(pick, jnp.concatenate([high, low], axis=0))


def fluxes(jac, traces):
    high, low = halves(traces)
    return dot(jac, jnp.concatenate([high, low, high], axis=0))


def pack(z, message, group, curve, open_sends, out_ref):
    lanes = lane_iota(16)
    target = curve + group - 1

    @pl.when((target >= 0) & (target < z.curves))
    def _():
        for slab in range(z.slabs):
            block = jnp.broadcast_to(open_sends, (16, LANES))
            for cut in range(z.cuts):
                part = message[cut * 16 : cut * 16 + 16]
                shift = (cut - slab) * z.slots % LANES
                part = pltpu.roll(part, shift, 1) if shift else part
                block = jnp.where(lanes // z.slots == cut, part, block)
            out_ref[target * z.slabs + slab] = block


def unpack(z, group, curve, in_ref):
    lanes = lane_iota(16)
    source = jnp.clip(curve + group - 1, 0, z.curves - 1)
    blocks = [in_ref[source * z.slabs + slab] for slab in range(z.slabs)]
    parts = []
    for cut in range(z.cuts):
        part = jnp.zeros((16, LANES), F32)
        for slab in range(z.slabs):
            shift = (slab - cut) * z.slots % LANES
            block = pltpu.roll(blocks[slab], shift, 1) if shift else blocks[slab]
            part = jnp.where(lanes // z.slots == slab, block, part)
        parts.append(part)
    return jnp.concatenate(parts, axis=0)


def ghost_take(z, slot_traces, where, face):
    index = jnp.maximum(where[face : face + 1], 0)
    lane = jnp.bitwise_and(index, LANES - 1)
    block = index // LANES
    found = jnp.zeros((z.trace_pad, LANES), F32)
    for group in range(3):
        found = jnp.where(block == group, lane_take(slot_traces[group], lane), found)
    return found


def regroup(z, lists_ref, level_ref):
    n = z.columns
    cap = z.slots // z.levels
    lane = lane_iota(1)
    source = lane // z.slots * cap + jnp.bitwise_and(lane, cap - 1)
    row_id = lax.broadcasted_iota(jnp.int32, (z.levels, n), 0)
    own_row = row_id == level_ref[...]
    both = []
    for at in range(2):
        lists = lists_ref[pl.ds(at * z.levels, z.levels), :]
        rows = []
        for group in range(3):
            taken = lane_take(lists, source + group * z.slabs * cap)
            rows.append(jnp.sum(jnp.where(own_row, taken, 0).astype(F32), axis=0, keepdims=True))
        rows.append(jnp.full((SUB - 3, n), float(FACES * n), F32))
        both.append(jnp.concatenate(rows, axis=0).astype(jnp.int32))
    return both


def prepare_kernel(
    z,
    curve_ref,
    start_ref,
    dep_ref,
    link_ref,
    weight_ref,
    lists_ref,
    level_ref,
    pick_ref,
    ints_ref,
    floats_ref,
    sends_ref,
    span_ref,
    table_ref,
    message_ref,
    state_ref,
):
    n = z.columns
    lanes = lane_iota()
    dep_row = dep_ref[...]
    dep = jnp.broadcast_to(dep_row, (SUB, n))
    key = (dep_row * n + lane_iota(1)).astype(F32)
    earlier = as_column(key) < jnp.broadcast_to(key, (n, n))
    pos_row = jnp.sum(jnp.where(earlier, 1.0, 0.0), axis=0, keepdims=True)
    here = as_column(pos_row) == lane_iota(n).astype(F32)
    element = lax.broadcasted_iota(jnp.int32, (n, n), 0).astype(F32)
    perm_row = jnp.sum(jnp.where(here, element, 0.0), axis=0, keepdims=True)
    pos = jnp.broadcast_to(pos_row.astype(jnp.int32), (SUB, n))
    perm = jnp.broadcast_to(perm_row.astype(jnp.int32), (SUB, n))
    dep_sorted = lane_take(dep, perm)
    for level in range(z.levels):
        before = jnp.sum(jnp.where(dep_row < level, 1.0, 0.0)).astype(jnp.int32)
        upto = jnp.sum(jnp.where(dep_row <= level, 1.0, 0.0)).astype(jnp.int32)
        span_ref[level] = before // z.width
        span_ref[z.levels + level] = jnp.where(upto > before, (upto + z.width - 1) // z.width, before // z.width)

    link = jnp.concatenate([link_ref[...], jnp.full((SUB - FACES, n), -1, jnp.int32)], axis=0)
    near = jnp.where(link >= 0, lane_take(pos, jnp.maximum(link, 0)), -1)
    near = lane_take(near, perm)
    weight = jnp.concatenate([weight_ref[...], jnp.zeros((SUB - FACES, n), F32)], axis=0)
    weight = lane_take(weight, perm)
    local = near >= 0
    near = jnp.maximum(near, 0)
    dep_near = lane_take(dep_sorted, near)
    zero = jnp.zeros_like(weight)

    send, recv = regroup(z, lists_ref, level_ref)
    slot_level = jnp.broadcast_to(level_ref[...], (SUB, n))
    rows = []
    slot_id = lax.broadcasted_iota(jnp.int32, (n, n), 0).astype(F32) + 1.0
    columns = [as_column(recv[group : group + 1].astype(F32)) for group in range(3)]
    for face in range(FACES):
        name = (lane_iota(n) + face * n).astype(F32)
        found = jnp.zeros((1, n), F32)
        for group in range(3):
            hit = jnp.where(columns[group] == name, slot_id + float(group * n), 0.0)
            found = jnp.maximum(found, jnp.max(hit, axis=0, keepdims=True))
        rows.append(found)
    rows.append(jnp.zeros((SUB - FACES, n), F32))
    slot = jnp.concatenate(rows, axis=0).astype(jnp.int32) - 1
    slot = lane_take(slot, perm)
    from_far = slot >= 0
    slot = jnp.maximum(slot, 0)
    far_level = lane_take(slot_level, jnp.bitwise_and(slot, n - 1))

    for at, value in enumerate((pos, perm, dep_sorted, near, slot)):
        ints_ref[at] = value
    floats_ref[0] = jnp.where(local & (dep_near < dep_sorted), weight, zero)
    floats_ref[1] = jnp.where(local & (dep_near > dep_sorted), weight, zero)
    floats_ref[2] = jnp.where(local & (dep_near <= dep_sorted), weight, zero)
    floats_ref[3] = jnp.where(local & (dep_near >= dep_sorted), weight, zero)
    floats_ref[4] = jnp.where(from_far & (far_level < dep_sorted), weight, zero)
    floats_ref[5] = jnp.where(from_far, weight, zero)
    floats_ref[6] = jnp.where(from_far & (far_level >= dep_sorted), weight, zero)

    send_element = jnp.bitwise_and(send, n - 1)
    sends_ref[0] = lane_take(pos, send_element)
    sends_ref[1] = send // n
    sends_ref[2] = lane_take(dep, send_element)
    recv_dep = lane_take(dep, jnp.bitwise_and(recv, n - 1))
    wish = jnp.where(slot_level <= recv_dep, 1.0, 0.0)

    state_ref[...] = jnp.zeros_like(state_ref)
    for group in range(GROUPS):
        count = min(z.rows, z.block - group * z.rows)
        state_ref[pl.ds(group * z.rows_pad, count), :] = start_ref[pl.ds(group * z.rows, count), :]
    state_ref[pl.ds(z.rows, 1), :] = jnp.ones((1, n), F32)
    state = lane_take(state_ref[...], perm[0:1])
    table = tables_of(state, pick_ref[...])
    table_ref[...] = table
    message_ref[...] = jnp.zeros_like(message_ref)
    row_id = lax.broadcasted_iota(jnp.int32, (z.trace_pad, n), 0)
    for group in range(3):
        where = sends_ref[0][group : group + 1]
        side = sends_ref[1][group : group + 1]
        message = jnp.zeros((z.trace_pad, n), F32)
        for face in range(FACES):
            piece = table[face * z.trace_pad : (face + 1) * z.trace_pad]
            message = jnp.where(side == face, lane_take(piece, where), message)
        message = jnp.where(row_id == z.wish, wish[group : group + 1], message)
        pack(z, message, group, curve_ref[0], jnp.zeros((1, n), F32), message_ref)


def block_copies(z, ii, inverse_ref, buffer_ref, sems):
    slot = lax.rem(ii, buffer_ref.shape[0])
    for group in range(GROUPS):
        i = jnp.minimum(group * z.rows + ii, z.block - 1)
        yield pltpu.make_async_copy(
            inverse_ref.at[i], buffer_ref.at[slot, group, pl.ds(0, z.block)], sems.at[slot, group]
        )


def chunk_tables(z, ints_ref, floats_ref, near_ref, weights_ref):
    for chunk in range(GROUPS):
        own = chunk * z.width + jnp.bitwise_and(lane_iota(), z.width - 1)
        near_ref[chunk] = lane_take(ints_ref[3], own)
        for at in range(3):
            weights_ref[chunk, at] = lane_take(floats_ref[at], own)


def chunk_copy(ii, chunks_ref, out_ref, sems):
    return pltpu.make_async_copy(chunks_ref.at[:, ii], out_ref.at[:, ii], sems.at[ii])


def arrange_blocks(z, inverse_ref, ints_ref, chunks_ref, out_ref, buffer_ref, sems, out_sems):
    n = z.columns
    perm = ints_ref[1]
    depth = buffer_ref.shape[0]
    orders = [pltpu.roll(perm, group * z.width, 1) if group else perm for group in range(GROUPS)]
    bits = [jnp.bitwise_and(lane_iota() // (z.width << b), 1) == 1 for b in range(3)]

    def row(ii, carry):
        @pl.when(ii + depth - 1 < z.rows)
        def _():
            for copy in block_copies(z, ii + depth - 1, inverse_ref, buffer_ref, sems):
                copy.start()

        for copy in block_copies(z, ii, inverse_ref, buffer_ref, sems):
            copy.wait()
        slot = lax.rem(ii, depth)
        for tile in range(z.block_pad // SUB):
            at = pl.ds(tile * SUB, SUB)
            spread = [lane_take(buffer_ref[slot, group, at, :], orders[group]) for group in range(GROUPS)]
            for b in range(3):
                spread = [
                    jnp.where(bits[b], spread[(x + (1 << b)) % GROUPS], spread[x])
                    for x in range(GROUPS)
                ]
            for chunk in range(GROUPS):
                chunks_ref[chunk, ii, at, :] = spread[-chunk % GROUPS]
        chunk_copy(ii, chunks_ref, out_ref, out_sems).start()
        return carry

    lax.fori_loop(0, z.rows, row, 0)


def blocks_kernel(
    z, inverse_ref, ints_ref, floats_ref, chunks_out, near_ref, weights_ref, buffer_ref, chunks_ref, sems, out_sems
):
    depth = buffer_ref.shape[0]
    buffer_ref[:, :, z.block :, :] = jnp.zeros((depth, GROUPS, z.block_pad - z.block, z.columns), F32)
    for first in range(depth - 1):
        for copy in block_copies(z, first, inverse_ref, buffer_ref, sems):
            copy.start()
    chunk_tables(z, ints_ref, floats_ref, near_ref, weights_ref)
    arrange_blocks(z, inverse_ref, ints_ref, chunks_ref, chunks_out, buffer_ref, sems, out_sems)
    for ii in range(z.rows):
        chunk_copy(ii, chunks_ref, chunks_out, out_sems).wait()


def first_base(z, traces, start_table_ref, ints_ref, floats_ref, right_ref, jac_ref, stack_ref, right_sorted_ref, base_ref):
    n = z.columns
    near = ints_ref[3]
    slot = ints_ref[4]
    for face in range(FACES):
        piece = start_table_ref[pl.ds((face ^ 1) * z.trace_pad, z.trace_pad), :]
        value = lane_take(piece, near[face : face + 1]) * floats_ref[3][face : face + 1]
        ghost = ghost_take(z, traces, slot, face) * floats_ref[6][face : face + 1]
        stack_ref[pl.ds(face * z.trace_pad, z.trace_pad), :] = value + ghost
    flow = fluxes(jac_ref[...], stack_ref[...])[: z.block_pad]
    right = jnp.concatenate([right_ref[...], jnp.zeros((z.block_pad - z.block, n), F32)], axis=0)
    right = lane_take(right, ints_ref[1][0:1])
    right_sorted_ref[...] = right
    base_ref[...] = right - flow


def send_kinds(z, traces, sends_ref, level_ref, kinds_ref):
    for group in range(3):
        wish = traces[group][z.wish : z.wish + 1] > 0.5
        side = sends_ref[1][group : group + 1]
        dep = sends_ref[2][group : group + 1]
        level = level_ref[...]
        kind = jnp.where(wish, jnp.where(dep <= level, 1, 3), jnp.where(dep >= level, 2, 1))
        kinds_ref[pl.ds(group, 1), :] = jnp.where(side < FACES, kind, 0)


def later_bases(z, traces, ints_ref, floats_ref, base_ref, right_ref, jac_ref, wide_ref, forward_base_ref, swept_base_ref):
    n = z.columns
    slot = ints_ref[4]
    missing_forward = jnp.zeros((1, n), F32)
    missing_swept = jnp.zeros((1, n), F32)
    for face in range(FACES):
        ghost = ghost_take(z, traces, slot, face)
        forward_weight = floats_ref[4][face : face + 1]
        swept_weight = floats_ref[5][face : face + 1]
        lost = jnp.where(ghost[z.flag : z.flag + 1] > 0.5, 0.0, 1.0)
        missing_forward += jnp.where(forward_weight > 0, lost, 0.0)
        missing_swept += jnp.where(swept_weight > 0, lost, 0.0)
        at = pl.ds(face * z.trace_pad, z.trace_pad)
        wide_ref[at, pl.ds(0, n)] = ghost * forward_weight
        wide_ref[at, pl.ds(n, n)] = ghost * swept_weight
    flow = fluxes(jac_ref[...], wide_ref[...])
    forward_base_ref[...] = base_ref[...] - flow[: z.block_pad, :n]
    swept_base_ref[...] = right_ref[...] - flow[: z.block_pad, n:]
    return missing_forward, missing_swept


def steps(
    z,
    span_ref,
    missing_forward,
    missing_swept,
    ints_ref,
    floats_ref,
    near_ref,
    weights_ref,
    jac_ref,
    pick_ref,
    chunks_ref,
    forward_table_ref,
    swept_table_ref,
    forward_ref,
    swept_ref,
    forward_base,
    swept_base,
    stack_ref,
    part_ref,
    fresh_ref,
    fetch=None,
    open_ref=None,
):
    n = z.columns
    near = ints_ref[3]
    dep = ints_ref[2]
    chunk_of = lane_iota(1) // z.width
    per_sum = GROUPS // 2
    part_ref[...] = jnp.where(
        lax.broadcasted_iota(jnp.int32, (z.rows_pad, n), 0) == z.rows, 1.0, 0.0
    )

    def spread(row):
        return jnp.broadcast_to(row, (SUB, n))

    def absent(flags, weights):
        lost = jnp.where(weights > 0, 1.0 - lane_take(flags, near), 0.0)
        return jnp.sum(lost, axis=0, keepdims=True)

    old_forward = spread(forward_table_ref[pl.ds(z.flag, 1), :])
    old_swept = spread(swept_table_ref[pl.ds(z.flag, 1), :])
    forward, swept = old_forward, old_swept
    for level in range(z.levels):
        missing = absent(forward, floats_ref[0]) + missing_forward
        forward = jnp.where((dep == level) & spread(missing < 0.5), 1.0, forward)
    settled = absent(forward, floats_ref[2]) + missing_swept
    for level in range(z.levels - 1, -1, -1):
        missing = absent(swept, floats_ref[1]) + settled
        swept = jnp.where((dep == level) & spread(missing < 0.5), 1.0, swept)
    counts = []
    for at, fresh in enumerate((forward - old_forward, swept - old_swept)):
        fresh = fresh[0:1]
        fresh_ref[pl.ds(at, 1), :] = fresh
        for half in range(2):
            scale = jnp.zeros((1, n), F32)
            for at_chunk in range(per_sum):
                scale = jnp.where(chunk_of == half * per_sum + at_chunk, float((2 * z.width) ** at_chunk), scale)
            counts.append(jnp.sum(fresh * scale).astype(jnp.int32))

    shift = (2 * z.width).bit_length() - 1

    def count_of(chunk, backward):
        low, high = counts[2 * backward], counts[2 * backward + 1]
        bits = jnp.where(chunk >= per_sum, high, low)
        bits = lax.shift_right_logical(bits, lax.rem(chunk, per_sum) * shift)
        return jnp.bitwise_and(bits, 2 * z.width - 1)

    def fetch_for(chunk, backward):
        needed = count_of(chunk, backward) > 0
        if backward:
            needed &= open_ref[chunk] == 0

        @pl.when(needed)
        def _():
            fetch(chunk).start()
            open_ref[chunk] = 1

    if fetch is not None:
        for chunk in range(GROUPS):
            open_ref[chunk] = 0
        for chunk in range(GROUPS):
            fetch_for(jnp.int32(chunk), False)
        for chunk in reversed(range(GROUPS)):
            fetch_for(jnp.int32(chunk), True)

    def step(level, chunk, backward):
        if fetch is not None:

            @pl.when(open_ref[chunk] == 1)
            def _():
                fetch(chunk).wait()
                open_ref[chunk] = 2

        old = forward_table_ref
        new = swept_table_ref
        base = swept_base if backward else forward_base
        rows = near_ref[chunk]
        old_weight = weights_ref[chunk, 2 if backward else 0]
        new_weight = weights_ref[chunk, 1]
        own = chunk * z.width + jnp.bitwise_and(lane_iota(1), z.width - 1)
        for face in range(FACES):
            at = pl.ds((face ^ 1) * z.trace_pad, z.trace_pad)
            row = rows[face : face + 1]
            value = lane_take(old[at, :], row) * old_weight[face : face + 1]
            if backward:
                value += lane_take(new[at, :], row) * new_weight[face : face + 1]
            stack_ref[pl.ds(face * z.trace_pad, z.trace_pad), :] = value
        flow = fluxes(jac_ref[...], stack_ref[...])[: z.block_pad]
        rest = lane_take(base[...], own) - flow
        for ii in range(z.rows):
            part_ref[pl.ds(ii, 1), :] = jnp.sum(chunks_ref[chunk, ii] * rest, axis=0, keepdims=True)
        part = part_ref[...]
        state = jnp.concatenate(
            [pltpu.roll(part, -g * z.width % n, 1) if g else part for g in range(GROUPS)], axis=0
        )
        table = tables_of(state, pick_ref[...])
        fresh = fresh_ref[pl.ds(1 if backward else 0, 1), :] > 0.5
        keep = fresh & (chunk_of == chunk) & (dep[0:1] == level)
        out_state = swept_ref if backward else forward_ref
        out_table = swept_table_ref if backward else forward_table_ref
        out_state[...] = jnp.where(keep, state, out_state[...])
        out_table[...] = jnp.where(keep, table, out_table[...])

    for backward in (False, True):

        def run(count, carry, backward=backward):
            level = z.levels - 1 - count if backward else count

            def one(chunk, inner):
                @pl.when(count_of(chunk, backward) > 0)
                def _():
                    step(level, chunk, backward)

                return inner

            return lax.fori_loop(span_ref[level], span_ref[z.levels + level], one, carry)

        lax.fori_loop(0, z.levels, run, 0)


def send_messages(z, curve, sends_ref, kinds_ref, forward_table_ref, swept_table_ref, message_ref):
    n = z.columns
    row_id = lax.broadcasted_iota(jnp.int32, (z.trace_pad, n), 0)
    messages = []
    still = jnp.zeros((1, n), F32)
    for group in range(3):
        where = sends_ref[0][group : group + 1]
        side = sends_ref[1][group : group + 1]
        kind = kinds_ref[pl.ds(group, 1), :]
        message = jnp.zeros((z.trace_pad, n), F32)
        for face in range(FACES):
            at = pl.ds(face * z.trace_pad, z.trace_pad)
            first = lane_take(forward_table_ref[at, :], where)
            second = lane_take(swept_table_ref[at, :], where)
            picked = jnp.where(kind == 1, first, second)
            message = jnp.where(side == face, picked, message)
        message = jnp.where((kind == 3) & (row_id == z.flag), 2.0, message)
        unsent = (kind > 0) & (message[z.flag : z.flag + 1] < 0.5)
        still = jnp.maximum(still, jnp.where(unsent, 1.0, 0.0))
        messages.append(message)
    still = jnp.broadcast_to(jnp.max(still, axis=1, keepdims=True), (1, n))
    message_ref[...] = jnp.broadcast_to(still[None], message_ref.shape)
    for group in range(3):
        pack(z, messages[group], group, curve, still, message_ref)


def first_kernel(
    z,
    curve_ref,
    span_ref,
    right_ref,
    level_ref,
    start_table_ref,
    arrived_ref,
    ints_ref,
    floats_ref,
    sends_ref,
    near_ref,
    weights_ref,
    jac_ref,
    pick_ref,
    chunks_in,
    message_ref,
    base_ref,
    right_sorted_ref,
    start_slots_ref,
    kinds_ref,
    forward_table_ref,
    swept_table_ref,
    forward_ref,
    swept_ref,
    stack_ref,
    part_ref,
    fresh_ref,
    chunks_ref,
    sems,
    open_ref,
):
    n = z.columns
    curve = curve_ref[0]

    def fetch(chunk):
        return pltpu.make_async_copy(chunks_in.at[chunk], chunks_ref.at[chunk], sems.at[chunk])

    traces = [unpack(z, group, curve, arrived_ref) for group in range(3)]
    for group in range(3):
        start_slots_ref[group] = traces[group]
    send_kinds(z, traces, sends_ref, level_ref, kinds_ref)
    first_base(
        z, traces, start_table_ref, ints_ref, floats_ref, right_ref, jac_ref, stack_ref, right_sorted_ref, base_ref
    )
    forward_table_ref[...] = jnp.zeros_like(forward_table_ref)
    swept_table_ref[...] = jnp.zeros_like(swept_table_ref)
    forward_ref[...] = jnp.zeros_like(forward_ref)
    swept_ref[...] = jnp.zeros_like(swept_ref)
    missing_forward = jnp.sum(jnp.where(floats_ref[4] > 0, 1.0, 0.0), axis=0, keepdims=True)
    missing_swept = jnp.sum(jnp.where(floats_ref[5] > 0, 1.0, 0.0), axis=0, keepdims=True)
    steps(
        z,
        span_ref,
        missing_forward,
        missing_swept,
        ints_ref,
        floats_ref,
        near_ref,
        weights_ref,
        jac_ref,
        pick_ref,
        chunks_ref,
        forward_table_ref,
        swept_table_ref,
        forward_ref,
        swept_ref,
        base_ref,
        right_sorted_ref,
        stack_ref,
        part_ref,
        fresh_ref,
        fetch,
        open_ref,
    )
    send_messages(z, curve, sends_ref, kinds_ref, forward_table_ref, swept_table_ref, message_ref)


def round_kernel(
    z,
    curve_ref,
    span_ref,
    arrived_ref,
    ints_ref,
    floats_ref,
    sends_ref,
    near_ref,
    weights_ref,
    jac_ref,
    pick_ref,
    chunks_in,
    base_ref,
    right_ref,
    start_slots_ref,
    kinds_ref,
    forward_table_in,
    swept_table_in,
    forward_in,
    swept_in,
    message_ref,
    more_ref,
    forward_table_ref,
    swept_table_ref,
    forward_ref,
    swept_ref,
    stack_ref,
    part_ref,
    fresh_ref,
    wide_ref,
    forward_base_ref,
    swept_base_ref,
    chunks_ref,
    sems,
    open_ref,
):
    n = z.columns
    curve = curve_ref[0]

    def fetch(chunk):
        return pltpu.make_async_copy(chunks_in.at[chunk], chunks_ref.at[chunk], sems.at[chunk])

    forward_table_ref[...] = forward_table_in[...]
    swept_table_ref[...] = swept_table_in[...]
    forward_ref[...] = forward_in[...]
    swept_ref[...] = swept_in[...]
    row_id = lax.broadcasted_iota(jnp.int32, (z.trace_pad, n), 0)
    still = jnp.max(arrived_ref[:, 0:1, :], axis=0)
    still = jnp.where(lane_iota(1) == n - 1, still, 0.0)
    more_ref[0] = jnp.max(still).astype(jnp.int32)
    traces = []
    for group in range(3):
        arrived = unpack(z, group, curve, arrived_ref)
        flag = arrived[z.flag : z.flag + 1]
        traces.append(jnp.where((flag > 1.5) & (row_id != z.flag), start_slots_ref[group], arrived))
    missing_forward, missing_swept = later_bases(
        z, traces, ints_ref, floats_ref, base_ref, right_ref, jac_ref, wide_ref, forward_base_ref, swept_base_ref
    )
    steps(
        z,
        span_ref,
        missing_forward,
        missing_swept,
        ints_ref,
        floats_ref,
        near_ref,
        weights_ref,
        jac_ref,
        pick_ref,
        chunks_ref,
        forward_table_ref,
        swept_table_ref,
        forward_ref,
        swept_ref,
        forward_base_ref,
        swept_base_ref,
        stack_ref,
        part_ref,
        fresh_ref,
        fetch,
        open_ref,
    )
    send_messages(z, curve, sends_ref, kinds_ref, forward_table_ref, swept_table_ref, message_ref)


def output_kernel(z, ints_ref, forward_ref, swept_ref, forward_out, swept_out):
    pos = ints_ref[0][0:1]
    for source, target in ((forward_ref, forward_out), (swept_ref, swept_out)):
        for group in range(GROUPS):
            count = min(z.rows, z.block - group * z.rows)
            block = lane_take(source[pl.ds(group * z.rows_pad, z.rows_pad), :], pos)
            target[pl.ds(group * z.rows, count), :] = block[:count]


def call(kernel, outs, inputs, scratch=(), aliases=None, smem_in=(), smem_out=(), hbm_in=(), hbm_out=(), vmem=24):
    whole, smem = pl.BlockSpec(memory_space=pltpu.VMEM), pl.BlockSpec(memory_space=pltpu.SMEM)
    hbm = pl.BlockSpec(memory_space=pltpu.HBM)
    return pl.pallas_call(
        kernel,
        out_shape=outs,
        in_specs=[smem if at in smem_in else hbm if at in hbm_in else whole for at in range(inputs)],
        out_specs=[smem if at in smem_out else hbm if at in hbm_out else whole for at in range(len(outs))],
        scratch_shapes=list(scratch),
        input_output_aliases=aliases or {},
        compiler_params=pltpu.CompilerParams(vmem_limit_bytes=vmem << 20),
    )


def shape(*dims, kind=F32):
    return jax.ShapeDtypeStruct(dims, kind)


def kept(*dims, kind=F32):
    return pltpu.VMEM(dims, kind)


def body(
    start_state,
    right_side,
    block_inverse,
    lifted_flux_jacobian,
    face_weight,
    dep_level,
    face_link,
    send_list,
    recv_list,
):
    curves, slabs = lax.axis_size("curve"), lax.axis_size("slab")
    levels = send_list.shape[0]
    cap = send_list.shape[1] // (curves * slabs)
    slots = levels * cap
    block, n = start_state.shape
    z = Sizes(block, n, levels, slots, curves, slabs)
    own = lax.axis_index("curve").astype(jnp.int32)
    curve = own.reshape(1)

    stride = slabs * cap
    lists = jnp.concatenate([send_list, recv_list], axis=0)
    lists = jnp.pad(lists, ((0, 0), (stride, n)), constant_values=FACES * n)
    lists = lax.dynamic_slice_in_dim(lists, own * stride, n, axis=1)
    slot_level = jnp.asarray(
        np.tile(np.repeat(np.arange(levels), cap), slabs).reshape(1, n), jnp.int32
    )
    pick = jnp.asarray(selector(z), BF16)
    jac = jnp.pad(
        lifted_flux_jacobian, ((0, 0), (0, z.jac_rows - block), (0, z.trace_pad - z.trace))
    )
    jac = jac.transpose(1, 0, 2).reshape(z.jac_rows, z.table_rows)
    rounded = lax.reduce_precision(jac, 8, 7)
    high, low = rounded.astype(BF16), (jac - rounded).astype(BF16)
    jac = jnp.concatenate([high, high, low], axis=1)

    ints, floats, sends, span, start_table, message = call(
        functools.partial(prepare_kernel, z),
        [
            kept(5, SUB, n, kind=jnp.int32),
            kept(7, SUB, n),
            kept(3, SUB, n, kind=jnp.int32),
            shape(2 * levels, kind=jnp.int32),
            kept(z.table_rows, n),
            shape(z.devices, 16, n),
        ],
        8,
        scratch=[pltpu.VMEM((z.state_rows, n), F32)],
        smem_in=(0,),
        smem_out=(3,),
        vmem=60,
    )(curve, start_state, dep_level.reshape(1, n), face_link, face_weight, lists, slot_level, pick)
    message, jac = lax.optimization_barrier((message, jac))

    def exchange(message):
        return lax.all_to_all(message, ("curve", "slab"), 0, 0, tiled=True)

    arrived = exchange(message)
    depth = 6
    chunks, near, weights = call(
        functools.partial(blocks_kernel, z),
        [
            shape(GROUPS, z.rows, z.block_pad, n),
            shape(GROUPS, SUB, n, kind=jnp.int32),
            shape(GROUPS, 3, SUB, n),
        ],
        3,
        scratch=[
            pltpu.VMEM((depth, GROUPS, z.block_pad, n), F32),
            pltpu.VMEM((GROUPS, z.rows, z.block_pad, n), F32),
            pltpu.SemaphoreType.DMA((depth, GROUPS)),
            pltpu.SemaphoreType.DMA((z.rows,)),
        ],
        hbm_in=(0,),
        hbm_out=(0,),
        vmem=48,
    )(block_inverse, ints, floats)
    tables = [
        kept(z.table_rows, n),
        kept(z.table_rows, n),
        kept(z.state_rows, n),
        kept(z.state_rows, n),
    ]
    scratch = [
        pltpu.VMEM((z.table_rows, n), F32),
        pltpu.VMEM((z.rows_pad, n), F32),
        pltpu.VMEM((SUB, n), F32),
    ]
    blocks = [
        pltpu.VMEM((GROUPS, z.rows, z.block_pad, n), F32),
        pltpu.SemaphoreType.DMA((GROUPS,)),
        pltpu.SMEM((GROUPS,), jnp.int32),
    ]
    message, base, right, start_slots, kinds, *state = call(
        functools.partial(first_kernel, z),
        [
            shape(z.devices, 16, n),
            kept(z.block_pad, n),
            kept(z.block_pad, n),
            kept(3, z.trace_pad, n),
            kept(3, n, kind=jnp.int32),
        ]
        + tables,
        14,
        scratch=scratch + blocks,
        smem_in=(0, 1),
        hbm_in=(13,),
        vmem=16,
    )(
        curve,
        span,
        right_side,
        slot_level,
        start_table,
        arrived,
        ints,
        floats,
        sends,
        near,
        weights,
        jac,
        pick,
        chunks,
    )

    round_call = call(
        functools.partial(round_kernel, z),
        [shape(z.devices, 16, n), shape(1, kind=jnp.int32)] + tables,
        19,
        scratch=scratch
        + [
            pltpu.VMEM((z.table_rows, 2 * n), F32),
            pltpu.VMEM((z.block_pad, n), F32),
            pltpu.VMEM((z.block_pad, n), F32),
        ]
        + blocks,
        aliases={15: 2, 16: 3, 17: 4, 18: 5},
        smem_in=(0, 1),
        smem_out=(1,),
        hbm_in=(10,),
        vmem=16,
    )

    def one_round(carry):
        _, message, state = carry
        message, more, *state = round_call(
            curve,
            span,
            exchange(message),
            ints,
            floats,
            sends,
            near,
            weights,
            jac,
            pick,
            chunks,
            base,
            right,
            start_slots,
            kinds,
            *state,
        )
        return more[0], message, tuple(state)

    start = (jnp.array(1, jnp.int32), message, tuple(state))
    _, _, state = lax.while_loop(lambda carry: carry[0] > 0, one_round, start)
    return tuple(
        call(functools.partial(output_kernel, z), [shape(block, n), shape(block, n)], 3)(
            ints, state[2], state[3]
        )
    )


def solution(mesh):
    split = ("curve", "slab")
    return jax.shard_map(
        body,
        mesh=mesh,
        in_specs=(
            P(None, split),
            P(None, split),
            P(None, None, split),
            P(),
            P(None, split),
            P(split),
            P(None, split),
            P(None, split),
            P(None, split),
        ),
        out_specs=(P(None, split), P(None, split)),
        check_vma=False,
    )
```

```python
import functools

import jax
import jax.numpy as jnp
import numpy as np
from jax import lax
from jax.experimental import pallas as pl
from jax.experimental.pallas import tpu as pltpu
from jax.sharding import PartitionSpec as P

VARS = 5
SIDE = 3
FACES = 6
LANES = 128
SUB = 8
GROUPS = 8
F32 = jnp.float32
BF16 = jnp.bfloat16


class Sizes:
    def __init__(self, block, columns, levels, slots, curves, slabs):
        self.block = block
        self.columns = columns
        self.levels = levels
        self.slots = slots
        self.curves = curves
        self.slabs = slabs
        self.devices = curves * slabs
        self.trace = VARS * SIDE * SIDE
        self.width = columns // GROUPS
        self.rows = -(-block // GROUPS)
        self.rows_pad = -(-(self.rows + 1) // SUB) * SUB
        self.state_rows = GROUPS * self.rows_pad
        self.block_pad = -(-block // SUB) * SUB
        self.flag = self.trace
        self.wish = self.trace + 1
        self.trace_pad = -(-(self.trace + 3) // 16) * 16
        self.open = self.trace + 2
        self.cuts = LANES // slots
        self.cut_rows = self.trace_pad // self.cuts
        self.tiles = self.cut_rows // 4
        self.table_rows = FACES * self.trace_pad
        self.jac_rows = -(-self.block_pad // 16) * 16
        assert columns == LANES and slabs * slots == LANES
        assert self.tiles * 4 * self.cuts == self.trace_pad and self.open == self.trace_pad - 1
        assert block < self.block_pad


def face_rows():
    nodes = np.arange(VARS * SIDE**3).reshape(VARS, SIDE, SIDE, SIDE)
    last = SIDE - 1
    sides = [
        nodes[:, 0],
        nodes[:, last],
        nodes[:, :, 0],
        nodes[:, :, last],
        nodes[:, :, :, 0],
        nodes[:, :, :, last],
    ]
    return [side.reshape(-1) for side in sides]


def selector(z):
    pick = np.zeros((z.table_rows, z.state_rows), np.float32)
    for face, rows in enumerate(face_rows()):
        for h, i in enumerate(rows):
            pick[face * z.trace_pad + h, i // z.rows * z.rows_pad + i % z.rows] = 1
        pick[face * z.trace_pad + z.flag, z.rows] = 1
    return np.concatenate([pick, pick], axis=1)


def lane_take(values, index):
    index = jnp.broadcast_to(index, values.shape)
    return jnp.take_along_axis(values, index, axis=1, mode="promise_in_bounds")


def lane_iota(rows=SUB):
    return lax.broadcasted_iota(jnp.int32, (rows, LANES), 1)


def halves(values):
    high = values.astype(BF16)
    low = (values - high.astype(F32)).astype(BF16)
    return high, low


def as_column(row):
    return jnp.broadcast_to(row, (LANES, LANES)).T


def dot(a, b):
    return jnp.dot(a, b, preferred_element_type=F32)


def tables_of(state, pick):
    high, low = halves(state)
    return dot(pick, jnp.concatenate([high, low], axis=0))


def fluxes(jac, traces):
    high, low = halves(traces)
    return dot(jac, jnp.concatenate([high, low, high], axis=0))


def pack(z, message, group, curve, out_ref):
    lanes = lane_iota(z.cut_rows)
    target = curve + group - 1

    @pl.when((target >= 0) & (target < z.curves))
    def _():
        parts = [message[cut * z.cut_rows : (cut + 1) * z.cut_rows] for cut in range(z.cuts)]
        for slab in range(z.slabs):
            block = parts[0]
            for cut in range(z.cuts):
                shift = (cut - slab) * z.slots % LANES
                part = pltpu.roll(parts[cut], shift, 1) if shift else parts[cut]
                block = jnp.where(lanes // z.slots == cut, part, block)
            for tile in range(z.tiles):
                out_ref[target * z.slabs + slab, tile] = block[tile * 4 : tile * 4 + 4]


def unpack(z, group, curve, in_ref):
    lanes = lane_iota(z.cut_rows)
    source = jnp.clip(curve + group - 1, 0, z.curves - 1)
    blocks = [
        jnp.concatenate([in_ref[source * z.slabs + slab, tile] for tile in range(z.tiles)], axis=0)
        for slab in range(z.slabs)
    ]
    parts = []
    for cut in range(z.cuts):
        part = blocks[0]
        for slab in range(z.slabs):
            shift = (slab - cut) * z.slots % LANES
            block = pltpu.roll(blocks[slab], shift, 1) if shift else blocks[slab]
            part = jnp.where(lanes // z.slots == slab, block, part)
        parts.append(part)
    return jnp.concatenate(parts, axis=0)


def ghost_take(z, slot_traces, where, face):
    index = jnp.maximum(where[face : face + 1], 0)
    lane = jnp.bitwise_and(index, LANES - 1)
    block = index // LANES
    found = jnp.zeros((z.trace_pad, LANES), F32)
    for group in range(3):
        found = jnp.where(block == group, lane_take(slot_traces[group], lane), found)
    return found


def regroup(z, lists_ref, level_ref):
    n = z.columns
    cap = z.slots // z.levels
    lane = lane_iota(1)
    source = lane // z.slots * cap + jnp.bitwise_and(lane, cap - 1)
    row_id = lax.broadcasted_iota(jnp.int32, (z.levels, n), 0)
    own_row = row_id == level_ref[...]
    both = []
    for at in range(2):
        lists = lists_ref[pl.ds(at * z.levels, z.levels), :]
        rows = []
        for group in range(3):
            taken = lane_take(lists, source + group * z.slabs * cap)
            rows.append(jnp.sum(jnp.where(own_row, taken, 0).astype(F32), axis=0, keepdims=True))
        rows.append(jnp.full((SUB - 3, n), float(FACES * n), F32))
        both.append(jnp.concatenate(rows, axis=0).astype(jnp.int32))
    return both


def prepare_kernel(
    z,
    curve_ref,
    start_ref,
    dep_ref,
    link_ref,
    weight_ref,
    lists_ref,
    level_ref,
    pick_ref,
    ints_ref,
    floats_ref,
    sends_ref,
    span_ref,
    table_ref,
    message_ref,
    state_ref,
):
    n = z.columns
    lanes = lane_iota()
    dep_row = dep_ref[...]
    dep = jnp.broadcast_to(dep_row, (SUB, n))
    key = (dep_row * n + lane_iota(1)).astype(F32)
    earlier = as_column(key) < jnp.broadcast_to(key, (n, n))
    pos_row = jnp.sum(jnp.where(earlier, 1.0, 0.0), axis=0, keepdims=True)
    here = as_column(pos_row) == lane_iota(n).astype(F32)
    element = lax.broadcasted_iota(jnp.int32, (n, n), 0).astype(F32)
    perm_row = jnp.sum(jnp.where(here, element, 0.0), axis=0, keepdims=True)
    pos = jnp.broadcast_to(pos_row.astype(jnp.int32), (SUB, n))
    perm = jnp.broadcast_to(perm_row.astype(jnp.int32), (SUB, n))
    dep_sorted = lane_take(dep, perm)
    for level in range(z.levels):
        before = jnp.sum(jnp.where(dep_row < level, 1.0, 0.0)).astype(jnp.int32)
        upto = jnp.sum(jnp.where(dep_row <= level, 1.0, 0.0)).astype(jnp.int32)
        span_ref[level] = before // z.width
        span_ref[z.levels + level] = jnp.where(upto > before, (upto + z.width - 1) // z.width, before // z.width)

    link = jnp.concatenate([link_ref[...], jnp.full((SUB - FACES, n), -1, jnp.int32)], axis=0)
    near = jnp.where(link >= 0, lane_take(pos, jnp.maximum(link, 0)), -1)
    near = lane_take(near, perm)
    weight = jnp.concatenate([weight_ref[...], jnp.zeros((SUB - FACES, n), F32)], axis=0)
    weight = lane_take(weight, perm)
    local = near >= 0
    near = jnp.maximum(near, 0)
    dep_near = lane_take(dep_sorted, near)
    zero = jnp.zeros_like(weight)

    send, recv = regroup(z, lists_ref, level_ref)
    slot_level = jnp.broadcast_to(level_ref[...], (SUB, n))
    rows = []
    slot_id = lax.broadcasted_iota(jnp.int32, (n, n), 0).astype(F32) + 1.0
    columns = [as_column(recv[group : group + 1].astype(F32)) for group in range(3)]
    for face in range(FACES):
        name = (lane_iota(n) + face * n).astype(F32)
        found = jnp.zeros((1, n), F32)
        for group in range(3):
            hit = jnp.where(columns[group] == name, slot_id + float(group * n), 0.0)
            found = jnp.maximum(found, jnp.max(hit, axis=0, keepdims=True))
        rows.append(found)
    rows.append(jnp.zeros((SUB - FACES, n), F32))
    slot = jnp.concatenate(rows, axis=0).astype(jnp.int32) - 1
    slot = lane_take(slot, perm)
    from_far = slot >= 0
    slot = jnp.maximum(slot, 0)
    far_level = lane_take(slot_level, jnp.bitwise_and(slot, n - 1))

    for at, value in enumerate((pos, perm, dep_sorted, near, slot)):
        ints_ref[at] = value
    floats_ref[0] = jnp.where(local & (dep_near < dep_sorted), weight, zero)
    floats_ref[1] = jnp.where(local & (dep_near > dep_sorted), weight, zero)
    floats_ref[2] = jnp.where(local & (dep_near <= dep_sorted), weight, zero)
    floats_ref[3] = jnp.where(local & (dep_near >= dep_sorted), weight, zero)
    floats_ref[4] = jnp.where(from_far & (far_level < dep_sorted), weight, zero)
    floats_ref[5] = jnp.where(from_far, weight, zero)
    floats_ref[6] = jnp.where(from_far & (far_level >= dep_sorted), weight, zero)

    send_element = jnp.bitwise_and(send, n - 1)
    sends_ref[0] = lane_take(pos, send_element)
    sends_ref[1] = send // n
    sends_ref[2] = lane_take(dep, send_element)
    recv_dep = lane_take(dep, jnp.bitwise_and(recv, n - 1))
    wish = jnp.where(slot_level <= recv_dep, 1.0, 0.0)

    state_ref[...] = jnp.zeros_like(state_ref)
    for group in range(GROUPS):
        count = min(z.rows, z.block - group * z.rows)
        state_ref[pl.ds(group * z.rows_pad, count), :] = start_ref[pl.ds(group * z.rows, count), :]
    state_ref[pl.ds(z.rows, 1), :] = jnp.ones((1, n), F32)
    state = lane_take(state_ref[...], perm[0:1])
    table = tables_of(state, pick_ref[...])
    table_ref[...] = table
    message_ref[...] = jnp.zeros_like(message_ref)
    row_id = lax.broadcasted_iota(jnp.int32, (z.trace_pad, n), 0)
    for group in range(3):
        where = sends_ref[0][group : group + 1]
        side = sends_ref[1][group : group + 1]
        message = jnp.zeros((z.trace_pad, n), F32)
        for face in range(FACES):
            piece = table[face * z.trace_pad : (face + 1) * z.trace_pad]
            message = jnp.where(side == face, lane_take(piece, where), message)
        message = jnp.where(row_id == z.wish, wish[group : group + 1], message)
        pack(z, message, group, curve_ref[0], message_ref)


def block_copies(z, ii, inverse_ref, buffer_ref, sems):
    slot = lax.rem(ii, buffer_ref.shape[0])
    for group in range(GROUPS):
        i = jnp.minimum(group * z.rows + ii, z.block - 1)
        yield pltpu.make_async_copy(
            inverse_ref.at[i], buffer_ref.at[slot, group, pl.ds(0, z.block)], sems.at[slot, group]
        )


def chunk_tables(z, ints_ref, floats_ref, near_ref, weights_ref):
    for chunk in range(GROUPS):
        own = chunk * z.width + jnp.bitwise_and(lane_iota(), z.width - 1)
        near_ref[chunk] = lane_take(ints_ref[3], own)
        for at in range(3):
            weights_ref[chunk, at] = lane_take(floats_ref[at], own)


def chunk_copy(ii, chunks_ref, out_ref, sems):
    return pltpu.make_async_copy(chunks_ref.at[:, ii], out_ref.at[:, ii], sems.at[ii])


def arrange_blocks(z, inverse_ref, ints_ref, chunks_ref, out_ref, buffer_ref, sems, out_sems):
    n = z.columns
    perm = ints_ref[1]
    depth = buffer_ref.shape[0]
    orders = [pltpu.roll(perm, group * z.width, 1) if group else perm for group in range(GROUPS)]
    bits = [jnp.bitwise_and(lane_iota() // (z.width << b), 1) == 1 for b in range(3)]

    def row(ii, carry):
        @pl.when(ii + depth - 1 < z.rows)
        def _():
            for copy in block_copies(z, ii + depth - 1, inverse_ref, buffer_ref, sems):
                copy.start()

        for copy in block_copies(z, ii, inverse_ref, buffer_ref, sems):
            copy.wait()
        slot = lax.rem(ii, depth)
        for tile in range(z.block_pad // SUB):
            at = pl.ds(tile * SUB, SUB)
            spread = [lane_take(buffer_ref[slot, group, at, :], orders[group]) for group in range(GROUPS)]
            for b in range(3):
                spread = [
                    jnp.where(bits[b], spread[(x + (1 << b)) % GROUPS], spread[x])
                    for x in range(GROUPS)
                ]
            for chunk in range(GROUPS):
                chunks_ref[chunk, ii, at, :] = spread[-chunk % GROUPS]
        chunk_copy(ii, chunks_ref, out_ref, out_sems).start()
        return carry

    lax.fori_loop(0, z.rows, row, 0)


def blocks_kernel(
    z, inverse_ref, ints_ref, floats_ref, chunks_out, near_ref, weights_ref, buffer_ref, chunks_ref, sems, out_sems
):
    depth = buffer_ref.shape[0]
    buffer_ref[:, :, z.block :, :] = jnp.zeros((depth, GROUPS, z.block_pad - z.block, z.columns), F32)
    for first in range(depth - 1):
        for copy in block_copies(z, first, inverse_ref, buffer_ref, sems):
            copy.start()
    chunk_tables(z, ints_ref, floats_ref, near_ref, weights_ref)
    arrange_blocks(z, inverse_ref, ints_ref, chunks_ref, chunks_out, buffer_ref, sems, out_sems)
    for ii in range(z.rows):
        chunk_copy(ii, chunks_ref, chunks_out, out_sems).wait()


def first_base(z, traces, start_table_ref, ints_ref, floats_ref, right_ref, jac_ref, stack_ref, right_sorted_ref, base_ref):
    n = z.columns
    near = ints_ref[3]
    slot = ints_ref[4]
    for face in range(FACES):
        piece = start_table_ref[pl.ds((face ^ 1) * z.trace_pad, z.trace_pad), :]
        value = lane_take(piece, near[face : face + 1]) * floats_ref[3][face : face + 1]
        ghost = ghost_take(z, traces, slot, face) * floats_ref[6][face : face + 1]
        stack_ref[pl.ds(face * z.trace_pad, z.trace_pad), :] = value + ghost
    flow = fluxes(jac_ref[...], stack_ref[...])[: z.block_pad]
    right = jnp.concatenate([right_ref[...], jnp.zeros((z.block_pad - z.block, n), F32)], axis=0)
    right = lane_take(right, ints_ref[1][0:1])
    right_sorted_ref[...] = right
    base_ref[...] = right - flow


def send_kinds(z, traces, sends_ref, level_ref, kinds_ref):
    for group in range(3):
        wish = traces[group][z.wish : z.wish + 1] > 0.5
        side = sends_ref[1][group : group + 1]
        dep = sends_ref[2][group : group + 1]
        level = level_ref[...]
        kind = jnp.where(wish, jnp.where(dep <= level, 1, 3), jnp.where(dep >= level, 2, 1))
        kinds_ref[pl.ds(group, 1), :] = jnp.where(side < FACES, kind, 0)


def later_bases(z, traces, ints_ref, floats_ref, base_ref, right_ref, jac_ref, wide_ref, forward_base_ref, swept_base_ref):
    n = z.columns
    slot = ints_ref[4]
    missing_forward = jnp.zeros((1, n), F32)
    missing_swept = jnp.zeros((1, n), F32)
    for face in range(FACES):
        ghost = ghost_take(z, traces, slot, face)
        forward_weight = floats_ref[4][face : face + 1]
        swept_weight = floats_ref[5][face : face + 1]
        lost = jnp.where(ghost[z.flag : z.flag + 1] > 0.5, 0.0, 1.0)
        missing_forward += jnp.where(forward_weight > 0, lost, 0.0)
        missing_swept += jnp.where(swept_weight > 0, lost, 0.0)
        at = pl.ds(face * z.trace_pad, z.trace_pad)
        wide_ref[at, pl.ds(0, n)] = ghost * forward_weight
        wide_ref[at, pl.ds(n, n)] = ghost * swept_weight
    flow = fluxes(jac_ref[...], wide_ref[...])
    forward_base_ref[...] = base_ref[...] - flow[: z.block_pad, :n]
    swept_base_ref[...] = right_ref[...] - flow[: z.block_pad, n:]
    return missing_forward, missing_swept


def steps(
    z,
    span_ref,
    missing_forward,
    missing_swept,
    ints_ref,
    floats_ref,
    near_ref,
    weights_ref,
    jac_ref,
    pick_ref,
    chunks_ref,
    forward_table_ref,
    swept_table_ref,
    forward_ref,
    swept_ref,
    forward_base,
    swept_base,
    stack_ref,
    part_ref,
    fresh_ref,
    fetch=None,
    open_ref=None,
):
    n = z.columns
    near = ints_ref[3]
    dep = ints_ref[2]
    chunk_of = lane_iota(1) // z.width
    per_sum = GROUPS // 2
    part_ref[...] = jnp.where(
        lax.broadcasted_iota(jnp.int32, (z.rows_pad, n), 0) == z.rows, 1.0, 0.0
    )

    def spread(row):
        return jnp.broadcast_to(row, (SUB, n))

    def absent(flags, weights):
        lost = jnp.where(weights > 0, 1.0 - lane_take(flags, near), 0.0)
        return jnp.sum(lost, axis=0, keepdims=True)

    old_forward = spread(forward_table_ref[pl.ds(z.flag, 1), :])
    old_swept = spread(swept_table_ref[pl.ds(z.flag, 1), :])
    forward, swept = old_forward, old_swept
    for level in range(z.levels):
        missing = absent(forward, floats_ref[0]) + missing_forward
        forward = jnp.where((dep == level) & spread(missing < 0.5), 1.0, forward)
    settled = absent(forward, floats_ref[2]) + missing_swept
    for level in range(z.levels - 1, -1, -1):
        missing = absent(swept, floats_ref[1]) + settled
        swept = jnp.where((dep == level) & spread(missing < 0.5), 1.0, swept)
    counts = []
    for at, fresh in enumerate((forward - old_forward, swept - old_swept)):
        fresh = fresh[0:1]
        fresh_ref[pl.ds(at, 1), :] = fresh
        for half in range(2):
            scale = jnp.zeros((1, n), F32)
            for at_chunk in range(per_sum):
                scale = jnp.where(chunk_of == half * per_sum + at_chunk, float((2 * z.width) ** at_chunk), scale)
            counts.append(jnp.sum(fresh * scale).astype(jnp.int32))

    shift = (2 * z.width).bit_length() - 1

    def count_of(chunk, backward):
        low, high = counts[2 * backward], counts[2 * backward + 1]
        bits = jnp.where(chunk >= per_sum, high, low)
        bits = lax.shift_right_logical(bits, lax.rem(chunk, per_sum) * shift)
        return jnp.bitwise_and(bits, 2 * z.width - 1)

    def fetch_for(chunk, backward):
        needed = count_of(chunk, backward) > 0
        if backward:
            needed &= open_ref[chunk] == 0

        @pl.when(needed)
        def _():
            fetch(chunk).start()
            open_ref[chunk] = 1

    if fetch is not None:
        for chunk in range(GROUPS):
            open_ref[chunk] = 0
        for chunk in range(GROUPS):
            fetch_for(jnp.int32(chunk), False)
        for chunk in reversed(range(GROUPS)):
            fetch_for(jnp.int32(chunk), True)

    def step(level, chunk, backward):
        if fetch is not None:

            @pl.when(open_ref[chunk] == 1)
            def _():
                fetch(chunk).wait()
                open_ref[chunk] = 2

        old = forward_table_ref
        new = swept_table_ref
        base = swept_base if backward else forward_base
        rows = near_ref[chunk]
        old_weight = weights_ref[chunk, 2 if backward else 0]
        new_weight = weights_ref[chunk, 1]
        own = chunk * z.width + jnp.bitwise_and(lane_iota(1), z.width - 1)
        for face in range(FACES):
            at = pl.ds((face ^ 1) * z.trace_pad, z.trace_pad)
            row = rows[face : face + 1]
            value = lane_take(old[at, :], row) * old_weight[face : face + 1]
            if backward:
                value += lane_take(new[at, :], row) * new_weight[face : face + 1]
            stack_ref[pl.ds(face * z.trace_pad, z.trace_pad), :] = value
        flow = fluxes(jac_ref[...], stack_ref[...])[: z.block_pad]
        rest = lane_take(base[...], own) - flow
        for ii in range(z.rows):
            part_ref[pl.ds(ii, 1), :] = jnp.sum(chunks_ref[chunk, ii] * rest, axis=0, keepdims=True)
        part = part_ref[...]
        state = jnp.concatenate(
            [pltpu.roll(part, -g * z.width % n, 1) if g else part for g in range(GROUPS)], axis=0
        )
        table = tables_of(state, pick_ref[...])
        fresh = fresh_ref[pl.ds(1 if backward else 0, 1), :] > 0.5
        keep = fresh & (chunk_of == chunk) & (dep[0:1] == level)
        out_state = swept_ref if backward else forward_ref
        out_table = swept_table_ref if backward else forward_table_ref
        out_state[...] = jnp.where(keep, state, out_state[...])
        out_table[...] = jnp.where(keep, table, out_table[...])

    for backward in (False, True):

        def run(count, carry, backward=backward):
            level = z.levels - 1 - count if backward else count

            def one(chunk, inner):
                @pl.when(count_of(chunk, backward) > 0)
                def _():
                    step(level, chunk, backward)

                return inner

            return lax.fori_loop(span_ref[level], span_ref[z.levels + level], one, carry)

        lax.fori_loop(0, z.levels, run, 0)


def send_messages(z, curve, sends_ref, kinds_ref, forward_table_ref, swept_table_ref, message_ref):
    n = z.columns
    row_id = lax.broadcasted_iota(jnp.int32, (z.trace_pad, n), 0)
    messages = []
    still = jnp.zeros((1, n), F32)
    for group in range(3):
        where = sends_ref[0][group : group + 1]
        side = sends_ref[1][group : group + 1]
        kind = kinds_ref[pl.ds(group, 1), :]
        message = jnp.zeros((z.trace_pad, n), F32)
        for face in range(FACES):
            at = pl.ds(face * z.trace_pad, z.trace_pad)
            first = lane_take(forward_table_ref[at, :], where)
            second = lane_take(swept_table_ref[at, :], where)
            picked = jnp.where(kind == 1, first, second)
            message = jnp.where(side == face, picked, message)
        message = jnp.where((kind == 3) & (row_id == z.flag), 2.0, message)
        unsent = (kind > 0) & (message[z.flag : z.flag + 1] < 0.5)
        still = jnp.maximum(still, jnp.where(unsent, 1.0, 0.0))
        messages.append(message)
    still = jnp.broadcast_to(jnp.max(still, axis=1, keepdims=True), (1, n))
    message_ref[...] = jnp.broadcast_to(still[None, None], message_ref.shape)
    for group in range(3):
        message = jnp.where(row_id == z.open, still, messages[group])
        pack(z, message, group, curve, message_ref)


def first_kernel(
    z,
    curve_ref,
    span_ref,
    right_ref,
    level_ref,
    start_table_ref,
    arrived_ref,
    ints_ref,
    floats_ref,
    sends_ref,
    near_ref,
    weights_ref,
    jac_ref,
    pick_ref,
    chunks_in,
    message_ref,
    base_ref,
    right_sorted_ref,
    start_slots_ref,
    kinds_ref,
    forward_table_ref,
    swept_table_ref,
    forward_ref,
    swept_ref,
    stack_ref,
    part_ref,
    fresh_ref,
    chunks_ref,
    sems,
    open_ref,
):
    n = z.columns
    curve = curve_ref[0]

    def fetch(chunk):
        return pltpu.make_async_copy(chunks_in.at[chunk], chunks_ref.at[chunk], sems.at[chunk])

    traces = [unpack(z, group, curve, arrived_ref) for group in range(3)]
    for group in range(3):
        start_slots_ref[group] = traces[group]
    send_kinds(z, traces, sends_ref, level_ref, kinds_ref)
    first_base(
        z, traces, start_table_ref, ints_ref, floats_ref, right_ref, jac_ref, stack_ref, right_sorted_ref, base_ref
    )
    forward_table_ref[...] = jnp.zeros_like(forward_table_ref)
    swept_table_ref[...] = jnp.zeros_like(swept_table_ref)
    forward_ref[...] = jnp.zeros_like(forward_ref)
    swept_ref[...] = jnp.zeros_like(swept_ref)
    missing_forward = jnp.sum(jnp.where(floats_ref[4] > 0, 1.0, 0.0), axis=0, keepdims=True)
    missing_swept = jnp.sum(jnp.where(floats_ref[5] > 0, 1.0, 0.0), axis=0, keepdims=True)
    steps(
        z,
        span_ref,
        missing_forward,
        missing_swept,
        ints_ref,
        floats_ref,
        near_ref,
        weights_ref,
        jac_ref,
        pick_ref,
        chunks_ref,
        forward_table_ref,
        swept_table_ref,
        forward_ref,
        swept_ref,
        base_ref,
        right_sorted_ref,
        stack_ref,
        part_ref,
        fresh_ref,
        fetch,
        open_ref,
    )
    send_messages(z, curve, sends_ref, kinds_ref, forward_table_ref, swept_table_ref, message_ref)


def round_kernel(
    z,
    curve_ref,
    span_ref,
    arrived_ref,
    ints_ref,
    floats_ref,
    sends_ref,
    near_ref,
    weights_ref,
    jac_ref,
    pick_ref,
    chunks_in,
    base_ref,
    right_ref,
    start_slots_ref,
    kinds_ref,
    forward_table_in,
    swept_table_in,
    forward_in,
    swept_in,
    message_ref,
    more_ref,
    forward_table_ref,
    swept_table_ref,
    forward_ref,
    swept_ref,
    stack_ref,
    part_ref,
    fresh_ref,
    wide_ref,
    forward_base_ref,
    swept_base_ref,
    chunks_ref,
    sems,
    open_ref,
):
    n = z.columns
    curve = curve_ref[0]

    def fetch(chunk):
        return pltpu.make_async_copy(chunks_in.at[chunk], chunks_ref.at[chunk], sems.at[chunk])

    forward_table_ref[...] = forward_table_in[...]
    swept_table_ref[...] = swept_table_in[...]
    forward_ref[...] = forward_in[...]
    swept_ref[...] = swept_in[...]
    row_id = lax.broadcasted_iota(jnp.int32, (z.trace_pad, n), 0)
    still = jnp.max(arrived_ref[:, z.tiles - 1, 3:4, :], axis=0)
    still = jnp.where(lane_iota(1) == n - 1, still, 0.0)
    more_ref[0] = jnp.max(still).astype(jnp.int32)
    traces = []
    for group in range(3):
        arrived = unpack(z, group, curve, arrived_ref)
        flag = arrived[z.flag : z.flag + 1]
        traces.append(jnp.where((flag > 1.5) & (row_id != z.flag), start_slots_ref[group], arrived))
    missing_forward, missing_swept = later_bases(
        z, traces, ints_ref, floats_ref, base_ref, right_ref, jac_ref, wide_ref, forward_base_ref, swept_base_ref
    )
    steps(
        z,
        span_ref,
        missing_forward,
        missing_swept,
        ints_ref,
        floats_ref,
        near_ref,
        weights_ref,
        jac_ref,
        pick_ref,
        chunks_ref,
        forward_table_ref,
        swept_table_ref,
        forward_ref,
        swept_ref,
        forward_base_ref,
        swept_base_ref,
        stack_ref,
        part_ref,
        fresh_ref,
        fetch,
        open_ref,
    )
    send_messages(z, curve, sends_ref, kinds_ref, forward_table_ref, swept_table_ref, message_ref)


def output_kernel(z, ints_ref, forward_ref, swept_ref, forward_out, swept_out):
    pos = ints_ref[0][0:1]
    for source, target in ((forward_ref, forward_out), (swept_ref, swept_out)):
        for group in range(GROUPS):
            count = min(z.rows, z.block - group * z.rows)
            block = lane_take(source[pl.ds(group * z.rows_pad, z.rows_pad), :], pos)
            target[pl.ds(group * z.rows, count), :] = block[:count]


def call(kernel, outs, inputs, scratch=(), aliases=None, smem_in=(), smem_out=(), hbm_in=(), hbm_out=(), vmem=24):
    whole, smem = pl.BlockSpec(memory_space=pltpu.VMEM), pl.BlockSpec(memory_space=pltpu.SMEM)
    hbm = pl.BlockSpec(memory_space=pltpu.HBM)
    return pl.pallas_call(
        kernel,
        out_shape=outs,
        in_specs=[smem if at in smem_in else hbm if at in hbm_in else whole for at in range(inputs)],
        out_specs=[smem if at in smem_out else hbm if at in hbm_out else whole for at in range(len(outs))],
        scratch_shapes=list(scratch),
        input_output_aliases=aliases or {},
        compiler_params=pltpu.CompilerParams(vmem_limit_bytes=vmem << 20),
    )


def shape(*dims, kind=F32):
    return jax.ShapeDtypeStruct(dims, kind)


def kept(*dims, kind=F32):
    return pltpu.VMEM(dims, kind)


def body(
    start_state,
    right_side,
    block_inverse,
    lifted_flux_jacobian,
    face_weight,
    dep_level,
    face_link,
    send_list,
    recv_list,
):
    curves, slabs = lax.axis_size("curve"), lax.axis_size("slab")
    levels = send_list.shape[0]
    cap = send_list.shape[1] // (curves * slabs)
    slots = levels * cap
    block, n = start_state.shape
    z = Sizes(block, n, levels, slots, curves, slabs)
    own = lax.axis_index("curve").astype(jnp.int32)
    curve = own.reshape(1)

    stride = slabs * cap
    lists = jnp.concatenate([send_list, recv_list], axis=0)
    lists = jnp.pad(lists, ((0, 0), (stride, n)), constant_values=FACES * n)
    lists = lax.dynamic_slice_in_dim(lists, own * stride, n, axis=1)
    slot_level = jnp.asarray(
        np.tile(np.repeat(np.arange(levels), cap), slabs).reshape(1, n), jnp.int32
    )
    pick = jnp.asarray(selector(z), BF16)
    jac = jnp.pad(
        lifted_flux_jacobian, ((0, 0), (0, z.jac_rows - block), (0, z.trace_pad - z.trace))
    )
    jac = jac.transpose(1, 0, 2).reshape(z.jac_rows, z.table_rows)
    rounded = lax.reduce_precision(jac, 8, 7)
    high, low = rounded.astype(BF16), (jac - rounded).astype(BF16)
    jac = jnp.concatenate([high, high, low], axis=1)

    ints, floats, sends, span, start_table, message = call(
        functools.partial(prepare_kernel, z),
        [
            kept(5, SUB, n, kind=jnp.int32),
            kept(7, SUB, n),
            kept(3, SUB, n, kind=jnp.int32),
            shape(2 * levels, kind=jnp.int32),
            kept(z.table_rows, n),
            shape(z.devices, z.tiles, 4, n),
        ],
        8,
        scratch=[pltpu.VMEM((z.state_rows, n), F32)],
        smem_in=(0,),
        smem_out=(3,),
        vmem=60,
    )(curve, start_state, dep_level.reshape(1, n), face_link, face_weight, lists, slot_level, pick)
    message, jac = lax.optimization_barrier((message, jac))

    def exchange(message):
        return lax.all_to_all(message, ("curve", "slab"), 0, 0, tiled=True)

    arrived = exchange(message)
    depth = 6
    chunks, near, weights = call(
        functools.partial(blocks_kernel, z),
        [
            shape(GROUPS, z.rows, z.block_pad, n),
            shape(GROUPS, SUB, n, kind=jnp.int32),
            shape(GROUPS, 3, SUB, n),
        ],
        3,
        scratch=[
            pltpu.VMEM((depth, GROUPS, z.block_pad, n), F32),
            pltpu.VMEM((GROUPS, z.rows, z.block_pad, n), F32),
            pltpu.SemaphoreType.DMA((depth, GROUPS)),
            pltpu.SemaphoreType.DMA((z.rows,)),
        ],
        hbm_in=(0,),
        hbm_out=(0,),
        vmem=48,
    )(block_inverse, ints, floats)
    tables = [
        kept(z.table_rows, n),
        kept(z.table_rows, n),
        kept(z.state_rows, n),
        kept(z.state_rows, n),
    ]
    scratch = [
        pltpu.VMEM((z.table_rows, n), F32),
        pltpu.VMEM((z.rows_pad, n), F32),
        pltpu.VMEM((SUB, n), F32),
    ]
    blocks = [
        pltpu.VMEM((GROUPS, z.rows, z.block_pad, n), F32),
        pltpu.SemaphoreType.DMA((GROUPS,)),
        pltpu.SMEM((GROUPS,), jnp.int32),
    ]
    message, base, right, start_slots, kinds, *state = call(
        functools.partial(first_kernel, z),
        [
            shape(z.devices, z.tiles, 4, n),
            kept(z.block_pad, n),
            kept(z.block_pad, n),
            kept(3, z.trace_pad, n),
            kept(3, n, kind=jnp.int32),
        ]
        + tables,
        14,
        scratch=scratch + blocks,
        smem_in=(0, 1),
        hbm_in=(13,),
        vmem=16,
    )(
        curve,
        span,
        right_side,
        slot_level,
        start_table,
        arrived,
        ints,
        floats,
        sends,
        near,
        weights,
        jac,
        pick,
        chunks,
    )

    round_call = call(
        functools.partial(round_kernel, z),
        [shape(z.devices, z.tiles, 4, n), shape(1, kind=jnp.int32)] + tables,
        19,
        scratch=scratch
        + [
            pltpu.VMEM((z.table_rows, 2 * n), F32),
            pltpu.VMEM((z.block_pad, n), F32),
            pltpu.VMEM((z.block_pad, n), F32),
        ]
        + blocks,
        aliases={15: 2, 16: 3, 17: 4, 18: 5},
        smem_in=(0, 1),
        smem_out=(1,),
        hbm_in=(10,),
        vmem=16,
    )

    def one_round(carry):
        _, message, state = carry
        message, more, *state = round_call(
            curve,
            span,
            exchange(message),
            ints,
            floats,
            sends,
            near,
            weights,
            jac,
            pick,
            chunks,
            base,
            right,
            start_slots,
            kinds,
            *state,
        )
        return more[0], message, tuple(state)

    start = (jnp.array(1, jnp.int32), message, tuple(state))
    _, _, state = lax.while_loop(lambda carry: carry[0] > 0, one_round, start)
    return tuple(
        call(functools.partial(output_kernel, z), [shape(block, n), shape(block, n)], 3)(
            ints, state[2], state[3]
        )
    )


def solution(mesh):
    split = ("curve", "slab")
    return jax.shard_map(
        body,
        mesh=mesh,
        in_specs=(
            P(None, split),
            P(None, split),
            P(None, None, split),
            P(),
            P(None, split),
            P(split),
            P(None, split),
            P(None, split),
            P(None, split),
        ),
        out_specs=(P(None, split), P(None, split)),
        check_vma=False,
    )
```

```python
import functools

import jax
import jax.numpy as jnp
import numpy as np
from jax import lax
from jax.experimental import pallas as pl
from jax.experimental.pallas import tpu as pltpu
from jax.sharding import PartitionSpec as P

VARS = 5
SIDE = 3
FACES = 6
LANES = 128
SUB = 8
GROUPS = 8
F32 = jnp.float32
BF16 = jnp.bfloat16


class Sizes:
    def __init__(self, block, columns, levels, slots, curves, slabs):
        self.block = block
        self.columns = columns
        self.levels = levels
        self.slots = slots
        self.curves = curves
        self.slabs = slabs
        self.devices = curves * slabs
        self.trace = VARS * SIDE * SIDE
        self.width = columns // GROUPS
        self.rows = -(-block // GROUPS)
        self.rows_pad = -(-(self.rows + 1) // SUB) * SUB
        self.state_rows = GROUPS * self.rows_pad
        self.block_pad = -(-block // SUB) * SUB
        self.flag = self.trace
        self.wish = self.trace + 1
        self.trace_pad = -(-(self.trace + 3) // 16) * 16
        self.open = self.trace + 2
        self.cuts = LANES // slots
        self.cut_rows = self.trace_pad // self.cuts
        self.tiles = self.cut_rows // 4
        self.table_rows = FACES * self.trace_pad
        self.jac_rows = -(-self.block_pad // 16) * 16
        assert columns == LANES and slabs * slots == LANES
        assert self.tiles * 4 * self.cuts == self.trace_pad and self.open == self.trace_pad - 1
        assert block < self.block_pad


def face_rows():
    nodes = np.arange(VARS * SIDE**3).reshape(VARS, SIDE, SIDE, SIDE)
    last = SIDE - 1
    sides = [
        nodes[:, 0],
        nodes[:, last],
        nodes[:, :, 0],
        nodes[:, :, last],
        nodes[:, :, :, 0],
        nodes[:, :, :, last],
    ]
    return [side.reshape(-1) for side in sides]


def selector(z):
    pick = np.zeros((z.table_rows, z.state_rows), np.float32)
    for face, rows in enumerate(face_rows()):
        for h, i in enumerate(rows):
            pick[face * z.trace_pad + h, i // z.rows * z.rows_pad + i % z.rows] = 1
        pick[face * z.trace_pad + z.flag, z.rows] = 1
    return np.concatenate([pick, pick], axis=1)


def lane_take(values, index):
    index = jnp.broadcast_to(index, values.shape)
    return jnp.take_along_axis(values, index, axis=1, mode="promise_in_bounds")


def lane_iota(rows=SUB):
    return lax.broadcasted_iota(jnp.int32, (rows, LANES), 1)


def halves(values):
    high = values.astype(BF16)
    low = (values - high.astype(F32)).astype(BF16)
    return high, low


def as_column(row):
    return jnp.broadcast_to(row, (LANES, LANES)).T


def dot(a, b):
    return jnp.dot(a, b, preferred_element_type=F32)


def tables_of(state, pick):
    high, low = halves(state)
    return dot(pick, jnp.concatenate([high, low], axis=0))


def fluxes(jac, traces):
    high, low = halves(traces)
    return dot(jac, jnp.concatenate([high, low, high], axis=0))


def pack(z, message, group, curve, out_ref):
    lanes = lane_iota(z.cut_rows)
    target = curve + group - 1

    @pl.when((target >= 0) & (target < z.curves))
    def _():
        parts = [message[cut * z.cut_rows : (cut + 1) * z.cut_rows] for cut in range(z.cuts)]
        for slab in range(z.slabs):
            block = parts[0]
            for cut in range(z.cuts):
                shift = (cut - slab) * z.slots % LANES
                part = pltpu.roll(parts[cut], shift, 1) if shift else parts[cut]
                block = jnp.where(lanes // z.slots == cut, part, block)
            for tile in range(z.tiles):
                out_ref[target * z.slabs + slab, tile] = block[tile * 4 : tile * 4 + 4]


def unpack(z, group, curve, in_ref):
    lanes = lane_iota(z.cut_rows)
    source = jnp.clip(curve + group - 1, 0, z.curves - 1)
    blocks = [
        jnp.concatenate([in_ref[source * z.slabs + slab, tile] for tile in range(z.tiles)], axis=0)
        for slab in range(z.slabs)
    ]
    parts = []
    for cut in range(z.cuts):
        part = blocks[0]
        for slab in range(z.slabs):
            shift = (slab - cut) * z.slots % LANES
            block = pltpu.roll(blocks[slab], shift, 1) if shift else blocks[slab]
            part = jnp.where(lanes // z.slots == slab, block, part)
        parts.append(part)
    return jnp.concatenate(parts, axis=0)


def ghost_take(z, slot_traces, where, face):
    index = jnp.maximum(where[face : face + 1], 0)
    lane = jnp.bitwise_and(index, LANES - 1)
    block = index // LANES
    found = jnp.zeros((z.trace_pad, LANES), F32)
    for group in range(3):
        found = jnp.where(block == group, lane_take(slot_traces[group], lane), found)
    return found


def regroup(z, lists_ref, level_ref):
    n = z.columns
    cap = z.slots // z.levels
    lane = lane_iota(1)
    source = lane // z.slots * cap + jnp.bitwise_and(lane, cap - 1)
    row_id = lax.broadcasted_iota(jnp.int32, (z.levels, n), 0)
    own_row = row_id == level_ref[...]
    both = []
    for at in range(2):
        lists = lists_ref[pl.ds(at * z.levels, z.levels), :]
        rows = []
        for group in range(3):
            taken = lane_take(lists, source + group * z.slabs * cap)
            rows.append(jnp.sum(jnp.where(own_row, taken, 0).astype(F32), axis=0, keepdims=True))
        rows.append(jnp.full((SUB - 3, n), float(FACES * n), F32))
        both.append(jnp.concatenate(rows, axis=0).astype(jnp.int32))
    return both


def prepare_kernel(
    z,
    curve_ref,
    start_ref,
    dep_ref,
    link_ref,
    weight_ref,
    lists_ref,
    level_ref,
    pick_ref,
    ints_ref,
    floats_ref,
    sends_ref,
    span_ref,
    table_ref,
    message_ref,
    state_ref,
):
    n = z.columns
    lanes = lane_iota()
    dep_row = dep_ref[...]
    dep = jnp.broadcast_to(dep_row, (SUB, n))
    key = (dep_row * n + lane_iota(1)).astype(F32)
    earlier = as_column(key) < jnp.broadcast_to(key, (n, n))
    pos_row = jnp.sum(jnp.where(earlier, 1.0, 0.0), axis=0, keepdims=True)
    here = as_column(pos_row) == lane_iota(n).astype(F32)
    element = lax.broadcasted_iota(jnp.int32, (n, n), 0).astype(F32)
    perm_row = jnp.sum(jnp.where(here, element, 0.0), axis=0, keepdims=True)
    pos = jnp.broadcast_to(pos_row.astype(jnp.int32), (SUB, n))
    perm = jnp.broadcast_to(perm_row.astype(jnp.int32), (SUB, n))
    dep_sorted = lane_take(dep, perm)
    for level in range(z.levels):
        before = jnp.sum(jnp.where(dep_row < level, 1.0, 0.0)).astype(jnp.int32)
        upto = jnp.sum(jnp.where(dep_row <= level, 1.0, 0.0)).astype(jnp.int32)
        span_ref[level] = before // z.width
        span_ref[z.levels + level] = jnp.where(upto > before, (upto + z.width - 1) // z.width, before // z.width)

    link = jnp.concatenate([link_ref[...], jnp.full((SUB - FACES, n), -1, jnp.int32)], axis=0)
    near = jnp.where(link >= 0, lane_take(pos, jnp.maximum(link, 0)), -1)
    near = lane_take(near, perm)
    weight = jnp.concatenate([weight_ref[...], jnp.zeros((SUB - FACES, n), F32)], axis=0)
    weight = lane_take(weight, perm)
    local = near >= 0
    near = jnp.maximum(near, 0)
    dep_near = lane_take(dep_sorted, near)
    zero = jnp.zeros_like(weight)

    send, recv = regroup(z, lists_ref, level_ref)
    slot_level = jnp.broadcast_to(level_ref[...], (SUB, n))
    rows = []
    slot_id = lax.broadcasted_iota(jnp.int32, (n, n), 0).astype(F32) + 1.0
    columns = [as_column(recv[group : group + 1].astype(F32)) for group in range(3)]
    for face in range(FACES):
        name = (lane_iota(n) + face * n).astype(F32)
        found = jnp.zeros((1, n), F32)
        for group in range(3):
            hit = jnp.where(columns[group] == name, slot_id + float(group * n), 0.0)
            found = jnp.maximum(found, jnp.max(hit, axis=0, keepdims=True))
        rows.append(found)
    rows.append(jnp.zeros((SUB - FACES, n), F32))
    slot = jnp.concatenate(rows, axis=0).astype(jnp.int32) - 1
    slot = lane_take(slot, perm)
    from_far = slot >= 0
    slot = jnp.maximum(slot, 0)
    far_level = lane_take(slot_level, jnp.bitwise_and(slot, n - 1))

    for at, value in enumerate((pos, perm, dep_sorted, near, slot)):
        ints_ref[at] = value
    floats_ref[0] = jnp.where(local & (dep_near < dep_sorted), weight, zero)
    floats_ref[1] = jnp.where(local & (dep_near > dep_sorted), weight, zero)
    floats_ref[2] = jnp.where(local & (dep_near <= dep_sorted), weight, zero)
    floats_ref[3] = jnp.where(local & (dep_near >= dep_sorted), weight, zero)
    floats_ref[4] = jnp.where(from_far & (far_level < dep_sorted), weight, zero)
    floats_ref[5] = jnp.where(from_far, weight, zero)
    floats_ref[6] = jnp.where(from_far & (far_level >= dep_sorted), weight, zero)

    send_element = jnp.bitwise_and(send, n - 1)
    sends_ref[0] = lane_take(pos, send_element)
    sends_ref[1] = send // n
    sends_ref[2] = lane_take(dep, send_element)
    recv_dep = lane_take(dep, jnp.bitwise_and(recv, n - 1))
    wish = jnp.where(slot_level <= recv_dep, 1.0, 0.0)

    state_ref[...] = jnp.zeros_like(state_ref)
    for group in range(GROUPS):
        count = min(z.rows, z.block - group * z.rows)
        state_ref[pl.ds(group * z.rows_pad, count), :] = start_ref[pl.ds(group * z.rows, count), :]
    state_ref[pl.ds(z.rows, 1), :] = jnp.ones((1, n), F32)
    state = lane_take(state_ref[...], perm[0:1])
    table = tables_of(state, pick_ref[...])
    table_ref[...] = table
    message_ref[...] = jnp.zeros_like(message_ref)
    row_id = lax.broadcasted_iota(jnp.int32, (z.trace_pad, n), 0)
    for group in range(3):
        where = sends_ref[0][group : group + 1]
        side = sends_ref[1][group : group + 1]
        message = jnp.zeros((z.trace_pad, n), F32)
        for face in range(FACES):
            piece = table[face * z.trace_pad : (face + 1) * z.trace_pad]
            message = jnp.where(side == face, lane_take(piece, where), message)
        message = jnp.where(row_id == z.wish, wish[group : group + 1], message)
        pack(z, message, group, curve_ref[0], message_ref)


def block_copies(z, ii, inverse_ref, buffer_ref, sems):
    slot = lax.rem(ii, buffer_ref.shape[0])
    for group in range(GROUPS):
        i = jnp.minimum(group * z.rows + ii, z.block - 1)
        yield pltpu.make_async_copy(
            inverse_ref.at[i], buffer_ref.at[slot, group, pl.ds(0, z.block)], sems.at[slot, group]
        )


def chunk_tables(z, ints_ref, floats_ref, near_ref, weights_ref):
    for chunk in range(GROUPS):
        own = chunk * z.width + jnp.bitwise_and(lane_iota(), z.width - 1)
        near_ref[chunk] = lane_take(ints_ref[3], own)
        for at in range(3):
            weights_ref[chunk, at] = lane_take(floats_ref[at], own)


def chunk_copy(ii, chunks_ref, out_ref, sems):
    return pltpu.make_async_copy(chunks_ref.at[:, ii], out_ref.at[:, ii], sems.at[ii])


def arrange_blocks(z, inverse_ref, ints_ref, chunks_ref, out_ref, buffer_ref, sems, out_sems):
    n = z.columns
    perm = ints_ref[1]
    depth = buffer_ref.shape[0]
    orders = [pltpu.roll(perm, group * z.width, 1) if group else perm for group in range(GROUPS)]
    bits = [jnp.bitwise_and(lane_iota() // (z.width << b), 1) == 1 for b in range(3)]

    def row(ii, carry):
        @pl.when(ii + depth - 1 < z.rows)
        def _():
            for copy in block_copies(z, ii + depth - 1, inverse_ref, buffer_ref, sems):
                copy.start()

        for copy in block_copies(z, ii, inverse_ref, buffer_ref, sems):
            copy.wait()
        slot = lax.rem(ii, depth)
        for tile in range(z.block_pad // SUB):
            at = pl.ds(tile * SUB, SUB)
            spread = [lane_take(buffer_ref[slot, group, at, :], orders[group]) for group in range(GROUPS)]
            for b in range(3):
                spread = [
                    jnp.where(bits[b], spread[(x + (1 << b)) % GROUPS], spread[x])
                    for x in range(GROUPS)
                ]
            for chunk in range(GROUPS):
                chunks_ref[chunk, ii, at, :] = spread[-chunk % GROUPS]
        chunk_copy(ii, chunks_ref, out_ref, out_sems).start()
        return carry

    lax.fori_loop(0, z.rows, row, 0)


def blocks_kernel(
    z, inverse_ref, ints_ref, floats_ref, chunks_out, near_ref, weights_ref, buffer_ref, chunks_ref, sems, out_sems
):
    depth = buffer_ref.shape[0]
    buffer_ref[:, :, z.block :, :] = jnp.zeros((depth, GROUPS, z.block_pad - z.block, z.columns), F32)
    for first in range(depth - 1):
        for copy in block_copies(z, first, inverse_ref, buffer_ref, sems):
            copy.start()
    chunk_tables(z, ints_ref, floats_ref, near_ref, weights_ref)
    arrange_blocks(z, inverse_ref, ints_ref, chunks_ref, chunks_out, buffer_ref, sems, out_sems)
    for ii in range(z.rows):
        chunk_copy(ii, chunks_ref, chunks_out, out_sems).wait()


def first_base(z, traces, start_table_ref, ints_ref, floats_ref, right_ref, jac_ref, stack_ref, right_sorted_ref, base_ref):
    n = z.columns
    near = ints_ref[3]
    slot = ints_ref[4]
    for face in range(FACES):
        piece = start_table_ref[pl.ds((face ^ 1) * z.trace_pad, z.trace_pad), :]
        value = lane_take(piece, near[face : face + 1]) * floats_ref[3][face : face + 1]
        ghost = ghost_take(z, traces, slot, face) * floats_ref[6][face : face + 1]
        stack_ref[pl.ds(face * z.trace_pad, z.trace_pad), :] = value + ghost
    flow = fluxes(jac_ref[...], stack_ref[...])[: z.block_pad]
    right = jnp.concatenate([right_ref[...], jnp.zeros((z.block_pad - z.block, n), F32)], axis=0)
    right = lane_take(right, ints_ref[1][0:1])
    right_sorted_ref[...] = right
    base_ref[...] = right - flow


def send_kinds(z, traces, sends_ref, level_ref, kinds_ref):
    for group in range(3):
        wish = traces[group][z.wish : z.wish + 1] > 0.5
        side = sends_ref[1][group : group + 1]
        dep = sends_ref[2][group : group + 1]
        level = level_ref[...]
        kind = jnp.where(wish, jnp.where(dep <= level, 1, 3), jnp.where(dep >= level, 2, 1))
        kinds_ref[pl.ds(group, 1), :] = jnp.where(side < FACES, kind, 0)


def later_bases(z, traces, ints_ref, floats_ref, base_ref, right_ref, jac_ref, wide_ref, forward_base_ref, swept_base_ref):
    n = z.columns
    slot = ints_ref[4]
    missing_forward = jnp.zeros((1, n), F32)
    missing_swept = jnp.zeros((1, n), F32)
    for face in range(FACES):
        ghost = ghost_take(z, traces, slot, face)
        forward_weight = floats_ref[4][face : face + 1]
        swept_weight = floats_ref[5][face : face + 1]
        lost = jnp.where(ghost[z.flag : z.flag + 1] > 0.5, 0.0, 1.0)
        missing_forward += jnp.where(forward_weight > 0, lost, 0.0)
        missing_swept += jnp.where(swept_weight > 0, lost, 0.0)
        at = pl.ds(face * z.trace_pad, z.trace_pad)
        wide_ref[at, pl.ds(0, n)] = ghost * forward_weight
        wide_ref[at, pl.ds(n, n)] = ghost * swept_weight
    flow = fluxes(jac_ref[...], wide_ref[...])
    forward_base_ref[...] = base_ref[...] - flow[: z.block_pad, :n]
    swept_base_ref[...] = right_ref[...] - flow[: z.block_pad, n:]
    return missing_forward, missing_swept


def steps(
    z,
    span_ref,
    missing_forward,
    missing_swept,
    ints_ref,
    floats_ref,
    near_ref,
    weights_ref,
    jac_ref,
    pick_ref,
    chunks_ref,
    forward_table_ref,
    swept_table_ref,
    forward_ref,
    swept_ref,
    forward_base,
    swept_base,
    stack_ref,
    part_ref,
    fresh_ref,
    fetch,
    open_ref,
    pending_out,
    pending_in=None,
):
    n = z.columns
    near = ints_ref[3]
    dep = ints_ref[2]
    chunk_of = lane_iota(1) // z.width
    per_sum = GROUPS // 2
    part_ref[...] = jnp.where(
        lax.broadcasted_iota(jnp.int32, (z.rows_pad, n), 0) == z.rows, 1.0, 0.0
    )

    def spread(row):
        return jnp.broadcast_to(row, (SUB, n))

    def absent(flags, weights):
        lost = jnp.where(weights > 0, 1.0 - lane_take(flags, near), 0.0)
        return jnp.sum(lost, axis=0, keepdims=True)

    old_forward = spread(forward_table_ref[pl.ds(z.flag, 1), :])
    old_swept = spread(swept_table_ref[pl.ds(z.flag, 1), :])

    def forward_levels():
        forward = old_forward
        for level in range(z.levels):
            missing = absent(forward, floats_ref[0]) + missing_forward
            forward = jnp.where((dep == level) & spread(missing < 0.5), 1.0, forward)
        return forward

    if pending_in is None:
        forward = forward_levels()
    else:
        unfinished = pending_in[0]
        for chunk in range(1, GROUPS):
            unfinished += pending_in[chunk]
        forward = lax.cond(unfinished > 0, forward_levels, lambda: old_forward)
    swept = old_swept
    settled = absent(forward, floats_ref[2]) + missing_swept
    for level in range(z.levels - 1, -1, -1):
        missing = absent(swept, floats_ref[1]) + settled
        swept = jnp.where((dep == level) & spread(missing < 0.5), 1.0, swept)
    shift = (2 * z.width).bit_length() - 1

    def packed_counts(row):
        found = []
        for half in range(2):
            scale = jnp.zeros((1, n), F32)
            for at_chunk in range(per_sum):
                scale = jnp.where(chunk_of == half * per_sum + at_chunk, float((2 * z.width) ** at_chunk), scale)
            found.append(jnp.sum(row * scale).astype(jnp.int32))
        return found

    def unpacked(pair, chunk):
        bits = jnp.where(chunk >= per_sum, pair[1], pair[0])
        bits = lax.shift_right_logical(bits, lax.rem(chunk, per_sum) * shift)
        return jnp.bitwise_and(bits, 2 * z.width - 1)

    counts = []
    for at, (new, old) in enumerate(((forward, old_forward), (swept, old_swept))):
        fresh = (new - old)[0:1]
        fresh_ref[pl.ds(at, 1), :] = fresh
        counts.append(packed_counts(fresh))
        left = packed_counts(1.0 - new[0:1])
        for chunk in range(GROUPS):
            pending_out[at * GROUPS + chunk] = unpacked(left, jnp.int32(chunk))

    def step(level, chunk, backward):
        @pl.when(open_ref[chunk] == 1)
        def _():
            fetch(chunk).wait()
            open_ref[chunk] = 2

        old = forward_table_ref
        new = swept_table_ref
        base = swept_base if backward else forward_base
        rows = near_ref[chunk]
        old_weight = weights_ref[chunk, 2 if backward else 0]
        new_weight = weights_ref[chunk, 1]
        own = chunk * z.width + jnp.bitwise_and(lane_iota(1), z.width - 1)
        for face in range(FACES):
            at = pl.ds((face ^ 1) * z.trace_pad, z.trace_pad)
            row = rows[face : face + 1]
            value = lane_take(old[at, :], row) * old_weight[face : face + 1]
            if backward:
                value += lane_take(new[at, :], row) * new_weight[face : face + 1]
            stack_ref[pl.ds(face * z.trace_pad, z.trace_pad), :] = value
        flow = fluxes(jac_ref[...], stack_ref[...])[: z.block_pad]
        rest = lane_take(base[...], own) - flow
        for ii in range(z.rows):
            part_ref[pl.ds(ii, 1), :] = jnp.sum(chunks_ref[chunk, ii] * rest, axis=0, keepdims=True)
        part = part_ref[...]
        state = jnp.concatenate(
            [pltpu.roll(part, -g * z.width % n, 1) if g else part for g in range(GROUPS)], axis=0
        )
        table = tables_of(state, pick_ref[...])
        fresh = fresh_ref[pl.ds(1 if backward else 0, 1), :] > 0.5
        keep = fresh & (chunk_of == chunk) & (dep[0:1] == level)
        out_state = swept_ref if backward else forward_ref
        out_table = swept_table_ref if backward else forward_table_ref
        out_state[...] = jnp.where(keep, state, out_state[...])
        out_table[...] = jnp.where(keep, table, out_table[...])

    for backward in (False, True):

        def run(count, carry, backward=backward):
            level = z.levels - 1 - count if backward else count

            def one(chunk, inner):
                @pl.when(unpacked(counts[int(backward)], chunk) > 0)
                def _():
                    step(level, chunk, backward)

                return inner

            return lax.fori_loop(span_ref[level], span_ref[z.levels + level], one, carry)

        lax.fori_loop(0, z.levels, run, 0)

    for chunk in range(GROUPS):

        @pl.when(open_ref[chunk] == 1)
        def _(chunk=chunk):
            fetch(chunk).wait()


def start_fetches(fetch, open_ref, pending_ref):
    for chunk in range(GROUPS):
        wanted = True if pending_ref is None else pending_ref[chunk] > 0
        open_ref[chunk] = 0

        @pl.when(wanted)
        def _(chunk=chunk):
            fetch(chunk).start()
            open_ref[chunk] = 1

    if pending_ref is not None:
        for chunk in reversed(range(GROUPS)):

            @pl.when((pending_ref[GROUPS + chunk] > 0) & (open_ref[chunk] == 0))
            def _(chunk=chunk):
                fetch(chunk).start()
                open_ref[chunk] = 1


def send_messages(z, curve, sends_ref, kinds_ref, forward_table_ref, swept_table_ref, message_ref):
    n = z.columns
    row_id = lax.broadcasted_iota(jnp.int32, (z.trace_pad, n), 0)
    messages = []
    still = jnp.zeros((1, n), F32)
    for group in range(3):
        where = sends_ref[0][group : group + 1]
        side = sends_ref[1][group : group + 1]
        kind = kinds_ref[pl.ds(group, 1), :]
        message = jnp.zeros((z.trace_pad, n), F32)
        for face in range(FACES):
            at = pl.ds(face * z.trace_pad, z.trace_pad)
            first = lane_take(forward_table_ref[at, :], where)
            second = lane_take(swept_table_ref[at, :], where)
            picked = jnp.where(kind == 1, first, second)
            message = jnp.where(side == face, picked, message)
        message = jnp.where((kind == 3) & (row_id == z.flag), 2.0, message)
        unsent = (kind > 0) & (message[z.flag : z.flag + 1] < 0.5)
        still = jnp.maximum(still, jnp.where(unsent, 1.0, 0.0))
        messages.append(message)
    still = jnp.broadcast_to(jnp.max(still, axis=1, keepdims=True), (1, n))
    message_ref[...] = jnp.broadcast_to(still[None, None], message_ref.shape)
    for group in range(3):
        message = jnp.where(row_id == z.open, still, messages[group])
        pack(z, message, group, curve, message_ref)


def first_kernel(
    z,
    curve_ref,
    span_ref,
    right_ref,
    level_ref,
    start_table_ref,
    arrived_ref,
    ints_ref,
    floats_ref,
    sends_ref,
    near_ref,
    weights_ref,
    jac_ref,
    pick_ref,
    chunks_in,
    message_ref,
    base_ref,
    right_sorted_ref,
    start_slots_ref,
    kinds_ref,
    pending_out,
    forward_table_ref,
    swept_table_ref,
    forward_ref,
    swept_ref,
    stack_ref,
    part_ref,
    fresh_ref,
    chunks_ref,
    sems,
    open_ref,
):
    n = z.columns
    curve = curve_ref[0]

    def fetch(chunk):
        return pltpu.make_async_copy(chunks_in.at[chunk], chunks_ref.at[chunk], sems.at[chunk])

    start_fetches(fetch, open_ref, None)
    traces = [unpack(z, group, curve, arrived_ref) for group in range(3)]
    for group in range(3):
        start_slots_ref[group] = traces[group]
    send_kinds(z, traces, sends_ref, level_ref, kinds_ref)
    first_base(
        z, traces, start_table_ref, ints_ref, floats_ref, right_ref, jac_ref, stack_ref, right_sorted_ref, base_ref
    )
    forward_table_ref[...] = jnp.zeros_like(forward_table_ref)
    swept_table_ref[...] = jnp.zeros_like(swept_table_ref)
    forward_ref[...] = jnp.zeros_like(forward_ref)
    swept_ref[...] = jnp.zeros_like(swept_ref)
    missing_forward = jnp.sum(jnp.where(floats_ref[4] > 0, 1.0, 0.0), axis=0, keepdims=True)
    missing_swept = jnp.sum(jnp.where(floats_ref[5] > 0, 1.0, 0.0), axis=0, keepdims=True)
    steps(
        z,
        span_ref,
        missing_forward,
        missing_swept,
        ints_ref,
        floats_ref,
        near_ref,
        weights_ref,
        jac_ref,
        pick_ref,
        chunks_ref,
        forward_table_ref,
        swept_table_ref,
        forward_ref,
        swept_ref,
        base_ref,
        right_sorted_ref,
        stack_ref,
        part_ref,
        fresh_ref,
        fetch,
        open_ref,
        pending_out,
    )
    send_messages(z, curve, sends_ref, kinds_ref, forward_table_ref, swept_table_ref, message_ref)


def round_kernel(
    z,
    curve_ref,
    span_ref,
    arrived_ref,
    ints_ref,
    floats_ref,
    sends_ref,
    near_ref,
    weights_ref,
    jac_ref,
    pick_ref,
    chunks_in,
    base_ref,
    right_ref,
    start_slots_ref,
    kinds_ref,
    forward_table_in,
    swept_table_in,
    forward_in,
    swept_in,
    pending_in,
    message_ref,
    more_ref,
    pending_out,
    forward_table_ref,
    swept_table_ref,
    forward_ref,
    swept_ref,
    stack_ref,
    part_ref,
    fresh_ref,
    wide_ref,
    forward_base_ref,
    swept_base_ref,
    chunks_ref,
    sems,
    open_ref,
):
    n = z.columns
    curve = curve_ref[0]

    def fetch(chunk):
        return pltpu.make_async_copy(chunks_in.at[chunk], chunks_ref.at[chunk], sems.at[chunk])

    start_fetches(fetch, open_ref, pending_in)
    forward_table_ref[...] = forward_table_in[...]
    swept_table_ref[...] = swept_table_in[...]
    forward_ref[...] = forward_in[...]
    swept_ref[...] = swept_in[...]
    row_id = lax.broadcasted_iota(jnp.int32, (z.trace_pad, n), 0)
    still = jnp.max(arrived_ref[:, z.tiles - 1, 3:4, :], axis=0)
    still = jnp.where(lane_iota(1) == n - 1, still, 0.0)
    more_ref[0] = jnp.max(still).astype(jnp.int32)
    traces = []
    for group in range(3):
        arrived = unpack(z, group, curve, arrived_ref)
        flag = arrived[z.flag : z.flag + 1]
        traces.append(jnp.where((flag > 1.5) & (row_id != z.flag), start_slots_ref[group], arrived))
    missing_forward, missing_swept = later_bases(
        z, traces, ints_ref, floats_ref, base_ref, right_ref, jac_ref, wide_ref, forward_base_ref, swept_base_ref
    )
    steps(
        z,
        span_ref,
        missing_forward,
        missing_swept,
        ints_ref,
        floats_ref,
        near_ref,
        weights_ref,
        jac_ref,
        pick_ref,
        chunks_ref,
        forward_table_ref,
        swept_table_ref,
        forward_ref,
        swept_ref,
        forward_base_ref,
        swept_base_ref,
        stack_ref,
        part_ref,
        fresh_ref,
        fetch,
        open_ref,
        pending_out,
        pending_in,
    )
    send_messages(z, curve, sends_ref, kinds_ref, forward_table_ref, swept_table_ref, message_ref)


def output_kernel(z, ints_ref, forward_ref, swept_ref, forward_out, swept_out):
    pos = ints_ref[0][0:1]
    for source, target in ((forward_ref, forward_out), (swept_ref, swept_out)):
        for group in range(GROUPS):
            count = min(z.rows, z.block - group * z.rows)
            block = lane_take(source[pl.ds(group * z.rows_pad, z.rows_pad), :], pos)
            target[pl.ds(group * z.rows, count), :] = block[:count]


def call(kernel, outs, inputs, scratch=(), aliases=None, smem_in=(), smem_out=(), hbm_in=(), hbm_out=(), vmem=24):
    whole, smem = pl.BlockSpec(memory_space=pltpu.VMEM), pl.BlockSpec(memory_space=pltpu.SMEM)
    hbm = pl.BlockSpec(memory_space=pltpu.HBM)
    return pl.pallas_call(
        kernel,
        out_shape=outs,
        in_specs=[smem if at in smem_in else hbm if at in hbm_in else whole for at in range(inputs)],
        out_specs=[smem if at in smem_out else hbm if at in hbm_out else whole for at in range(len(outs))],
        scratch_shapes=list(scratch),
        input_output_aliases=aliases or {},
        compiler_params=pltpu.CompilerParams(vmem_limit_bytes=vmem << 20),
    )


def shape(*dims, kind=F32):
    return jax.ShapeDtypeStruct(dims, kind)


def kept(*dims, kind=F32):
    return pltpu.VMEM(dims, kind)


def body(
    start_state,
    right_side,
    block_inverse,
    lifted_flux_jacobian,
    face_weight,
    dep_level,
    face_link,
    send_list,
    recv_list,
):
    curves, slabs = lax.axis_size("curve"), lax.axis_size("slab")
    levels = send_list.shape[0]
    cap = send_list.shape[1] // (curves * slabs)
    slots = levels * cap
    block, n = start_state.shape
    z = Sizes(block, n, levels, slots, curves, slabs)
    own = lax.axis_index("curve").astype(jnp.int32)
    curve = own.reshape(1)

    stride = slabs * cap
    lists = jnp.concatenate([send_list, recv_list], axis=0)
    lists = jnp.pad(lists, ((0, 0), (stride, n)), constant_values=FACES * n)
    lists = lax.dynamic_slice_in_dim(lists, own * stride, n, axis=1)
    slot_level = jnp.asarray(
        np.tile(np.repeat(np.arange(levels), cap), slabs).reshape(1, n), jnp.int32
    )
    pick = jnp.asarray(selector(z), BF16)
    jac = jnp.pad(
        lifted_flux_jacobian, ((0, 0), (0, z.jac_rows - block), (0, z.trace_pad - z.trace))
    )
    jac = jac.transpose(1, 0, 2).reshape(z.jac_rows, z.table_rows)
    rounded = lax.reduce_precision(jac, 8, 7)
    high, low = rounded.astype(BF16), (jac - rounded).astype(BF16)
    jac = jnp.concatenate([high, high, low], axis=1)

    ints, floats, sends, span, start_table, message = call(
        functools.partial(prepare_kernel, z),
        [
            kept(5, SUB, n, kind=jnp.int32),
            kept(7, SUB, n),
            kept(3, SUB, n, kind=jnp.int32),
            shape(2 * levels, kind=jnp.int32),
            kept(z.table_rows, n),
            shape(z.devices, z.tiles, 4, n),
        ],
        8,
        scratch=[pltpu.VMEM((z.state_rows, n), F32)],
        smem_in=(0,),
        smem_out=(3,),
        vmem=60,
    )(curve, start_state, dep_level.reshape(1, n), face_link, face_weight, lists, slot_level, pick)
    message, jac = lax.optimization_barrier((message, jac))

    def exchange(message):
        return lax.all_to_all(message, ("curve", "slab"), 0, 0, tiled=True)

    arrived = exchange(message)
    depth = 6
    chunks, near, weights = call(
        functools.partial(blocks_kernel, z),
        [
            shape(GROUPS, z.rows, z.block_pad, n),
            shape(GROUPS, SUB, n, kind=jnp.int32),
            shape(GROUPS, 3, SUB, n),
        ],
        3,
        scratch=[
            pltpu.VMEM((depth, GROUPS, z.block_pad, n), F32),
            pltpu.VMEM((GROUPS, z.rows, z.block_pad, n), F32),
            pltpu.SemaphoreType.DMA((depth, GROUPS)),
            pltpu.SemaphoreType.DMA((z.rows,)),
        ],
        hbm_in=(0,),
        hbm_out=(0,),
        vmem=48,
    )(block_inverse, ints, floats)
    tables = [
        kept(z.table_rows, n),
        kept(z.table_rows, n),
        kept(z.state_rows, n),
        kept(z.state_rows, n),
    ]
    scratch = [
        pltpu.VMEM((z.table_rows, n), F32),
        pltpu.VMEM((z.rows_pad, n), F32),
        pltpu.VMEM((SUB, n), F32),
    ]
    blocks = [
        pltpu.VMEM((GROUPS, z.rows, z.block_pad, n), F32),
        pltpu.SemaphoreType.DMA((GROUPS,)),
        pltpu.SMEM((GROUPS,), jnp.int32),
    ]
    message, base, right, start_slots, kinds, pending, *state = call(
        functools.partial(first_kernel, z),
        [
            shape(z.devices, z.tiles, 4, n),
            kept(z.block_pad, n),
            kept(z.block_pad, n),
            kept(3, z.trace_pad, n),
            kept(3, n, kind=jnp.int32),
            shape(2 * GROUPS, kind=jnp.int32),
        ]
        + tables,
        14,
        scratch=scratch + blocks,
        smem_in=(0, 1),
        smem_out=(5,),
        hbm_in=(13,),
        vmem=16,
    )(
        curve,
        span,
        right_side,
        slot_level,
        start_table,
        arrived,
        ints,
        floats,
        sends,
        near,
        weights,
        jac,
        pick,
        chunks,
    )

    round_call = call(
        functools.partial(round_kernel, z),
        [shape(z.devices, z.tiles, 4, n), shape(1, kind=jnp.int32), shape(2 * GROUPS, kind=jnp.int32)] + tables,
        20,
        scratch=scratch
        + [
            pltpu.VMEM((z.table_rows, 2 * n), F32),
            pltpu.VMEM((z.block_pad, n), F32),
            pltpu.VMEM((z.block_pad, n), F32),
        ]
        + blocks,
        aliases={15: 3, 16: 4, 17: 5, 18: 6},
        smem_in=(0, 1, 19),
        smem_out=(1, 2),
        hbm_in=(10,),
        vmem=16,
    )

    def one_round(carry):
        _, message, pending, state = carry
        message, more, pending, *state = round_call(
            curve,
            span,
            exchange(message),
            ints,
            floats,
            sends,
            near,
            weights,
            jac,
            pick,
            chunks,
            base,
            right,
            start_slots,
            kinds,
            *state,
            pending,
        )
        return more[0], message, pending, tuple(state)

    start = (jnp.array(1, jnp.int32), message, pending, tuple(state))
    _, _, _, state = lax.while_loop(lambda carry: carry[0] > 0, one_round, start)
    return tuple(
        call(functools.partial(output_kernel, z), [shape(block, n), shape(block, n)], 3)(
            ints, state[2], state[3]
        )
    )


def solution(mesh):
    split = ("curve", "slab")
    return jax.shard_map(
        body,
        mesh=mesh,
        in_specs=(
            P(None, split),
            P(None, split),
            P(None, None, split),
            P(),
            P(None, split),
            P(split),
            P(None, split),
            P(None, split),
            P(None, split),
        ),
        out_specs=(P(None, split), P(None, split)),
        check_vma=False,
    )
```

```python
import functools

import jax
import jax.numpy as jnp
import numpy as np
from jax import lax
from jax.experimental import pallas as pl
from jax.experimental.pallas import tpu as pltpu
from jax.sharding import PartitionSpec as P

VARS = 5
SIDE = 3
FACES = 6
LANES = 128
SUB = 8
GROUPS = 8
F32 = jnp.float32
BF16 = jnp.bfloat16


class Sizes:
    def __init__(self, block, columns, levels, slots, curves, slabs):
        self.block = block
        self.columns = columns
        self.levels = levels
        self.slots = slots
        self.curves = curves
        self.slabs = slabs
        self.devices = curves * slabs
        self.trace = VARS * SIDE * SIDE
        self.width = columns // GROUPS
        self.rows = -(-block // GROUPS)
        self.rows_pad = -(-(self.rows + 1) // SUB) * SUB
        self.state_rows = GROUPS * self.rows_pad
        self.block_pad = -(-block // SUB) * SUB
        self.flag = self.trace
        self.wish = self.trace + 1
        self.trace_pad = -(-(self.trace + 3) // 16) * 16
        self.open = self.trace + 2
        self.cuts = LANES // slots
        self.cut_rows = self.trace_pad // self.cuts
        self.tiles = self.cut_rows // 4
        self.table_rows = FACES * self.trace_pad
        self.jac_rows = -(-self.block_pad // 16) * 16
        assert columns == LANES and slabs * slots == LANES
        assert self.tiles * 4 * self.cuts == self.trace_pad and self.open == self.trace_pad - 1
        assert block < self.block_pad


def face_rows():
    nodes = np.arange(VARS * SIDE**3).reshape(VARS, SIDE, SIDE, SIDE)
    last = SIDE - 1
    sides = [
        nodes[:, 0],
        nodes[:, last],
        nodes[:, :, 0],
        nodes[:, :, last],
        nodes[:, :, :, 0],
        nodes[:, :, :, last],
    ]
    return [side.reshape(-1) for side in sides]


def selector(z):
    pick = np.zeros((z.table_rows, z.state_rows), np.float32)
    for face, rows in enumerate(face_rows()):
        for h, i in enumerate(rows):
            pick[face * z.trace_pad + h, i // z.rows * z.rows_pad + i % z.rows] = 1
        pick[face * z.trace_pad + z.flag, z.rows] = 1
    return np.concatenate([pick, pick], axis=1)


def lane_take(values, index):
    index = jnp.broadcast_to(index, values.shape)
    return jnp.take_along_axis(values, index, axis=1, mode="promise_in_bounds")


def lane_iota(rows=SUB):
    return lax.broadcasted_iota(jnp.int32, (rows, LANES), 1)


def halves(values):
    high = values.astype(BF16)
    low = (values - high.astype(F32)).astype(BF16)
    return high, low


def as_column(row):
    return jnp.broadcast_to(row, (LANES, LANES)).T


def dot(a, b):
    return jnp.dot(a, b, preferred_element_type=F32)


def tables_of(state, pick):
    high, low = halves(state)
    return dot(pick, jnp.concatenate([high, low], axis=0))


def fluxes(jac, traces):
    high, low = halves(traces)
    return dot(jac, jnp.concatenate([high, low, high], axis=0))


def pack(z, message, group, curve, out_ref):
    lanes = lane_iota(z.cut_rows)
    target = curve + group - 1

    @pl.when((target >= 0) & (target < z.curves))
    def _():
        parts = [message[cut * z.cut_rows : (cut + 1) * z.cut_rows] for cut in range(z.cuts)]
        for slab in range(z.slabs):
            block = parts[0]
            for cut in range(z.cuts):
                shift = (cut - slab) * z.slots % LANES
                part = pltpu.roll(parts[cut], shift, 1) if shift else parts[cut]
                block = jnp.where(lanes // z.slots == cut, part, block)
            for tile in range(z.tiles):
                out_ref[target * z.slabs + slab, tile] = block[tile * 4 : tile * 4 + 4]


def unpack(z, group, curve, in_ref):
    lanes = lane_iota(z.cut_rows)
    source = jnp.clip(curve + group - 1, 0, z.curves - 1)
    blocks = [
        jnp.concatenate([in_ref[source * z.slabs + slab, tile] for tile in range(z.tiles)], axis=0)
        for slab in range(z.slabs)
    ]
    parts = []
    for cut in range(z.cuts):
        part = blocks[0]
        for slab in range(z.slabs):
            shift = (slab - cut) * z.slots % LANES
            block = pltpu.roll(blocks[slab], shift, 1) if shift else blocks[slab]
            part = jnp.where(lanes // z.slots == slab, block, part)
        parts.append(part)
    return jnp.concatenate(parts, axis=0)


def ghost_take(z, slot_traces, where, face):
    index = jnp.maximum(where[face : face + 1], 0)
    lane = jnp.bitwise_and(index, LANES - 1)
    block = index // LANES
    found = jnp.zeros((z.trace_pad, LANES), F32)
    for group in range(3):
        found = jnp.where(block == group, lane_take(slot_traces[group], lane), found)
    return found


def regroup(z, curve, list_ref, level_ref):
    n = z.columns
    cap = z.slots // z.levels
    stride = z.slabs * cap
    width = z.devices * cap
    lane = lane_iota(1)
    source = lane // z.slots * cap + jnp.bitwise_and(lane, cap - 1)
    own_row = lax.broadcasted_iota(jnp.int32, (z.levels, n), 0) == level_ref[...]
    shift = lax.rem(2 * width - (curve - 1) * stride, width)
    lists = pltpu.roll(list_ref[...], shift, 1)[:, :n]
    rows = []
    for group in range(3):
        taken = lane_take(lists, source + group * stride)
        row = jnp.sum(jnp.where(own_row, taken, 0).astype(F32), axis=0, keepdims=True)
        target = curve + group - 1
        rows.append(jnp.where((target >= 0) & (target < z.curves), row, float(FACES * n)))
    rows.append(jnp.full((SUB - 3, n), float(FACES * n), F32))
    return jnp.concatenate(rows, axis=0).astype(jnp.int32)


def prepare_kernel(
    z,
    curve_ref,
    start_ref,
    dep_ref,
    link_ref,
    weight_ref,
    send_ref,
    recv_ref,
    level_ref,
    pick_ref,
    ints_ref,
    floats_ref,
    sends_ref,
    span_ref,
    table_ref,
    message_ref,
    state_ref,
):
    n = z.columns
    lanes = lane_iota()
    dep_row = dep_ref[...]
    dep = jnp.broadcast_to(dep_row, (SUB, n))
    key = (dep_row * n + lane_iota(1)).astype(F32)
    earlier = as_column(key) < jnp.broadcast_to(key, (n, n))
    pos_row = jnp.sum(jnp.where(earlier, 1.0, 0.0), axis=0, keepdims=True)
    here = as_column(pos_row) == lane_iota(n).astype(F32)
    element = lax.broadcasted_iota(jnp.int32, (n, n), 0).astype(F32)
    perm_row = jnp.sum(jnp.where(here, element, 0.0), axis=0, keepdims=True)
    pos = jnp.broadcast_to(pos_row.astype(jnp.int32), (SUB, n))
    perm = jnp.broadcast_to(perm_row.astype(jnp.int32), (SUB, n))
    dep_sorted = lane_take(dep, perm)
    for level in range(z.levels):
        before = jnp.sum(jnp.where(dep_row < level, 1.0, 0.0)).astype(jnp.int32)
        upto = jnp.sum(jnp.where(dep_row <= level, 1.0, 0.0)).astype(jnp.int32)
        span_ref[level] = before // z.width
        span_ref[z.levels + level] = jnp.where(upto > before, (upto + z.width - 1) // z.width, before // z.width)

    link = jnp.concatenate([link_ref[...], jnp.full((SUB - FACES, n), -1, jnp.int32)], axis=0)
    near = jnp.where(link >= 0, lane_take(pos, jnp.maximum(link, 0)), -1)
    near = lane_take(near, perm)
    weight = jnp.concatenate([weight_ref[...], jnp.zeros((SUB - FACES, n), F32)], axis=0)
    weight = lane_take(weight, perm)
    local = near >= 0
    near = jnp.maximum(near, 0)
    dep_near = lane_take(dep_sorted, near)
    zero = jnp.zeros_like(weight)

    send = regroup(z, curve_ref[0], send_ref, level_ref)
    recv = regroup(z, curve_ref[0], recv_ref, level_ref)
    slot_level = jnp.broadcast_to(level_ref[...], (SUB, n))
    rows = []
    slot_id = lax.broadcasted_iota(jnp.int32, (n, n), 0).astype(F32) + 1.0
    columns = [as_column(recv[group : group + 1].astype(F32)) for group in range(3)]
    for face in range(FACES):
        name = (lane_iota(n) + face * n).astype(F32)
        found = jnp.zeros((1, n), F32)
        for group in range(3):
            hit = jnp.where(columns[group] == name, slot_id + float(group * n), 0.0)
            found = jnp.maximum(found, jnp.max(hit, axis=0, keepdims=True))
        rows.append(found)
    rows.append(jnp.zeros((SUB - FACES, n), F32))
    slot = jnp.concatenate(rows, axis=0).astype(jnp.int32) - 1
    slot = lane_take(slot, perm)
    from_far = slot >= 0
    slot = jnp.maximum(slot, 0)
    far_level = lane_take(slot_level, jnp.bitwise_and(slot, n - 1))

    for at, value in enumerate((pos, perm, dep_sorted, near, slot)):
        ints_ref[at] = value
    floats_ref[0] = jnp.where(local & (dep_near < dep_sorted), weight, zero)
    floats_ref[1] = jnp.where(local & (dep_near > dep_sorted), weight, zero)
    floats_ref[2] = jnp.where(local & (dep_near <= dep_sorted), weight, zero)
    floats_ref[3] = jnp.where(local & (dep_near >= dep_sorted), weight, zero)
    floats_ref[4] = jnp.where(from_far & (far_level < dep_sorted), weight, zero)
    floats_ref[5] = jnp.where(from_far, weight, zero)
    floats_ref[6] = jnp.where(from_far & (far_level >= dep_sorted), weight, zero)

    send_element = jnp.bitwise_and(send, n - 1)
    sends_ref[0] = lane_take(pos, send_element)
    sends_ref[1] = send // n
    sends_ref[2] = lane_take(dep, send_element)
    recv_dep = lane_take(dep, jnp.bitwise_and(recv, n - 1))
    wish = jnp.where(slot_level <= recv_dep, 1.0, 0.0)

    state_ref[...] = jnp.zeros_like(state_ref)
    for group in range(GROUPS):
        count = min(z.rows, z.block - group * z.rows)
        state_ref[pl.ds(group * z.rows_pad, count), :] = start_ref[pl.ds(group * z.rows, count), :]
    state_ref[pl.ds(z.rows, 1), :] = jnp.ones((1, n), F32)
    state = lane_take(state_ref[...], perm[0:1])
    table = tables_of(state, pick_ref[...])
    table_ref[...] = table
    message_ref[...] = jnp.zeros_like(message_ref)
    row_id = lax.broadcasted_iota(jnp.int32, (z.trace_pad, n), 0)
    for group in range(3):
        where = sends_ref[0][group : group + 1]
        side = sends_ref[1][group : group + 1]
        message = jnp.zeros((z.trace_pad, n), F32)
        for face in range(FACES):
            piece = table[face * z.trace_pad : (face + 1) * z.trace_pad]
            message = jnp.where(side == face, lane_take(piece, where), message)
        message = jnp.where(row_id == z.wish, wish[group : group + 1], message)
        pack(z, message, group, curve_ref[0], message_ref)


def block_copies(z, ii, inverse_ref, buffer_ref, sems):
    slot = lax.rem(ii, buffer_ref.shape[0])
    for group in range(GROUPS):
        i = jnp.minimum(group * z.rows + ii, z.block - 1)
        yield pltpu.make_async_copy(
            inverse_ref.at[i], buffer_ref.at[slot, group, pl.ds(0, z.block)], sems.at[slot, group]
        )


def chunk_tables(z, ints_ref, floats_ref, near_ref, weights_ref):
    for chunk in range(GROUPS):
        own = chunk * z.width + jnp.bitwise_and(lane_iota(), z.width - 1)
        near_ref[chunk] = lane_take(ints_ref[3], own)
        for at in range(3):
            weights_ref[chunk, at] = lane_take(floats_ref[at], own)


def chunk_copy(ii, chunks_ref, out_ref, sems):
    return pltpu.make_async_copy(chunks_ref.at[:, ii], out_ref.at[:, ii], sems.at[ii])


def arrange_blocks(z, inverse_ref, ints_ref, chunks_ref, out_ref, buffer_ref, sems, out_sems):
    n = z.columns
    perm = ints_ref[1]
    depth = buffer_ref.shape[0]
    orders = [pltpu.roll(perm, group * z.width, 1) if group else perm for group in range(GROUPS)]
    bits = [jnp.bitwise_and(lane_iota() // (z.width << b), 1) == 1 for b in range(3)]

    def row(ii, carry):
        @pl.when(ii + depth - 1 < z.rows)
        def _():
            for copy in block_copies(z, ii + depth - 1, inverse_ref, buffer_ref, sems):
                copy.start()

        for copy in block_copies(z, ii, inverse_ref, buffer_ref, sems):
            copy.wait()
        slot = lax.rem(ii, depth)
        for tile in range(z.block_pad // SUB):
            at = pl.ds(tile * SUB, SUB)
            spread = [lane_take(buffer_ref[slot, group, at, :], orders[group]) for group in range(GROUPS)]
            for b in range(3):
                spread = [
                    jnp.where(bits[b], spread[(x + (1 << b)) % GROUPS], spread[x])
                    for x in range(GROUPS)
                ]
            for chunk in range(GROUPS):
                chunks_ref[chunk, ii, at, :] = spread[-chunk % GROUPS]
        chunk_copy(ii, chunks_ref, out_ref, out_sems).start()
        return carry

    lax.fori_loop(0, z.rows, row, 0)


def blocks_kernel(
    z, inverse_ref, ints_ref, floats_ref, chunks_out, near_ref, weights_ref, buffer_ref, chunks_ref, sems, out_sems
):
    depth = buffer_ref.shape[0]
    buffer_ref[:, :, z.block :, :] = jnp.zeros((depth, GROUPS, z.block_pad - z.block, z.columns), F32)
    for first in range(depth - 1):
        for copy in block_copies(z, first, inverse_ref, buffer_ref, sems):
            copy.start()
    chunk_tables(z, ints_ref, floats_ref, near_ref, weights_ref)
    arrange_blocks(z, inverse_ref, ints_ref, chunks_ref, chunks_out, buffer_ref, sems, out_sems)
    for ii in range(z.rows):
        chunk_copy(ii, chunks_ref, chunks_out, out_sems).wait()


def first_base(z, traces, start_table_ref, ints_ref, floats_ref, right_ref, jac_ref, stack_ref, right_sorted_ref, base_ref):
    n = z.columns
    near = ints_ref[3]
    slot = ints_ref[4]
    for face in range(FACES):
        piece = start_table_ref[pl.ds((face ^ 1) * z.trace_pad, z.trace_pad), :]
        value = lane_take(piece, near[face : face + 1]) * floats_ref[3][face : face + 1]
        ghost = ghost_take(z, traces, slot, face) * floats_ref[6][face : face + 1]
        stack_ref[pl.ds(face * z.trace_pad, z.trace_pad), :] = value + ghost
    flow = fluxes(jac_ref[...], stack_ref[...])[: z.block_pad]
    right = jnp.concatenate([right_ref[...], jnp.zeros((z.block_pad - z.block, n), F32)], axis=0)
    right = lane_take(right, ints_ref[1][0:1])
    right_sorted_ref[...] = right
    base_ref[...] = right - flow


def send_kinds(z, traces, sends_ref, level_ref, kinds_ref):
    for group in range(3):
        wish = traces[group][z.wish : z.wish + 1] > 0.5
        side = sends_ref[1][group : group + 1]
        dep = sends_ref[2][group : group + 1]
        level = level_ref[...]
        kind = jnp.where(wish, jnp.where(dep <= level, 1, 3), jnp.where(dep >= level, 2, 1))
        kinds_ref[pl.ds(group, 1), :] = jnp.where(side < FACES, kind, 0)


def later_bases(z, traces, ints_ref, floats_ref, base_ref, right_ref, jac_ref, wide_ref, forward_base_ref, swept_base_ref):
    n = z.columns
    slot = ints_ref[4]
    missing_forward = jnp.zeros((1, n), F32)
    missing_swept = jnp.zeros((1, n), F32)
    for face in range(FACES):
        ghost = ghost_take(z, traces, slot, face)
        forward_weight = floats_ref[4][face : face + 1]
        swept_weight = floats_ref[5][face : face + 1]
        lost = jnp.where(ghost[z.flag : z.flag + 1] > 0.5, 0.0, 1.0)
        missing_forward += jnp.where(forward_weight > 0, lost, 0.0)
        missing_swept += jnp.where(swept_weight > 0, lost, 0.0)
        at = pl.ds(face * z.trace_pad, z.trace_pad)
        wide_ref[at, pl.ds(0, n)] = ghost * forward_weight
        wide_ref[at, pl.ds(n, n)] = ghost * swept_weight
    flow = fluxes(jac_ref[...], wide_ref[...])
    forward_base_ref[...] = base_ref[...] - flow[: z.block_pad, :n]
    swept_base_ref[...] = right_ref[...] - flow[: z.block_pad, n:]
    return missing_forward, missing_swept


def steps(
    z,
    span_ref,
    missing_forward,
    missing_swept,
    ints_ref,
    floats_ref,
    near_ref,
    weights_ref,
    jac_ref,
    pick_ref,
    chunks_ref,
    forward_table_ref,
    swept_table_ref,
    forward_ref,
    swept_ref,
    forward_base,
    swept_base,
    stack_ref,
    part_ref,
    fresh_ref,
    fetch,
    open_ref,
    pending_out,
    pending_in=None,
):
    n = z.columns
    near = ints_ref[3]
    dep = ints_ref[2]
    chunk_of = lane_iota(1) // z.width
    per_sum = GROUPS // 2
    part_ref[...] = jnp.where(
        lax.broadcasted_iota(jnp.int32, (z.rows_pad, n), 0) == z.rows, 1.0, 0.0
    )

    def spread(row):
        return jnp.broadcast_to(row, (SUB, n))

    def absent(flags, weights):
        lost = jnp.where(weights > 0, 1.0 - lane_take(flags, near), 0.0)
        return jnp.sum(lost, axis=0, keepdims=True)

    old_forward = spread(forward_table_ref[pl.ds(z.flag, 1), :])
    old_swept = spread(swept_table_ref[pl.ds(z.flag, 1), :])

    def forward_levels():
        forward = old_forward
        for level in range(z.levels):
            missing = absent(forward, floats_ref[0]) + missing_forward
            forward = jnp.where((dep == level) & spread(missing < 0.5), 1.0, forward)
        return forward

    if pending_in is None:
        forward = forward_levels()
    else:
        unfinished = pending_in[0]
        for chunk in range(1, GROUPS):
            unfinished += pending_in[chunk]
        forward = lax.cond(unfinished > 0, forward_levels, lambda: old_forward)
    swept = old_swept
    settled = absent(forward, floats_ref[2]) + missing_swept
    for level in range(z.levels - 1, -1, -1):
        missing = absent(swept, floats_ref[1]) + settled
        swept = jnp.where((dep == level) & spread(missing < 0.5), 1.0, swept)
    shift = (2 * z.width).bit_length() - 1

    def packed_counts(row):
        found = []
        for half in range(2):
            scale = jnp.zeros((1, n), F32)
            for at_chunk in range(per_sum):
                scale = jnp.where(chunk_of == half * per_sum + at_chunk, float((2 * z.width) ** at_chunk), scale)
            found.append(jnp.sum(row * scale).astype(jnp.int32))
        return found

    def unpacked(pair, chunk):
        bits = jnp.where(chunk >= per_sum, pair[1], pair[0])
        bits = lax.shift_right_logical(bits, lax.rem(chunk, per_sum) * shift)
        return jnp.bitwise_and(bits, 2 * z.width - 1)

    counts = []
    for at, (new, old) in enumerate(((forward, old_forward), (swept, old_swept))):
        fresh = (new - old)[0:1]
        fresh_ref[pl.ds(at, 1), :] = fresh
        counts.append(packed_counts(fresh))
        left = packed_counts(1.0 - new[0:1])
        for chunk in range(GROUPS):
            pending_out[at * GROUPS + chunk] = unpacked(left, jnp.int32(chunk))

    def step(level, chunk, backward):
        @pl.when(open_ref[chunk] == 1)
        def _():
            fetch(chunk).wait()
            open_ref[chunk] = 2

        old = forward_table_ref
        new = swept_table_ref
        base = swept_base if backward else forward_base
        rows = near_ref[chunk]
        old_weight = weights_ref[chunk, 2 if backward else 0]
        new_weight = weights_ref[chunk, 1]
        own = chunk * z.width + jnp.bitwise_and(lane_iota(1), z.width - 1)
        values = []
        for face in range(FACES):
            at = pl.ds((face ^ 1) * z.trace_pad, z.trace_pad)
            row = rows[face : face + 1]
            value = lane_take(old[at, :], row) * old_weight[face : face + 1]
            if backward:
                value += lane_take(new[at, :], row) * new_weight[face : face + 1]
            values.append(value)
        flow = fluxes(jac_ref[...], jnp.concatenate(values, axis=0))[: z.block_pad]
        rest = lane_take(base[...], own) - flow
        for ii in range(z.rows):
            part_ref[pl.ds(ii, 1), :] = jnp.sum(chunks_ref[chunk, ii] * rest, axis=0, keepdims=True)
        part = part_ref[...]
        state = jnp.concatenate(
            [pltpu.roll(part, -g * z.width % n, 1) if g else part for g in range(GROUPS)], axis=0
        )
        table = tables_of(state, pick_ref[...])
        fresh = fresh_ref[pl.ds(1 if backward else 0, 1), :] > 0.5
        keep = fresh & (chunk_of == chunk) & (dep[0:1] == level)
        out_state = swept_ref if backward else forward_ref
        out_table = swept_table_ref if backward else forward_table_ref
        out_state[...] = jnp.where(keep, state, out_state[...])
        out_table[...] = jnp.where(keep, table, out_table[...])

    for backward in (False, True):

        def run(count, carry, backward=backward):
            level = z.levels - 1 - count if backward else count

            def one(chunk, inner):
                @pl.when(unpacked(counts[int(backward)], chunk) > 0)
                def _():
                    step(level, chunk, backward)

                return inner

            return lax.fori_loop(span_ref[level], span_ref[z.levels + level], one, carry)

        lax.fori_loop(0, z.levels, run, 0)

    for chunk in range(GROUPS):

        @pl.when(open_ref[chunk] == 1)
        def _(chunk=chunk):
            fetch(chunk).wait()


def start_fetches(fetch, open_ref, pending_ref):
    for chunk in range(GROUPS):
        wanted = True if pending_ref is None else pending_ref[chunk] > 0
        open_ref[chunk] = 0

        @pl.when(wanted)
        def _(chunk=chunk):
            fetch(chunk).start()
            open_ref[chunk] = 1

    if pending_ref is not None:
        for chunk in reversed(range(GROUPS)):

            @pl.when((pending_ref[GROUPS + chunk] > 0) & (open_ref[chunk] == 0))
            def _(chunk=chunk):
                fetch(chunk).start()
                open_ref[chunk] = 1


def send_messages(z, curve, sends_ref, kinds_ref, forward_table_ref, swept_table_ref, message_ref):
    n = z.columns
    row_id = lax.broadcasted_iota(jnp.int32, (z.trace_pad, n), 0)
    messages = []
    still = jnp.zeros((1, n), F32)
    for group in range(3):
        where = sends_ref[0][group : group + 1]
        side = sends_ref[1][group : group + 1]
        kind = kinds_ref[pl.ds(group, 1), :]
        message = jnp.zeros((z.trace_pad, n), F32)
        for face in range(FACES):
            at = pl.ds(face * z.trace_pad, z.trace_pad)
            first = lane_take(forward_table_ref[at, :], where)
            second = lane_take(swept_table_ref[at, :], where)
            picked = jnp.where(kind == 1, first, second)
            message = jnp.where(side == face, picked, message)
        message = jnp.where((kind == 3) & (row_id == z.flag), 2.0, message)
        unsent = (kind > 0) & (message[z.flag : z.flag + 1] < 0.5)
        still = jnp.maximum(still, jnp.where(unsent, 1.0, 0.0))
        messages.append(message)
    still = jnp.broadcast_to(jnp.max(still, axis=1, keepdims=True), (1, n))
    message_ref[...] = jnp.broadcast_to(still[None, None], message_ref.shape)
    for group in range(3):
        message = jnp.where(row_id == z.open, still, messages[group])
        pack(z, message, group, curve, message_ref)


def first_kernel(
    z,
    curve_ref,
    span_ref,
    right_ref,
    level_ref,
    start_table_ref,
    arrived_ref,
    ints_ref,
    floats_ref,
    sends_ref,
    near_ref,
    weights_ref,
    jac_ref,
    pick_ref,
    chunks_in,
    message_ref,
    base_ref,
    right_sorted_ref,
    start_slots_ref,
    kinds_ref,
    pending_out,
    forward_table_ref,
    swept_table_ref,
    forward_ref,
    swept_ref,
    stack_ref,
    part_ref,
    fresh_ref,
    chunks_ref,
    sems,
    open_ref,
):
    n = z.columns
    curve = curve_ref[0]

    def fetch(chunk):
        return pltpu.make_async_copy(chunks_in.at[chunk], chunks_ref.at[chunk], sems.at[chunk])

    start_fetches(fetch, open_ref, None)
    traces = [unpack(z, group, curve, arrived_ref) for group in range(3)]
    for group in range(3):
        start_slots_ref[group] = traces[group]
    send_kinds(z, traces, sends_ref, level_ref, kinds_ref)
    first_base(
        z, traces, start_table_ref, ints_ref, floats_ref, right_ref, jac_ref, stack_ref, right_sorted_ref, base_ref
    )
    forward_table_ref[...] = jnp.zeros_like(forward_table_ref)
    swept_table_ref[...] = jnp.zeros_like(swept_table_ref)
    forward_ref[...] = jnp.zeros_like(forward_ref)
    swept_ref[...] = jnp.zeros_like(swept_ref)
    missing_forward = jnp.sum(jnp.where(floats_ref[4] > 0, 1.0, 0.0), axis=0, keepdims=True)
    missing_swept = jnp.sum(jnp.where(floats_ref[5] > 0, 1.0, 0.0), axis=0, keepdims=True)
    steps(
        z,
        span_ref,
        missing_forward,
        missing_swept,
        ints_ref,
        floats_ref,
        near_ref,
        weights_ref,
        jac_ref,
        pick_ref,
        chunks_ref,
        forward_table_ref,
        swept_table_ref,
        forward_ref,
        swept_ref,
        base_ref,
        right_sorted_ref,
        stack_ref,
        part_ref,
        fresh_ref,
        fetch,
        open_ref,
        pending_out,
    )
    send_messages(z, curve, sends_ref, kinds_ref, forward_table_ref, swept_table_ref, message_ref)


def round_kernel(
    z,
    curve_ref,
    span_ref,
    arrived_ref,
    ints_ref,
    floats_ref,
    sends_ref,
    near_ref,
    weights_ref,
    jac_ref,
    pick_ref,
    chunks_in,
    base_ref,
    right_ref,
    start_slots_ref,
    kinds_ref,
    forward_table_in,
    swept_table_in,
    forward_in,
    swept_in,
    pending_in,
    message_ref,
    more_ref,
    pending_out,
    forward_table_ref,
    swept_table_ref,
    forward_ref,
    swept_ref,
    stack_ref,
    part_ref,
    fresh_ref,
    wide_ref,
    forward_base_ref,
    swept_base_ref,
    chunks_ref,
    sems,
    open_ref,
):
    n = z.columns
    curve = curve_ref[0]

    def fetch(chunk):
        return pltpu.make_async_copy(chunks_in.at[chunk], chunks_ref.at[chunk], sems.at[chunk])

    start_fetches(fetch, open_ref, pending_in)
    forward_table_ref[...] = forward_table_in[...]
    swept_table_ref[...] = swept_table_in[...]
    forward_ref[...] = forward_in[...]
    swept_ref[...] = swept_in[...]
    row_id = lax.broadcasted_iota(jnp.int32, (z.trace_pad, n), 0)
    still = jnp.max(arrived_ref[:, z.tiles - 1, 3:4, :], axis=0)
    still = jnp.where(lane_iota(1) == n - 1, still, 0.0)
    more = jnp.max(still).astype(jnp.int32)
    more_ref[0] = more
    traces = []
    for group in range(3):
        arrived = unpack(z, group, curve, arrived_ref)
        flag = arrived[z.flag : z.flag + 1]
        traces.append(jnp.where((flag > 1.5) & (row_id != z.flag), start_slots_ref[group], arrived))
    missing_forward, missing_swept = later_bases(
        z, traces, ints_ref, floats_ref, base_ref, right_ref, jac_ref, wide_ref, forward_base_ref, swept_base_ref
    )
    steps(
        z,
        span_ref,
        missing_forward,
        missing_swept,
        ints_ref,
        floats_ref,
        near_ref,
        weights_ref,
        jac_ref,
        pick_ref,
        chunks_ref,
        forward_table_ref,
        swept_table_ref,
        forward_ref,
        swept_ref,
        forward_base_ref,
        swept_base_ref,
        stack_ref,
        part_ref,
        fresh_ref,
        fetch,
        open_ref,
        pending_out,
        pending_in,
    )

    @pl.when(more > 0)
    def _():
        send_messages(z, curve, sends_ref, kinds_ref, forward_table_ref, swept_table_ref, message_ref)


def output_kernel(z, ints_ref, forward_ref, swept_ref, forward_out, swept_out):
    pos = ints_ref[0][0:1]
    for source, target in ((forward_ref, forward_out), (swept_ref, swept_out)):
        for group in range(GROUPS):
            count = min(z.rows, z.block - group * z.rows)
            block = lane_take(source[pl.ds(group * z.rows_pad, z.rows_pad), :], pos)
            target[pl.ds(group * z.rows, count), :] = block[:count]


def call(kernel, outs, inputs, scratch=(), aliases=None, smem_in=(), smem_out=(), hbm_in=(), hbm_out=(), vmem=24):
    whole, smem = pl.BlockSpec(memory_space=pltpu.VMEM), pl.BlockSpec(memory_space=pltpu.SMEM)
    hbm = pl.BlockSpec(memory_space=pltpu.HBM)
    return pl.pallas_call(
        kernel,
        out_shape=outs,
        in_specs=[smem if at in smem_in else hbm if at in hbm_in else whole for at in range(inputs)],
        out_specs=[smem if at in smem_out else hbm if at in hbm_out else whole for at in range(len(outs))],
        scratch_shapes=list(scratch),
        input_output_aliases=aliases or {},
        compiler_params=pltpu.CompilerParams(vmem_limit_bytes=vmem << 20),
    )


def shape(*dims, kind=F32):
    return jax.ShapeDtypeStruct(dims, kind)


def kept(*dims, kind=F32):
    return pltpu.VMEM(dims, kind)


def body(
    start_state,
    right_side,
    block_inverse,
    lifted_flux_jacobian,
    face_weight,
    dep_level,
    face_link,
    send_list,
    recv_list,
):
    curves, slabs = lax.axis_size("curve"), lax.axis_size("slab")
    levels = send_list.shape[0]
    cap = send_list.shape[1] // (curves * slabs)
    slots = levels * cap
    block, n = start_state.shape
    z = Sizes(block, n, levels, slots, curves, slabs)
    own = lax.axis_index("curve").astype(jnp.int32)
    curve = own.reshape(1)

    slot_level = jnp.asarray(
        np.tile(np.repeat(np.arange(levels), cap), slabs).reshape(1, n), jnp.int32
    )
    pick = jnp.asarray(selector(z), BF16)
    jac = jnp.pad(
        lifted_flux_jacobian, ((0, 0), (0, z.jac_rows - block), (0, z.trace_pad - z.trace))
    )
    jac = jac.transpose(1, 0, 2).reshape(z.jac_rows, z.table_rows)
    rounded = lax.reduce_precision(jac, 8, 7)
    high, low = rounded.astype(BF16), (jac - rounded).astype(BF16)
    jac = jnp.concatenate([high, high, low], axis=1)

    ints, floats, sends, span, start_table, message = call(
        functools.partial(prepare_kernel, z),
        [
            kept(5, SUB, n, kind=jnp.int32),
            kept(7, SUB, n),
            kept(3, SUB, n, kind=jnp.int32),
            shape(2 * levels, kind=jnp.int32),
            kept(z.table_rows, n),
            shape(z.devices, z.tiles, 4, n),
        ],
        9,
        scratch=[pltpu.VMEM((z.state_rows, n), F32)],
        smem_in=(0,),
        smem_out=(3,),
        vmem=60,
    )(curve, start_state, dep_level.reshape(1, n), face_link, face_weight, send_list, recv_list, slot_level, pick)
    message, jac = lax.optimization_barrier((message, jac))

    def exchange(message):
        return lax.all_to_all(message, ("curve", "slab"), 0, 0, tiled=True)

    arrived = exchange(message)
    depth = 6
    chunks, near, weights = call(
        functools.partial(blocks_kernel, z),
        [
            shape(GROUPS, z.rows, z.block_pad, n),
            shape(GROUPS, SUB, n, kind=jnp.int32),
            shape(GROUPS, 3, SUB, n),
        ],
        3,
        scratch=[
            pltpu.VMEM((depth, GROUPS, z.block_pad, n), F32),
            pltpu.VMEM((GROUPS, z.rows, z.block_pad, n), F32),
            pltpu.SemaphoreType.DMA((depth, GROUPS)),
            pltpu.SemaphoreType.DMA((z.rows,)),
        ],
        hbm_in=(0,),
        hbm_out=(0,),
        vmem=48,
    )(block_inverse, ints, floats)
    tables = [
        kept(z.table_rows, n),
        kept(z.table_rows, n),
        kept(z.state_rows, n),
        kept(z.state_rows, n),
    ]
    scratch = [
        pltpu.VMEM((z.table_rows, n), F32),
        pltpu.VMEM((z.rows_pad, n), F32),
        pltpu.VMEM((SUB, n), F32),
    ]
    blocks = [
        pltpu.VMEM((GROUPS, z.rows, z.block_pad, n), F32),
        pltpu.SemaphoreType.DMA((GROUPS,)),
        pltpu.SMEM((GROUPS,), jnp.int32),
    ]
    message, base, right, start_slots, kinds, pending, *state = call(
        functools.partial(first_kernel, z),
        [
            shape(z.devices, z.tiles, 4, n),
            kept(z.block_pad, n),
            kept(z.block_pad, n),
            kept(3, z.trace_pad, n),
            kept(3, n, kind=jnp.int32),
            shape(2 * GROUPS, kind=jnp.int32),
        ]
        + tables,
        14,
        scratch=scratch + blocks,
        smem_in=(0, 1),
        smem_out=(5,),
        hbm_in=(13,),
        vmem=16,
    )(
        curve,
        span,
        right_side,
        slot_level,
        start_table,
        arrived,
        ints,
        floats,
        sends,
        near,
        weights,
        jac,
        pick,
        chunks,
    )

    round_call = call(
        functools.partial(round_kernel, z),
        [shape(z.devices, z.tiles, 4, n), shape(1, kind=jnp.int32), shape(2 * GROUPS, kind=jnp.int32)] + tables,
        20,
        scratch=scratch
        + [
            pltpu.VMEM((z.table_rows, 2 * n), F32),
            pltpu.VMEM((z.block_pad, n), F32),
            pltpu.VMEM((z.block_pad, n), F32),
        ]
        + blocks,
        aliases={15: 3, 16: 4, 17: 5, 18: 6},
        smem_in=(0, 1, 19),
        smem_out=(1, 2),
        hbm_in=(10,),
        vmem=16,
    )

    def one_round(carry):
        _, message, pending, state = carry
        message, more, pending, *state = round_call(
            curve,
            span,
            exchange(message),
            ints,
            floats,
            sends,
            near,
            weights,
            jac,
            pick,
            chunks,
            base,
            right,
            start_slots,
            kinds,
            *state,
            pending,
        )
        return more[0], message, pending, tuple(state)

    start = (jnp.array(1, jnp.int32), message, pending, tuple(state))
    _, _, _, state = lax.while_loop(lambda carry: carry[0] > 0, one_round, start)
    return tuple(
        call(functools.partial(output_kernel, z), [shape(block, n), shape(block, n)], 3)(
            ints, state[2], state[3]
        )
    )


def solution(mesh):
    split = ("curve", "slab")
    return jax.shard_map(
        body,
        mesh=mesh,
        in_specs=(
            P(None, split),
            P(None, split),
            P(None, None, split),
            P(),
            P(None, split),
            P(split),
            P(None, split),
            P(None, split),
            P(None, split),
        ),
        out_specs=(P(None, split), P(None, split)),
        check_vma=False,
    )
```

```python
import functools

import jax
import jax.numpy as jnp
import numpy as np
from jax import lax
from jax.experimental import pallas as pl
from jax.experimental.pallas import tpu as pltpu
from jax.sharding import PartitionSpec as P

VARS = 5
SIDE = 3
FACES = 6
LANES = 128
SUB = 8
GROUPS = 8
F32 = jnp.float32
BF16 = jnp.bfloat16


class Sizes:
    def __init__(self, block, columns, levels, slots, curves, slabs):
        self.block = block
        self.columns = columns
        self.levels = levels
        self.slots = slots
        self.curves = curves
        self.slabs = slabs
        self.devices = curves * slabs
        self.trace = VARS * SIDE * SIDE
        self.width = columns // GROUPS
        self.rows = -(-block // GROUPS)
        self.rows_pad = -(-(self.rows + 1) // SUB) * SUB
        self.state_rows = GROUPS * self.rows_pad
        self.block_pad = -(-block // SUB) * SUB
        self.flag = self.trace
        self.wish = self.trace + 1
        self.trace_pad = -(-(self.trace + 3) // 16) * 16
        self.open = self.trace + 2
        self.cuts = LANES // slots
        self.cut_rows = self.trace_pad // self.cuts
        self.tiles = self.cut_rows // 4
        self.table_rows = FACES * self.trace_pad
        self.jac_rows = -(-self.block_pad // 16) * 16
        assert columns == LANES and slabs * slots == LANES
        assert self.tiles * 4 * self.cuts == self.trace_pad and self.open == self.trace_pad - 1
        assert block < self.block_pad


def face_rows():
    nodes = np.arange(VARS * SIDE**3).reshape(VARS, SIDE, SIDE, SIDE)
    last = SIDE - 1
    sides = [
        nodes[:, 0],
        nodes[:, last],
        nodes[:, :, 0],
        nodes[:, :, last],
        nodes[:, :, :, 0],
        nodes[:, :, :, last],
    ]
    return [side.reshape(-1) for side in sides]


def selector(z):
    pick = np.zeros((z.table_rows, z.state_rows), np.float32)
    for face, rows in enumerate(face_rows()):
        for h, i in enumerate(rows):
            pick[face * z.trace_pad + h, i // z.rows * z.rows_pad + i % z.rows] = 1
        pick[face * z.trace_pad + z.flag, z.rows] = 1
    return np.concatenate([pick, pick], axis=1)


def lane_take(values, index):
    index = jnp.broadcast_to(index, values.shape)
    return jnp.take_along_axis(values, index, axis=1, mode="promise_in_bounds")


def lane_iota(rows=SUB):
    return lax.broadcasted_iota(jnp.int32, (rows, LANES), 1)


def halves(values):
    high = values.astype(BF16)
    low = (values - high.astype(F32)).astype(BF16)
    return high, low


def as_column(row):
    return jnp.broadcast_to(row, (LANES, LANES)).T


def dot(a, b):
    return jnp.dot(a, b, preferred_element_type=F32)


def tables_of(state, pick):
    high, low = halves(state)
    return dot(pick, jnp.concatenate([high, low], axis=0))


def fluxes(jac, traces):
    high, low = halves(traces)
    return dot(jac, jnp.concatenate([high, low, high], axis=0))


def pack(z, message, group, curve, out_ref):
    lanes = lane_iota(z.cut_rows)
    target = curve + group - 1

    @pl.when((target >= 0) & (target < z.curves))
    def _():
        parts = [message[cut * z.cut_rows : (cut + 1) * z.cut_rows] for cut in range(z.cuts)]
        for slab in range(z.slabs):
            block = parts[0]
            for cut in range(z.cuts):
                shift = (cut - slab) * z.slots % LANES
                part = pltpu.roll(parts[cut], shift, 1) if shift else parts[cut]
                block = jnp.where(lanes // z.slots == cut, part, block)
            for tile in range(z.tiles):
                out_ref[target * z.slabs + slab, tile] = block[tile * 4 : tile * 4 + 4]


def unpack(z, group, curve, in_ref):
    lanes = lane_iota(z.cut_rows)
    source = jnp.clip(curve + group - 1, 0, z.curves - 1)
    blocks = [
        jnp.concatenate([in_ref[source * z.slabs + slab, tile] for tile in range(z.tiles)], axis=0)
        for slab in range(z.slabs)
    ]
    parts = []
    for cut in range(z.cuts):
        part = blocks[0]
        for slab in range(z.slabs):
            shift = (slab - cut) * z.slots % LANES
            block = pltpu.roll(blocks[slab], shift, 1) if shift else blocks[slab]
            part = jnp.where(lanes // z.slots == slab, block, part)
        parts.append(part)
    return jnp.concatenate(parts, axis=0)


def ghost_take(z, slot_traces, where, face):
    index = jnp.maximum(where[face : face + 1], 0)
    lane = jnp.bitwise_and(index, LANES - 1)
    block = index // LANES
    found = jnp.zeros((z.trace_pad, LANES), F32)
    for group in range(3):
        found = jnp.where(block == group, lane_take(slot_traces[group], lane), found)
    return found


def regroup(z, curve, list_ref, level_ref):
    n = z.columns
    cap = z.slots // z.levels
    stride = z.slabs * cap
    width = z.devices * cap
    lane = lane_iota(1)
    source = lane // z.slots * cap + jnp.bitwise_and(lane, cap - 1)
    own_row = lax.broadcasted_iota(jnp.int32, (z.levels, n), 0) == level_ref[...]
    shift = lax.rem(2 * width - (curve - 1) * stride, width)
    lists = pltpu.roll(list_ref[...], shift, 1)[:, :n]
    rows = []
    for group in range(3):
        taken = lane_take(lists, source + group * stride)
        row = jnp.sum(jnp.where(own_row, taken, 0).astype(F32), axis=0, keepdims=True)
        target = curve + group - 1
        rows.append(jnp.where((target >= 0) & (target < z.curves), row, float(FACES * n)))
    rows.append(jnp.full((SUB - 3, n), float(FACES * n), F32))
    return jnp.concatenate(rows, axis=0).astype(jnp.int32)


def prepare_kernel(
    z,
    curve_ref,
    start_ref,
    dep_ref,
    link_ref,
    weight_ref,
    send_ref,
    recv_ref,
    level_ref,
    pick_ref,
    ints_ref,
    floats_ref,
    sends_ref,
    span_ref,
    table_ref,
    message_ref,
    state_ref,
):
    n = z.columns
    lanes = lane_iota()
    dep_row = dep_ref[...]
    dep = jnp.broadcast_to(dep_row, (SUB, n))
    key = (dep_row * n + lane_iota(1)).astype(F32)
    earlier = as_column(key) < jnp.broadcast_to(key, (n, n))
    pos_row = jnp.sum(jnp.where(earlier, 1.0, 0.0), axis=0, keepdims=True)
    here = as_column(pos_row) == lane_iota(n).astype(F32)
    element = lax.broadcasted_iota(jnp.int32, (n, n), 0).astype(F32)
    perm_row = jnp.sum(jnp.where(here, element, 0.0), axis=0, keepdims=True)
    pos = jnp.broadcast_to(pos_row.astype(jnp.int32), (SUB, n))
    perm = jnp.broadcast_to(perm_row.astype(jnp.int32), (SUB, n))
    dep_sorted = lane_take(dep, perm)
    for level in range(z.levels):
        before = jnp.sum(jnp.where(dep_row < level, 1.0, 0.0)).astype(jnp.int32)
        upto = jnp.sum(jnp.where(dep_row <= level, 1.0, 0.0)).astype(jnp.int32)
        span_ref[level] = before // z.width
        span_ref[z.levels + level] = jnp.where(upto > before, (upto + z.width - 1) // z.width, before // z.width)

    link = jnp.concatenate([link_ref[...], jnp.full((SUB - FACES, n), -1, jnp.int32)], axis=0)
    near = jnp.where(link >= 0, lane_take(pos, jnp.maximum(link, 0)), -1)
    near = lane_take(near, perm)
    weight = jnp.concatenate([weight_ref[...], jnp.zeros((SUB - FACES, n), F32)], axis=0)
    weight = lane_take(weight, perm)
    local = near >= 0
    near = jnp.maximum(near, 0)
    dep_near = lane_take(dep_sorted, near)
    zero = jnp.zeros_like(weight)

    send = regroup(z, curve_ref[0], send_ref, level_ref)
    recv = regroup(z, curve_ref[0], recv_ref, level_ref)
    slot_level = jnp.broadcast_to(level_ref[...], (SUB, n))
    rows = []
    slot_id = lax.broadcasted_iota(jnp.int32, (n, n), 0).astype(F32) + 1.0
    columns = [as_column(recv[group : group + 1].astype(F32)) for group in range(3)]
    for face in range(FACES):
        name = (lane_iota(n) + face * n).astype(F32)
        found = jnp.zeros((1, n), F32)
        for group in range(3):
            hit = jnp.where(columns[group] == name, slot_id + float(group * n), 0.0)
            found = jnp.maximum(found, jnp.max(hit, axis=0, keepdims=True))
        rows.append(found)
    rows.append(jnp.zeros((SUB - FACES, n), F32))
    slot = jnp.concatenate(rows, axis=0).astype(jnp.int32) - 1
    slot = lane_take(slot, perm)
    from_far = slot >= 0
    slot = jnp.maximum(slot, 0)
    far_level = lane_take(slot_level, jnp.bitwise_and(slot, n - 1))

    for at, value in enumerate((pos, perm, dep_sorted, near, slot)):
        ints_ref[at] = value
    floats_ref[0] = jnp.where(local & (dep_near < dep_sorted), weight, zero)
    floats_ref[1] = jnp.where(local & (dep_near > dep_sorted), weight, zero)
    floats_ref[2] = jnp.where(local & (dep_near <= dep_sorted), weight, zero)
    floats_ref[3] = jnp.where(local & (dep_near >= dep_sorted), weight, zero)
    floats_ref[4] = jnp.where(from_far & (far_level < dep_sorted), weight, zero)
    floats_ref[5] = jnp.where(from_far, weight, zero)
    floats_ref[6] = jnp.where(from_far & (far_level >= dep_sorted), weight, zero)

    send_element = jnp.bitwise_and(send, n - 1)
    sends_ref[0] = lane_take(pos, send_element)
    sends_ref[1] = send // n
    sends_ref[2] = lane_take(dep, send_element)
    recv_dep = lane_take(dep, jnp.bitwise_and(recv, n - 1))
    wish = jnp.where(slot_level <= recv_dep, 1.0, 0.0)

    state_ref[...] = jnp.zeros_like(state_ref)
    for group in range(GROUPS):
        count = min(z.rows, z.block - group * z.rows)
        state_ref[pl.ds(group * z.rows_pad, count), :] = start_ref[pl.ds(group * z.rows, count), :]
    state_ref[pl.ds(z.rows, 1), :] = jnp.ones((1, n), F32)
    state = lane_take(state_ref[...], perm[0:1])
    table = tables_of(state, pick_ref[...])
    table_ref[...] = table
    message_ref[...] = jnp.zeros_like(message_ref)
    row_id = lax.broadcasted_iota(jnp.int32, (z.trace_pad, n), 0)
    for group in range(3):
        where = sends_ref[0][group : group + 1]
        side = sends_ref[1][group : group + 1]
        message = jnp.zeros((z.trace_pad, n), F32)
        for face in range(FACES):
            piece = table[face * z.trace_pad : (face + 1) * z.trace_pad]
            message = jnp.where(side == face, lane_take(piece, where), message)
        message = jnp.where(row_id == z.wish, wish[group : group + 1], message)
        pack(z, message, group, curve_ref[0], message_ref)


def block_copies(z, ii, inverse_ref, buffer_ref, sems):
    slot = lax.rem(ii, buffer_ref.shape[0])
    for group in range(GROUPS):
        i = jnp.minimum(group * z.rows + ii, z.block - 1)
        yield pltpu.make_async_copy(
            inverse_ref.at[i], buffer_ref.at[slot, group, pl.ds(0, z.block)], sems.at[slot, group]
        )


def chunk_tables(z, ints_ref, floats_ref, near_ref, weights_ref):
    for chunk in range(GROUPS):
        own = chunk * z.width + jnp.bitwise_and(lane_iota(), z.width - 1)
        near_ref[chunk] = lane_take(ints_ref[3], own)
        for at in range(3):
            weights_ref[chunk, at] = lane_take(floats_ref[at], own)


def chunk_copy(ii, chunks_ref, out_ref, sems):
    return pltpu.make_async_copy(chunks_ref.at[:, ii], out_ref.at[:, ii], sems.at[ii])


def arrange_blocks(z, inverse_ref, ints_ref, chunks_ref, out_ref, buffer_ref, sems, out_sems):
    n = z.columns
    perm = ints_ref[1]
    depth = buffer_ref.shape[0]
    orders = [pltpu.roll(perm, group * z.width, 1) if group else perm for group in range(GROUPS)]
    bits = [jnp.bitwise_and(lane_iota() // (z.width << b), 1) == 1 for b in range(3)]

    def row(ii, carry):
        @pl.when(ii + depth - 1 < z.rows)
        def _():
            for copy in block_copies(z, ii + depth - 1, inverse_ref, buffer_ref, sems):
                copy.start()

        for copy in block_copies(z, ii, inverse_ref, buffer_ref, sems):
            copy.wait()
        slot = lax.rem(ii, depth)
        for tile in range(z.block_pad // SUB):
            at = pl.ds(tile * SUB, SUB)
            spread = [lane_take(buffer_ref[slot, group, at, :], orders[group]) for group in range(GROUPS)]
            for b in range(3):
                spread = [
                    jnp.where(bits[b], spread[(x + (1 << b)) % GROUPS], spread[x])
                    for x in range(GROUPS)
                ]
            for chunk in range(GROUPS):
                chunks_ref[chunk, ii, at, :] = spread[-chunk % GROUPS]
        chunk_copy(ii, chunks_ref, out_ref, out_sems).start()
        return carry

    lax.fori_loop(0, z.rows, row, 0)


def blocks_kernel(
    z, inverse_ref, ints_ref, floats_ref, chunks_out, near_ref, weights_ref, buffer_ref, chunks_ref, sems, out_sems
):
    depth = buffer_ref.shape[0]
    buffer_ref[:, :, z.block :, :] = jnp.zeros((depth, GROUPS, z.block_pad - z.block, z.columns), F32)
    for first in range(depth - 1):
        for copy in block_copies(z, first, inverse_ref, buffer_ref, sems):
            copy.start()
    chunk_tables(z, ints_ref, floats_ref, near_ref, weights_ref)
    arrange_blocks(z, inverse_ref, ints_ref, chunks_ref, chunks_out, buffer_ref, sems, out_sems)
    for ii in range(z.rows):
        chunk_copy(ii, chunks_ref, chunks_out, out_sems).wait()


def first_base(z, traces, start_table_ref, ints_ref, floats_ref, right_ref, jac_ref, stack_ref, right_sorted_ref, base_ref):
    n = z.columns
    near = ints_ref[3]
    slot = ints_ref[4]
    for face in range(FACES):
        piece = start_table_ref[pl.ds((face ^ 1) * z.trace_pad, z.trace_pad), :]
        value = lane_take(piece, near[face : face + 1]) * floats_ref[3][face : face + 1]
        ghost = ghost_take(z, traces, slot, face) * floats_ref[6][face : face + 1]
        stack_ref[pl.ds(face * z.trace_pad, z.trace_pad), :] = value + ghost
    flow = fluxes(jac_ref[...], stack_ref[...])[: z.block_pad]
    right = jnp.concatenate([right_ref[...], jnp.zeros((z.block_pad - z.block, n), F32)], axis=0)
    right = lane_take(right, ints_ref[1][0:1])
    right_sorted_ref[...] = right
    base_ref[...] = right - flow


def send_kinds(z, traces, sends_ref, level_ref, kinds_ref):
    for group in range(3):
        wish = traces[group][z.wish : z.wish + 1] > 0.5
        side = sends_ref[1][group : group + 1]
        dep = sends_ref[2][group : group + 1]
        level = level_ref[...]
        kind = jnp.where(wish, jnp.where(dep <= level, 1, 3), jnp.where(dep >= level, 2, 1))
        kinds_ref[pl.ds(group, 1), :] = jnp.where(side < FACES, kind, 0)


def urgent_rows(z, sends_ref, kinds_ref, urgent_ref):
    n = z.columns
    place = lane_iota(n).astype(F32)
    urgent_ref[...] = jnp.zeros_like(urgent_ref)
    for at in range(2):
        found = jnp.zeros((1, n), F32)
        for group in range(3):
            kind = kinds_ref[pl.ds(group, 1), :]
            where = jnp.where(kind == at + 1, sends_ref[0][group : group + 1], -1).astype(F32)
            hit = jnp.where(as_column(where) == place, 1.0, 0.0)
            found = jnp.maximum(found, jnp.max(hit, axis=0, keepdims=True))
        urgent_ref[pl.ds(at, 1), :] = found


def later_bases(z, traces, ints_ref, floats_ref, base_ref, right_ref, jac_ref, wide_ref, forward_base_ref, swept_base_ref):
    n = z.columns
    slot = ints_ref[4]
    missing_forward = jnp.zeros((1, n), F32)
    missing_swept = jnp.zeros((1, n), F32)
    for face in range(FACES):
        ghost = ghost_take(z, traces, slot, face)
        forward_weight = floats_ref[4][face : face + 1]
        swept_weight = floats_ref[5][face : face + 1]
        lost = jnp.where(ghost[z.flag : z.flag + 1] > 0.5, 0.0, 1.0)
        missing_forward += jnp.where(forward_weight > 0, lost, 0.0)
        missing_swept += jnp.where(swept_weight > 0, lost, 0.0)
        at = pl.ds(face * z.trace_pad, z.trace_pad)
        wide_ref[at, pl.ds(0, n)] = ghost * forward_weight
        wide_ref[at, pl.ds(n, n)] = ghost * swept_weight
    flow = fluxes(jac_ref[...], wide_ref[...])
    forward_base_ref[...] = base_ref[...] - flow[: z.block_pad, :n]
    swept_base_ref[...] = right_ref[...] - flow[: z.block_pad, n:]
    forward_base_ref[pl.ds(z.block, 1), :] = missing_forward
    swept_base_ref[pl.ds(z.block, 1), :] = missing_swept
    return missing_forward, missing_swept


def steps(
    z,
    span_ref,
    missing_forward,
    missing_swept,
    ints_ref,
    floats_ref,
    near_ref,
    weights_ref,
    jac_ref,
    pick_ref,
    chunks_ref,
    forward_table_ref,
    swept_table_ref,
    forward_ref,
    swept_ref,
    forward_base,
    swept_base,
    stack_ref,
    part_ref,
    fresh_ref,
    fetch,
    open_ref,
    pending_out,
    pending_in=None,
    urgent_ref=None,
    last=None,
):
    n = z.columns
    near = ints_ref[3]
    dep = ints_ref[2]
    chunk_of = lane_iota(1) // z.width
    per_sum = GROUPS // 2
    part_ref[...] = jnp.where(
        lax.broadcasted_iota(jnp.int32, (z.rows_pad, n), 0) == z.rows, 1.0, 0.0
    )

    def spread(row):
        return jnp.broadcast_to(row, (SUB, n))

    def absent(flags, weights):
        lost = jnp.where(weights > 0, 1.0 - lane_take(flags, near), 0.0)
        return jnp.sum(lost, axis=0, keepdims=True)

    old_forward = spread(forward_table_ref[pl.ds(z.flag, 1), :])
    old_swept = spread(swept_table_ref[pl.ds(z.flag, 1), :])

    def forward_levels():
        forward = old_forward
        for level in range(z.levels):
            missing = absent(forward, floats_ref[0]) + missing_forward
            forward = jnp.where((dep == level) & spread(missing < 0.5), 1.0, forward)
        return forward

    if pending_in is None:
        forward = forward_levels()
    else:
        unfinished = pending_in[0]
        for chunk in range(1, GROUPS):
            unfinished += pending_in[chunk]
        forward = lax.cond(unfinished > 0, forward_levels, lambda: old_forward)
    swept = old_swept
    settled = absent(forward, floats_ref[2]) + missing_swept
    for level in range(z.levels - 1, -1, -1):
        missing = absent(swept, floats_ref[1]) + settled
        swept = jnp.where((dep == level) & spread(missing < 0.5), 1.0, swept)
    shift = (2 * z.width).bit_length() - 1

    def packed_counts(row):
        found = []
        for half in range(2):
            scale = jnp.zeros((1, n), F32)
            for at_chunk in range(per_sum):
                scale = jnp.where(chunk_of == half * per_sum + at_chunk, float((2 * z.width) ** at_chunk), scale)
            found.append(jnp.sum(row * scale).astype(jnp.int32))
        return found

    def unpacked(pair, chunk):
        bits = jnp.where(chunk >= per_sum, pair[1], pair[0])
        bits = lax.shift_right_logical(bits, lax.rem(chunk, per_sum) * shift)
        return jnp.bitwise_and(bits, 2 * z.width - 1)

    counts = []
    urgent = []
    for at, (new, old) in enumerate(((forward, old_forward), (swept, old_swept))):
        fresh = (new - old)[0:1]
        fresh_ref[pl.ds(at, 1), :] = fresh
        counts.append(packed_counts(fresh))
        left = packed_counts(1.0 - old[0:1])
        if urgent_ref is not None:
            urgent.append(packed_counts(fresh * urgent_ref[pl.ds(at, 1), :]))
        for chunk in range(GROUPS):
            pending_out[at * GROUPS + chunk] = unpacked(left, jnp.int32(chunk))

    limits = [jnp.int32(GROUPS - 1), jnp.int32(0)]
    if urgent:
        highest, lowest = jnp.int32(-1), jnp.int32(GROUPS)
        for chunk in range(GROUPS):
            highest = jnp.where(unpacked(urgent[0], jnp.int32(chunk)) > 0, chunk, highest)
        for chunk in reversed(range(GROUPS)):
            lowest = jnp.where(unpacked(urgent[1], jnp.int32(chunk)) > 0, chunk, lowest)
        highest = jnp.where(lowest < GROUPS, GROUPS - 1, highest)
        limits = [jnp.where(last, GROUPS - 1, highest), jnp.where(last, 0, lowest)]

    def step(level, chunk, backward):
        @pl.when(open_ref[chunk] == 1)
        def _():
            fetch(chunk).wait()
            open_ref[chunk] = 2

        old = forward_table_ref
        new = swept_table_ref
        base = swept_base if backward else forward_base
        rows = near_ref[chunk]
        old_weight = weights_ref[chunk, 2 if backward else 0]
        new_weight = weights_ref[chunk, 1]
        own = chunk * z.width + jnp.bitwise_and(lane_iota(1), z.width - 1)
        values = []
        for face in range(FACES):
            at = pl.ds((face ^ 1) * z.trace_pad, z.trace_pad)
            row = rows[face : face + 1]
            value = lane_take(old[at, :], row) * old_weight[face : face + 1]
            if backward:
                value += lane_take(new[at, :], row) * new_weight[face : face + 1]
            values.append(value)
        flow = fluxes(jac_ref[...], jnp.concatenate(values, axis=0))[: z.block_pad]
        rest = lane_take(base[...], own) - flow
        for ii in range(z.rows):
            part_ref[pl.ds(ii, 1), :] = jnp.sum(chunks_ref[chunk, ii] * rest, axis=0, keepdims=True)
        part = part_ref[...]
        state = jnp.concatenate(
            [pltpu.roll(part, -g * z.width % n, 1) if g else part for g in range(GROUPS)], axis=0
        )
        table = tables_of(state, pick_ref[...])
        fresh = fresh_ref[pl.ds(1 if backward else 0, 1), :] > 0.5
        keep = fresh & (chunk_of == chunk) & (dep[0:1] == level)
        out_state = swept_ref if backward else forward_ref
        out_table = swept_table_ref if backward else forward_table_ref
        out_state[...] = jnp.where(keep, state, out_state[...])
        out_table[...] = jnp.where(keep, table, out_table[...])

    for backward in (False, True):

        def run(count, carry, backward=backward):
            level = z.levels - 1 - count if backward else count

            def one(chunk, inner):
                now = chunk >= limits[1] if backward else chunk <= limits[0]

                @pl.when(now & (unpacked(counts[int(backward)], chunk) > 0))
                def _():
                    step(level, chunk, backward)

                return inner

            return lax.fori_loop(span_ref[level], span_ref[z.levels + level], one, carry)

        lax.fori_loop(0, z.levels, run, 0)

    for chunk in range(GROUPS):

        @pl.when(open_ref[chunk] == 1)
        def _(chunk=chunk):
            fetch(chunk).wait()


def start_fetches(fetch, open_ref, pending_ref):
    for chunk in range(GROUPS):
        wanted = True if pending_ref is None else pending_ref[chunk] > 0
        open_ref[chunk] = 0

        @pl.when(wanted)
        def _(chunk=chunk):
            fetch(chunk).start()
            open_ref[chunk] = 1

    if pending_ref is not None:
        for chunk in reversed(range(GROUPS)):

            @pl.when((pending_ref[GROUPS + chunk] > 0) & (open_ref[chunk] == 0))
            def _(chunk=chunk):
                fetch(chunk).start()
                open_ref[chunk] = 1


def send_messages(z, curve, sends_ref, kinds_ref, forward_table_ref, swept_table_ref, message_ref):
    n = z.columns
    row_id = lax.broadcasted_iota(jnp.int32, (z.trace_pad, n), 0)
    messages = []
    still = jnp.zeros((1, n), F32)
    for group in range(3):
        where = sends_ref[0][group : group + 1]
        side = sends_ref[1][group : group + 1]
        kind = kinds_ref[pl.ds(group, 1), :]
        message = jnp.zeros((z.trace_pad, n), F32)
        for face in range(FACES):
            at = pl.ds(face * z.trace_pad, z.trace_pad)
            first = lane_take(forward_table_ref[at, :], where)
            second = lane_take(swept_table_ref[at, :], where)
            picked = jnp.where(kind == 1, first, second)
            message = jnp.where(side == face, picked, message)
        message = jnp.where((kind == 3) & (row_id == z.flag), 2.0, message)
        unsent = (kind > 0) & (message[z.flag : z.flag + 1] < 0.5)
        still = jnp.maximum(still, jnp.where(unsent, 1.0, 0.0))
        messages.append(message)
    still = jnp.broadcast_to(jnp.max(still, axis=1, keepdims=True), (1, n))
    message_ref[...] = jnp.broadcast_to(still[None, None], message_ref.shape)
    for group in range(3):
        message = jnp.where(row_id == z.open, still, messages[group])
        pack(z, message, group, curve, message_ref)


def first_kernel(
    z,
    curve_ref,
    span_ref,
    right_ref,
    level_ref,
    start_table_ref,
    arrived_ref,
    ints_ref,
    floats_ref,
    sends_ref,
    near_ref,
    weights_ref,
    jac_ref,
    pick_ref,
    chunks_in,
    message_ref,
    base_ref,
    right_sorted_ref,
    start_slots_ref,
    kinds_ref,
    urgent_ref,
    pending_out,
    forward_table_ref,
    swept_table_ref,
    forward_ref,
    swept_ref,
    stack_ref,
    part_ref,
    fresh_ref,
    chunks_ref,
    sems,
    open_ref,
):
    n = z.columns
    curve = curve_ref[0]

    def fetch(chunk):
        return pltpu.make_async_copy(chunks_in.at[chunk], chunks_ref.at[chunk], sems.at[chunk])

    start_fetches(fetch, open_ref, None)
    traces = [unpack(z, group, curve, arrived_ref) for group in range(3)]
    for group in range(3):
        start_slots_ref[group] = traces[group]
    send_kinds(z, traces, sends_ref, level_ref, kinds_ref)
    urgent_rows(z, sends_ref, kinds_ref, urgent_ref)
    first_base(
        z, traces, start_table_ref, ints_ref, floats_ref, right_ref, jac_ref, stack_ref, right_sorted_ref, base_ref
    )
    forward_table_ref[...] = jnp.zeros_like(forward_table_ref)
    swept_table_ref[...] = jnp.zeros_like(swept_table_ref)
    forward_ref[...] = jnp.zeros_like(forward_ref)
    swept_ref[...] = jnp.zeros_like(swept_ref)
    missing_forward = jnp.sum(jnp.where(floats_ref[4] > 0, 1.0, 0.0), axis=0, keepdims=True)
    missing_swept = jnp.sum(jnp.where(floats_ref[5] > 0, 1.0, 0.0), axis=0, keepdims=True)
    base_ref[pl.ds(z.block, 1), :] = missing_forward
    right_sorted_ref[pl.ds(z.block, 1), :] = missing_swept
    steps(
        z,
        span_ref,
        missing_forward,
        missing_swept,
        ints_ref,
        floats_ref,
        near_ref,
        weights_ref,
        jac_ref,
        pick_ref,
        chunks_ref,
        forward_table_ref,
        swept_table_ref,
        forward_ref,
        swept_ref,
        base_ref,
        right_sorted_ref,
        stack_ref,
        part_ref,
        fresh_ref,
        fetch,
        open_ref,
        pending_out,
        None,
        urgent_ref,
        False,
    )
    send_messages(z, curve, sends_ref, kinds_ref, forward_table_ref, swept_table_ref, message_ref)


def round_kernel(
    z,
    curve_ref,
    span_ref,
    arrived_ref,
    ints_ref,
    floats_ref,
    sends_ref,
    near_ref,
    weights_ref,
    jac_ref,
    pick_ref,
    chunks_in,
    base_ref,
    right_ref,
    start_slots_ref,
    kinds_ref,
    forward_table_in,
    swept_table_in,
    forward_in,
    swept_in,
    pending_in,
    urgent_ref,
    message_ref,
    more_ref,
    pending_out,
    forward_base_ref,
    swept_base_ref,
    forward_table_ref,
    swept_table_ref,
    forward_ref,
    swept_ref,
    stack_ref,
    part_ref,
    fresh_ref,
    wide_ref,
    chunks_ref,
    sems,
    open_ref,
):
    n = z.columns
    curve = curve_ref[0]

    def fetch(chunk):
        return pltpu.make_async_copy(chunks_in.at[chunk], chunks_ref.at[chunk], sems.at[chunk])

    start_fetches(fetch, open_ref, pending_in)
    forward_table_ref[...] = forward_table_in[...]
    swept_table_ref[...] = swept_table_in[...]
    forward_ref[...] = forward_in[...]
    swept_ref[...] = swept_in[...]
    row_id = lax.broadcasted_iota(jnp.int32, (z.trace_pad, n), 0)
    still = jnp.max(arrived_ref[:, z.tiles - 1, 3:4, :], axis=0)
    still = jnp.where(lane_iota(1) == n - 1, still, 0.0)
    more = jnp.max(still).astype(jnp.int32)
    more_ref[0] = more
    traces = []
    for group in range(3):
        arrived = unpack(z, group, curve, arrived_ref)
        flag = arrived[z.flag : z.flag + 1]
        traces.append(jnp.where((flag > 1.5) & (row_id != z.flag), start_slots_ref[group], arrived))
    missing_forward, missing_swept = later_bases(
        z, traces, ints_ref, floats_ref, base_ref, right_ref, jac_ref, wide_ref, forward_base_ref, swept_base_ref
    )
    steps(
        z,
        span_ref,
        missing_forward,
        missing_swept,
        ints_ref,
        floats_ref,
        near_ref,
        weights_ref,
        jac_ref,
        pick_ref,
        chunks_ref,
        forward_table_ref,
        swept_table_ref,
        forward_ref,
        swept_ref,
        forward_base_ref,
        swept_base_ref,
        stack_ref,
        part_ref,
        fresh_ref,
        fetch,
        open_ref,
        pending_out,
        pending_in,
        urgent_ref,
        more == 0,
    )

    @pl.when(more > 0)
    def _():
        send_messages(z, curve, sends_ref, kinds_ref, forward_table_ref, swept_table_ref, message_ref)


def rest_kernel(
    z,
    span_ref,
    ints_ref,
    floats_ref,
    near_ref,
    weights_ref,
    jac_ref,
    pick_ref,
    chunks_in,
    forward_base_ref,
    swept_base_ref,
    forward_table_in,
    swept_table_in,
    forward_in,
    swept_in,
    pending_in,
    forward_table_ref,
    swept_table_ref,
    forward_ref,
    swept_ref,
    stack_ref,
    part_ref,
    fresh_ref,
    chunks_ref,
    sems,
    open_ref,
    pending_out,
):
    def fetch(chunk):
        return pltpu.make_async_copy(chunks_in.at[chunk], chunks_ref.at[chunk], sems.at[chunk])

    start_fetches(fetch, open_ref, pending_in)
    forward_table_ref[...] = forward_table_in[...]
    swept_table_ref[...] = swept_table_in[...]
    forward_ref[...] = forward_in[...]
    swept_ref[...] = swept_in[...]
    steps(
        z,
        span_ref,
        forward_base_ref[pl.ds(z.block, 1), :],
        swept_base_ref[pl.ds(z.block, 1), :],
        ints_ref,
        floats_ref,
        near_ref,
        weights_ref,
        jac_ref,
        pick_ref,
        chunks_ref,
        forward_table_ref,
        swept_table_ref,
        forward_ref,
        swept_ref,
        forward_base_ref,
        swept_base_ref,
        stack_ref,
        part_ref,
        fresh_ref,
        fetch,
        open_ref,
        pending_out,
        pending_in,
    )


def output_kernel(z, ints_ref, forward_ref, swept_ref, forward_out, swept_out):
    pos = ints_ref[0][0:1]
    for source, target in ((forward_ref, forward_out), (swept_ref, swept_out)):
        for group in range(GROUPS):
            count = min(z.rows, z.block - group * z.rows)
            block = lane_take(source[pl.ds(group * z.rows_pad, z.rows_pad), :], pos)
            target[pl.ds(group * z.rows, count), :] = block[:count]


def call(kernel, outs, inputs, scratch=(), aliases=None, smem_in=(), smem_out=(), hbm_in=(), hbm_out=(), vmem=24):
    whole, smem = pl.BlockSpec(memory_space=pltpu.VMEM), pl.BlockSpec(memory_space=pltpu.SMEM)
    hbm = pl.BlockSpec(memory_space=pltpu.HBM)
    return pl.pallas_call(
        kernel,
        out_shape=outs,
        in_specs=[smem if at in smem_in else hbm if at in hbm_in else whole for at in range(inputs)],
        out_specs=[smem if at in smem_out else hbm if at in hbm_out else whole for at in range(len(outs))],
        scratch_shapes=list(scratch),
        input_output_aliases=aliases or {},
        compiler_params=pltpu.CompilerParams(vmem_limit_bytes=vmem << 20),
    )


def shape(*dims, kind=F32):
    return jax.ShapeDtypeStruct(dims, kind)


def kept(*dims, kind=F32):
    return pltpu.VMEM(dims, kind)


def body(
    start_state,
    right_side,
    block_inverse,
    lifted_flux_jacobian,
    face_weight,
    dep_level,
    face_link,
    send_list,
    recv_list,
):
    curves, slabs = lax.axis_size("curve"), lax.axis_size("slab")
    levels = send_list.shape[0]
    cap = send_list.shape[1] // (curves * slabs)
    slots = levels * cap
    block, n = start_state.shape
    z = Sizes(block, n, levels, slots, curves, slabs)
    own = lax.axis_index("curve").astype(jnp.int32)
    curve = own.reshape(1)

    slot_level = jnp.asarray(
        np.tile(np.repeat(np.arange(levels), cap), slabs).reshape(1, n), jnp.int32
    )
    pick = jnp.asarray(selector(z), BF16)
    jac = jnp.pad(
        lifted_flux_jacobian, ((0, 0), (0, z.jac_rows - block), (0, z.trace_pad - z.trace))
    )
    jac = jac.transpose(1, 0, 2).reshape(z.jac_rows, z.table_rows)
    rounded = lax.reduce_precision(jac, 8, 7)
    high, low = rounded.astype(BF16), (jac - rounded).astype(BF16)
    jac = jnp.concatenate([high, high, low], axis=1)

    ints, floats, sends, span, start_table, message = call(
        functools.partial(prepare_kernel, z),
        [
            kept(5, SUB, n, kind=jnp.int32),
            kept(7, SUB, n),
            kept(3, SUB, n, kind=jnp.int32),
            shape(2 * levels, kind=jnp.int32),
            kept(z.table_rows, n),
            shape(z.devices, z.tiles, 4, n),
        ],
        9,
        scratch=[pltpu.VMEM((z.state_rows, n), F32)],
        smem_in=(0,),
        smem_out=(3,),
        vmem=60,
    )(curve, start_state, dep_level.reshape(1, n), face_link, face_weight, send_list, recv_list, slot_level, pick)
    message, jac = lax.optimization_barrier((message, jac))

    def exchange(message):
        return lax.all_to_all(message, ("curve", "slab"), 0, 0, tiled=True)

    arrived = exchange(message)
    depth = 6
    chunks, near, weights = call(
        functools.partial(blocks_kernel, z),
        [
            shape(GROUPS, z.rows, z.block_pad, n),
            shape(GROUPS, SUB, n, kind=jnp.int32),
            shape(GROUPS, 3, SUB, n),
        ],
        3,
        scratch=[
            pltpu.VMEM((depth, GROUPS, z.block_pad, n), F32),
            pltpu.VMEM((GROUPS, z.rows, z.block_pad, n), F32),
            pltpu.SemaphoreType.DMA((depth, GROUPS)),
            pltpu.SemaphoreType.DMA((z.rows,)),
        ],
        hbm_in=(0,),
        hbm_out=(0,),
        vmem=48,
    )(block_inverse, ints, floats)
    tables = [
        kept(z.table_rows, n),
        kept(z.table_rows, n),
        kept(z.state_rows, n),
        kept(z.state_rows, n),
    ]
    scratch = [
        pltpu.VMEM((z.table_rows, n), F32),
        pltpu.VMEM((z.rows_pad, n), F32),
        pltpu.VMEM((SUB, n), F32),
    ]
    blocks = [
        pltpu.VMEM((GROUPS, z.rows, z.block_pad, n), F32),
        pltpu.SemaphoreType.DMA((GROUPS,)),
        pltpu.SMEM((GROUPS,), jnp.int32),
    ]
    message, base, right, start_slots, kinds, urgent, pending, *state = call(
        functools.partial(first_kernel, z),
        [
            shape(z.devices, z.tiles, 4, n),
            kept(z.block_pad, n),
            kept(z.block_pad, n),
            kept(3, z.trace_pad, n),
            kept(3, n, kind=jnp.int32),
            kept(SUB, n),
            shape(2 * GROUPS, kind=jnp.int32),
        ]
        + tables,
        14,
        scratch=scratch + blocks,
        smem_in=(0, 1),
        smem_out=(6,),
        hbm_in=(13,),
        vmem=16,
    )(
        curve,
        span,
        right_side,
        slot_level,
        start_table,
        arrived,
        ints,
        floats,
        sends,
        near,
        weights,
        jac,
        pick,
        chunks,
    )

    round_call = call(
        functools.partial(round_kernel, z),
        [
            shape(z.devices, z.tiles, 4, n),
            shape(1, kind=jnp.int32),
            shape(2 * GROUPS, kind=jnp.int32),
            kept(z.block_pad, n),
            kept(z.block_pad, n),
        ]
        + tables,
        21,
        scratch=scratch + [pltpu.VMEM((z.table_rows, 2 * n), F32)] + blocks,
        aliases={15: 5, 16: 6, 17: 7, 18: 8},
        smem_in=(0, 1, 19),
        smem_out=(1, 2),
        hbm_in=(10,),
        vmem=16,
    )

    rest_call = call(
        functools.partial(rest_kernel, z),
        tables,
        15,
        scratch=scratch + blocks + [pltpu.SMEM((2 * GROUPS,), jnp.int32)],
        aliases={10: 0, 11: 1, 12: 2, 13: 3},
        smem_in=(0, 14),
        hbm_in=(7,),
        vmem=16,
    )

    def one_round(carry):
        _, message, pending, bases, state = carry
        arrived = exchange(message)
        state = rest_call(span, ints, floats, near, weights, jac, pick, chunks, *bases, *state, pending)
        message, more, pending, *rest = round_call(
            curve,
            span,
            arrived,
            ints,
            floats,
            sends,
            near,
            weights,
            jac,
            pick,
            chunks,
            base,
            right,
            start_slots,
            kinds,
            *state,
            pending,
            urgent,
        )
        return more[0], message, pending, tuple(rest[:2]), tuple(rest[2:])

    start = (jnp.array(1, jnp.int32), message, pending, (base, right), tuple(state))
    *_, state = lax.while_loop(lambda carry: carry[0] > 0, one_round, start)
    return tuple(
        call(functools.partial(output_kernel, z), [shape(block, n), shape(block, n)], 3)(
            ints, state[2], state[3]
        )
    )


def solution(mesh):
    split = ("curve", "slab")
    return jax.shard_map(
        body,
        mesh=mesh,
        in_specs=(
            P(None, split),
            P(None, split),
            P(None, None, split),
            P(),
            P(None, split),
            P(split),
            P(None, split),
            P(None, split),
            P(None, split),
        ),
        out_specs=(P(None, split), P(None, split)),
        check_vma=False,
    )
```

```python
import functools

import jax
import jax.numpy as jnp
import numpy as np
from jax import lax
from jax.experimental import pallas as pl
from jax.experimental.pallas import tpu as pltpu
from jax.sharding import PartitionSpec as P

VARS = 5
SIDE = 3
FACES = 6
LANES = 128
SUB = 8
GROUPS = 8
F32 = jnp.float32
BF16 = jnp.bfloat16


class Sizes:
    def __init__(self, block, columns, levels, slots, curves, slabs):
        self.block = block
        self.columns = columns
        self.levels = levels
        self.slots = slots
        self.curves = curves
        self.slabs = slabs
        self.devices = curves * slabs
        self.trace = VARS * SIDE * SIDE
        self.width = columns // GROUPS
        self.rows = -(-block // GROUPS)
        self.rows_pad = -(-(self.rows + 1) // SUB) * SUB
        self.state_rows = GROUPS * self.rows_pad
        self.block_pad = -(-block // SUB) * SUB
        self.flag = self.trace
        self.wish = self.trace + 1
        self.trace_pad = -(-(self.trace + 3) // 16) * 16
        self.open = self.trace + 2
        self.cuts = LANES // slots
        self.cut_rows = self.trace_pad // self.cuts
        self.tiles = self.cut_rows // 4
        self.table_rows = FACES * self.trace_pad
        self.jac_rows = -(-self.block_pad // 16) * 16
        assert columns == LANES and slabs * slots == LANES
        assert self.tiles * 4 * self.cuts == self.trace_pad and self.open == self.trace_pad - 1
        assert block < self.block_pad


def face_rows():
    nodes = np.arange(VARS * SIDE**3).reshape(VARS, SIDE, SIDE, SIDE)
    last = SIDE - 1
    sides = [
        nodes[:, 0],
        nodes[:, last],
        nodes[:, :, 0],
        nodes[:, :, last],
        nodes[:, :, :, 0],
        nodes[:, :, :, last],
    ]
    return [side.reshape(-1) for side in sides]


def selector(z):
    pick = np.zeros((z.table_rows, z.state_rows), np.float32)
    for face, rows in enumerate(face_rows()):
        for h, i in enumerate(rows):
            pick[face * z.trace_pad + h, i // z.rows * z.rows_pad + i % z.rows] = 1
        pick[face * z.trace_pad + z.flag, z.rows] = 1
    return np.concatenate([pick, pick], axis=1)


def lane_take(values, index):
    index = jnp.broadcast_to(index, values.shape)
    return jnp.take_along_axis(values, index, axis=1, mode="promise_in_bounds")


def lane_iota(rows=SUB):
    return lax.broadcasted_iota(jnp.int32, (rows, LANES), 1)


def halves(values):
    high = values.astype(BF16)
    low = (values - high.astype(F32)).astype(BF16)
    return high, low


def as_column(row):
    return jnp.broadcast_to(row, (LANES, LANES)).T


def dot(a, b):
    return jnp.dot(a, b, preferred_element_type=F32)


def tables_of(state, pick):
    high, low = halves(state)
    return dot(pick, jnp.concatenate([high, low], axis=0))


def fluxes(jac, traces):
    high, low = halves(traces)
    return dot(jac, jnp.concatenate([high, low, high], axis=0))


def pack(z, message, group, curve, out_ref):
    lanes = lane_iota(z.cut_rows)
    target = curve + group - 1

    @pl.when((target >= 0) & (target < z.curves))
    def _():
        parts = [message[cut * z.cut_rows : (cut + 1) * z.cut_rows] for cut in range(z.cuts)]
        for slab in range(z.slabs):
            block = parts[0]
            for cut in range(z.cuts):
                shift = (cut - slab) * z.slots % LANES
                part = pltpu.roll(parts[cut], shift, 1) if shift else parts[cut]
                block = jnp.where(lanes // z.slots == cut, part, block)
            for tile in range(z.tiles):
                out_ref[target * z.slabs + slab, tile] = block[tile * 4 : tile * 4 + 4]


def unpack(z, group, curve, in_ref):
    lanes = lane_iota(z.cut_rows)
    source = jnp.clip(curve + group - 1, 0, z.curves - 1)
    blocks = [
        jnp.concatenate([in_ref[source * z.slabs + slab, tile] for tile in range(z.tiles)], axis=0)
        for slab in range(z.slabs)
    ]
    parts = []
    for cut in range(z.cuts):
        part = blocks[0]
        for slab in range(z.slabs):
            shift = (slab - cut) * z.slots % LANES
            block = pltpu.roll(blocks[slab], shift, 1) if shift else blocks[slab]
            part = jnp.where(lanes // z.slots == slab, block, part)
        parts.append(part)
    return jnp.concatenate(parts, axis=0)


def ghost_take(z, slot_traces, where, face):
    index = jnp.maximum(where[face : face + 1], 0)
    lane = jnp.bitwise_and(index, LANES - 1)
    block = index // LANES
    found = jnp.zeros((z.trace_pad, LANES), F32)
    for group in range(3):
        found = jnp.where(block == group, lane_take(slot_traces[group], lane), found)
    return found


def regroup(z, curve, list_ref, level_ref):
    n = z.columns
    cap = z.slots // z.levels
    stride = z.slabs * cap
    width = z.devices * cap
    lane = lane_iota(1)
    source = lane // z.slots * cap + jnp.bitwise_and(lane, cap - 1)
    own_row = lax.broadcasted_iota(jnp.int32, (z.levels, n), 0) == level_ref[...]
    shift = lax.rem(2 * width - (curve - 1) * stride, width)
    lists = pltpu.roll(list_ref[...], shift, 1)[:, :n]
    rows = []
    for group in range(3):
        taken = lane_take(lists, source + group * stride)
        row = jnp.sum(jnp.where(own_row, taken, 0).astype(F32), axis=0, keepdims=True)
        target = curve + group - 1
        rows.append(jnp.where((target >= 0) & (target < z.curves), row, float(FACES * n)))
    rows.append(jnp.full((SUB - 3, n), float(FACES * n), F32))
    return jnp.concatenate(rows, axis=0).astype(jnp.int32)


def prepare_kernel(
    z,
    curve_ref,
    start_ref,
    dep_ref,
    link_ref,
    weight_ref,
    send_ref,
    recv_ref,
    level_ref,
    pick_ref,
    lifted_ref,
    ints_ref,
    floats_ref,
    sends_ref,
    span_ref,
    table_ref,
    message_ref,
    jac_ref,
    state_ref,
    wide_ref,
):
    wide_ref[...] = jnp.zeros_like(wide_ref)
    for face in range(FACES):
        lifted = lifted_ref[face]
        high = lifted.astype(BF16).astype(F32)
        for part, value in enumerate((high, high, lifted - high)):
            at = part * z.table_rows + face * z.trace_pad
            wide_ref[pl.ds(0, z.block), pl.ds(at, z.trace)] = value
    jac_ref[...] = wide_ref[...].astype(BF16)
    n = z.columns
    lanes = lane_iota()
    dep_row = dep_ref[...]
    dep = jnp.broadcast_to(dep_row, (SUB, n))
    key = (dep_row * n + lane_iota(1)).astype(F32)
    earlier = as_column(key) < jnp.broadcast_to(key, (n, n))
    pos_row = jnp.sum(jnp.where(earlier, 1.0, 0.0), axis=0, keepdims=True)
    here = as_column(pos_row) == lane_iota(n).astype(F32)
    element = lax.broadcasted_iota(jnp.int32, (n, n), 0).astype(F32)
    perm_row = jnp.sum(jnp.where(here, element, 0.0), axis=0, keepdims=True)
    pos = jnp.broadcast_to(pos_row.astype(jnp.int32), (SUB, n))
    perm = jnp.broadcast_to(perm_row.astype(jnp.int32), (SUB, n))
    dep_sorted = lane_take(dep, perm)
    for level in range(z.levels):
        before = jnp.sum(jnp.where(dep_row < level, 1.0, 0.0)).astype(jnp.int32)
        upto = jnp.sum(jnp.where(dep_row <= level, 1.0, 0.0)).astype(jnp.int32)
        span_ref[level] = before // z.width
        span_ref[z.levels + level] = jnp.where(upto > before, (upto + z.width - 1) // z.width, before // z.width)

    link = jnp.concatenate([link_ref[...], jnp.full((SUB - FACES, n), -1, jnp.int32)], axis=0)
    near = jnp.where(link >= 0, lane_take(pos, jnp.maximum(link, 0)), -1)
    near = lane_take(near, perm)
    weight = jnp.concatenate([weight_ref[...], jnp.zeros((SUB - FACES, n), F32)], axis=0)
    weight = lane_take(weight, perm)
    local = near >= 0
    near = jnp.maximum(near, 0)
    dep_near = lane_take(dep_sorted, near)
    zero = jnp.zeros_like(weight)

    send = regroup(z, curve_ref[0], send_ref, level_ref)
    recv = regroup(z, curve_ref[0], recv_ref, level_ref)
    slot_level = jnp.broadcast_to(level_ref[...], (SUB, n))
    rows = []
    slot_id = lax.broadcasted_iota(jnp.int32, (n, n), 0).astype(F32) + 1.0
    columns = [as_column(recv[group : group + 1].astype(F32)) for group in range(3)]
    for face in range(FACES):
        name = (lane_iota(n) + face * n).astype(F32)
        found = jnp.zeros((1, n), F32)
        for group in range(3):
            hit = jnp.where(columns[group] == name, slot_id + float(group * n), 0.0)
            found = jnp.maximum(found, jnp.max(hit, axis=0, keepdims=True))
        rows.append(found)
    rows.append(jnp.zeros((SUB - FACES, n), F32))
    slot = jnp.concatenate(rows, axis=0).astype(jnp.int32) - 1
    slot = lane_take(slot, perm)
    from_far = slot >= 0
    slot = jnp.maximum(slot, 0)
    far_level = lane_take(slot_level, jnp.bitwise_and(slot, n - 1))

    for at, value in enumerate((pos, perm, dep_sorted, near, slot)):
        ints_ref[at] = value
    floats_ref[0] = jnp.where(local & (dep_near < dep_sorted), weight, zero)
    floats_ref[1] = jnp.where(local & (dep_near > dep_sorted), weight, zero)
    floats_ref[2] = jnp.where(local & (dep_near <= dep_sorted), weight, zero)
    floats_ref[3] = jnp.where(local & (dep_near >= dep_sorted), weight, zero)
    floats_ref[4] = jnp.where(from_far & (far_level < dep_sorted), weight, zero)
    floats_ref[5] = jnp.where(from_far, weight, zero)
    floats_ref[6] = jnp.where(from_far & (far_level >= dep_sorted), weight, zero)

    send_element = jnp.bitwise_and(send, n - 1)
    sends_ref[0] = lane_take(pos, send_element)
    sends_ref[1] = send // n
    sends_ref[2] = lane_take(dep, send_element)
    recv_dep = lane_take(dep, jnp.bitwise_and(recv, n - 1))
    wish = jnp.where(slot_level <= recv_dep, 1.0, 0.0)

    state_ref[...] = jnp.zeros_like(state_ref)
    for group in range(GROUPS):
        count = min(z.rows, z.block - group * z.rows)
        state_ref[pl.ds(group * z.rows_pad, count), :] = start_ref[pl.ds(group * z.rows, count), :]
    state_ref[pl.ds(z.rows, 1), :] = jnp.ones((1, n), F32)
    state = lane_take(state_ref[...], perm[0:1])
    table = tables_of(state, pick_ref[...])
    table_ref[...] = table
    message_ref[...] = jnp.zeros_like(message_ref)
    row_id = lax.broadcasted_iota(jnp.int32, (z.trace_pad, n), 0)
    for group in range(3):
        where = sends_ref[0][group : group + 1]
        side = sends_ref[1][group : group + 1]
        message = jnp.zeros((z.trace_pad, n), F32)
        for face in range(FACES):
            piece = table[face * z.trace_pad : (face + 1) * z.trace_pad]
            message = jnp.where(side == face, lane_take(piece, where), message)
        message = jnp.where(row_id == z.wish, wish[group : group + 1], message)
        pack(z, message, group, curve_ref[0], message_ref)


def block_copies(z, ii, inverse_ref, buffer_ref, sems):
    slot = lax.rem(ii, buffer_ref.shape[0])
    for group in range(GROUPS):
        i = jnp.minimum(group * z.rows + ii, z.block - 1)
        yield pltpu.make_async_copy(
            inverse_ref.at[i], buffer_ref.at[slot, group, pl.ds(0, z.block)], sems.at[slot, group]
        )


def chunk_tables(z, ints_ref, floats_ref, near_ref, weights_ref):
    for chunk in range(GROUPS):
        own = chunk * z.width + jnp.bitwise_and(lane_iota(), z.width - 1)
        near_ref[chunk] = lane_take(ints_ref[3], own)
        for at in range(3):
            weights_ref[chunk, at] = lane_take(floats_ref[at], own)


def chunk_copy(ii, chunks_ref, out_ref, sems):
    return pltpu.make_async_copy(chunks_ref.at[:, ii], out_ref.at[:, ii], sems.at[ii])


def arrange_blocks(z, inverse_ref, ints_ref, chunks_ref, out_ref, buffer_ref, sems, out_sems):
    n = z.columns
    perm = ints_ref[1]
    depth = buffer_ref.shape[0]
    orders = [pltpu.roll(perm, group * z.width, 1) if group else perm for group in range(GROUPS)]
    bits = [jnp.bitwise_and(lane_iota() // (z.width << b), 1) == 1 for b in range(3)]

    def row(ii, carry):
        @pl.when(ii + depth - 1 < z.rows)
        def _():
            for copy in block_copies(z, ii + depth - 1, inverse_ref, buffer_ref, sems):
                copy.start()

        for copy in block_copies(z, ii, inverse_ref, buffer_ref, sems):
            copy.wait()
        slot = lax.rem(ii, depth)
        for tile in range(z.block_pad // SUB):
            at = pl.ds(tile * SUB, SUB)
            spread = [lane_take(buffer_ref[slot, group, at, :], orders[group]) for group in range(GROUPS)]
            for b in range(3):
                spread = [
                    jnp.where(bits[b], spread[(x + (1 << b)) % GROUPS], spread[x])
                    for x in range(GROUPS)
                ]
            for chunk in range(GROUPS):
                chunks_ref[chunk, ii, at, :] = spread[-chunk % GROUPS]
        chunk_copy(ii, chunks_ref, out_ref, out_sems).start()
        return carry

    lax.fori_loop(0, z.rows, row, 0)


def blocks_kernel(
    z, inverse_ref, ints_ref, floats_ref, chunks_out, near_ref, weights_ref, buffer_ref, chunks_ref, sems, out_sems
):
    depth = buffer_ref.shape[0]
    buffer_ref[:, :, z.block :, :] = jnp.zeros((depth, GROUPS, z.block_pad - z.block, z.columns), F32)
    for first in range(depth - 1):
        for copy in block_copies(z, first, inverse_ref, buffer_ref, sems):
            copy.start()
    chunk_tables(z, ints_ref, floats_ref, near_ref, weights_ref)
    arrange_blocks(z, inverse_ref, ints_ref, chunks_ref, chunks_out, buffer_ref, sems, out_sems)
    for ii in range(z.rows):
        chunk_copy(ii, chunks_ref, chunks_out, out_sems).wait()


def first_base(z, traces, start_table_ref, ints_ref, floats_ref, right_ref, jac_ref, stack_ref, right_sorted_ref, base_ref):
    n = z.columns
    near = ints_ref[3]
    slot = ints_ref[4]
    for face in range(FACES):
        piece = start_table_ref[pl.ds((face ^ 1) * z.trace_pad, z.trace_pad), :]
        value = lane_take(piece, near[face : face + 1]) * floats_ref[3][face : face + 1]
        ghost = ghost_take(z, traces, slot, face) * floats_ref[6][face : face + 1]
        stack_ref[pl.ds(face * z.trace_pad, z.trace_pad), :] = value + ghost
    flow = fluxes(jac_ref[...], stack_ref[...])[: z.block_pad]
    right = jnp.concatenate([right_ref[...], jnp.zeros((z.block_pad - z.block, n), F32)], axis=0)
    right = lane_take(right, ints_ref[1][0:1])
    right_sorted_ref[...] = right
    base_ref[...] = right - flow


def send_kinds(z, traces, sends_ref, level_ref, kinds_ref):
    for group in range(3):
        wish = traces[group][z.wish : z.wish + 1] > 0.5
        side = sends_ref[1][group : group + 1]
        dep = sends_ref[2][group : group + 1]
        level = level_ref[...]
        kind = jnp.where(wish, jnp.where(dep <= level, 1, 3), jnp.where(dep >= level, 2, 1))
        kinds_ref[pl.ds(group, 1), :] = jnp.where(side < FACES, kind, 0)


def urgent_rows(z, sends_ref, kinds_ref, urgent_ref):
    n = z.columns
    place = lane_iota(n).astype(F32)
    urgent_ref[...] = jnp.zeros_like(urgent_ref)
    for at in range(2):
        found = jnp.zeros((1, n), F32)
        for group in range(3):
            kind = kinds_ref[pl.ds(group, 1), :]
            where = jnp.where(kind == at + 1, sends_ref[0][group : group + 1], -1).astype(F32)
            hit = jnp.where(as_column(where) == place, 1.0, 0.0)
            found = jnp.maximum(found, jnp.max(hit, axis=0, keepdims=True))
        urgent_ref[pl.ds(at, 1), :] = found


def later_bases(z, traces, ints_ref, floats_ref, base_ref, right_ref, jac_ref, wide_ref, forward_base_ref, swept_base_ref):
    n = z.columns
    slot = ints_ref[4]
    missing_forward = jnp.zeros((1, n), F32)
    missing_swept = jnp.zeros((1, n), F32)
    for face in range(FACES):
        ghost = ghost_take(z, traces, slot, face)
        forward_weight = floats_ref[4][face : face + 1]
        swept_weight = floats_ref[5][face : face + 1]
        lost = jnp.where(ghost[z.flag : z.flag + 1] > 0.5, 0.0, 1.0)
        missing_forward += jnp.where(forward_weight > 0, lost, 0.0)
        missing_swept += jnp.where(swept_weight > 0, lost, 0.0)
        at = pl.ds(face * z.trace_pad, z.trace_pad)
        wide_ref[at, pl.ds(0, n)] = ghost * forward_weight
        wide_ref[at, pl.ds(n, n)] = ghost * swept_weight
    flow = fluxes(jac_ref[...], wide_ref[...])
    forward_base_ref[...] = base_ref[...] - flow[: z.block_pad, :n]
    swept_base_ref[...] = right_ref[...] - flow[: z.block_pad, n:]
    forward_base_ref[pl.ds(z.block, 1), :] = missing_forward
    swept_base_ref[pl.ds(z.block, 1), :] = missing_swept
    return missing_forward, missing_swept


def steps(
    z,
    span_ref,
    missing_forward,
    missing_swept,
    ints_ref,
    floats_ref,
    near_ref,
    weights_ref,
    jac_ref,
    pick_ref,
    chunks_ref,
    forward_table_ref,
    swept_table_ref,
    forward_ref,
    swept_ref,
    forward_base,
    swept_base,
    stack_ref,
    part_ref,
    fresh_ref,
    fetch,
    open_ref,
    pending_out,
    pending_in=None,
    urgent_ref=None,
    last=None,
):
    n = z.columns
    near = ints_ref[3]
    dep = ints_ref[2]
    chunk_of = lane_iota(1) // z.width
    per_sum = GROUPS // 2
    part_ref[...] = jnp.where(
        lax.broadcasted_iota(jnp.int32, (z.rows_pad, n), 0) == z.rows, 1.0, 0.0
    )

    def spread(row):
        return jnp.broadcast_to(row, (SUB, n))

    def absent(flags, weights):
        lost = jnp.where(weights > 0, 1.0 - lane_take(flags, near), 0.0)
        return jnp.sum(lost, axis=0, keepdims=True)

    old_forward = spread(forward_table_ref[pl.ds(z.flag, 1), :])
    old_swept = spread(swept_table_ref[pl.ds(z.flag, 1), :])

    def forward_levels():
        forward = old_forward
        for level in range(z.levels):
            missing = absent(forward, floats_ref[0]) + missing_forward
            forward = jnp.where((dep == level) & spread(missing < 0.5), 1.0, forward)
        return forward

    if pending_in is None:
        forward = forward_levels()
    else:
        unfinished = pending_in[0]
        for chunk in range(1, GROUPS):
            unfinished += pending_in[chunk]
        forward = lax.cond(unfinished > 0, forward_levels, lambda: old_forward)
    swept = old_swept
    settled = absent(forward, floats_ref[2]) + missing_swept
    for level in range(z.levels - 1, -1, -1):
        missing = absent(swept, floats_ref[1]) + settled
        swept = jnp.where((dep == level) & spread(missing < 0.5), 1.0, swept)
    shift = (2 * z.width).bit_length() - 1

    def packed_counts(row):
        found = []
        for half in range(2):
            scale = jnp.zeros((1, n), F32)
            for at_chunk in range(per_sum):
                scale = jnp.where(chunk_of == half * per_sum + at_chunk, float((2 * z.width) ** at_chunk), scale)
            found.append(jnp.sum(row * scale).astype(jnp.int32))
        return found

    def unpacked(pair, chunk):
        bits = jnp.where(chunk >= per_sum, pair[1], pair[0])
        bits = lax.shift_right_logical(bits, lax.rem(chunk, per_sum) * shift)
        return jnp.bitwise_and(bits, 2 * z.width - 1)

    counts = []
    urgent = []
    for at, (new, old) in enumerate(((forward, old_forward), (swept, old_swept))):
        fresh = (new - old)[0:1]
        fresh_ref[pl.ds(at, 1), :] = fresh
        counts.append(packed_counts(fresh))
        left = packed_counts(1.0 - old[0:1])
        if urgent_ref is not None:
            urgent.append(packed_counts(fresh * urgent_ref[pl.ds(at, 1), :]))
        for chunk in range(GROUPS):
            pending_out[at * GROUPS + chunk] = unpacked(left, jnp.int32(chunk))

    limits = [jnp.int32(GROUPS - 1), jnp.int32(0)]
    if urgent:
        highest, lowest = jnp.int32(-1), jnp.int32(GROUPS)
        for chunk in range(GROUPS):
            highest = jnp.where(unpacked(urgent[0], jnp.int32(chunk)) > 0, chunk, highest)
        for chunk in reversed(range(GROUPS)):
            lowest = jnp.where(unpacked(urgent[1], jnp.int32(chunk)) > 0, chunk, lowest)
        highest = jnp.where(lowest < GROUPS, GROUPS - 1, highest)
        limits = [jnp.where(last, GROUPS - 1, highest), jnp.where(last, 0, lowest)]

    def step(level, chunk, backward):
        @pl.when(open_ref[chunk] == 1)
        def _():
            fetch(chunk).wait()
            open_ref[chunk] = 2

        old = forward_table_ref
        new = swept_table_ref
        base = swept_base if backward else forward_base
        rows = near_ref[chunk]
        old_weight = weights_ref[chunk, 2 if backward else 0]
        new_weight = weights_ref[chunk, 1]
        own = chunk * z.width + jnp.bitwise_and(lane_iota(1), z.width - 1)
        values = []
        for face in range(FACES):
            at = pl.ds((face ^ 1) * z.trace_pad, z.trace_pad)
            row = rows[face : face + 1]
            value = lane_take(old[at, :], row) * old_weight[face : face + 1]
            if backward:
                value += lane_take(new[at, :], row) * new_weight[face : face + 1]
            values.append(value)
        flow = fluxes(jac_ref[...], jnp.concatenate(values, axis=0))[: z.block_pad]
        rest = lane_take(base[...], own) - flow
        for ii in range(z.rows):
            part_ref[pl.ds(ii, 1), :] = jnp.sum(chunks_ref[chunk, ii] * rest, axis=0, keepdims=True)
        part = part_ref[...]
        state = jnp.concatenate(
            [pltpu.roll(part, -g * z.width % n, 1) if g else part for g in range(GROUPS)], axis=0
        )
        table = tables_of(state, pick_ref[...])
        fresh = fresh_ref[pl.ds(1 if backward else 0, 1), :] > 0.5
        keep = fresh & (chunk_of == chunk) & (dep[0:1] == level)
        out_state = swept_ref if backward else forward_ref
        out_table = swept_table_ref if backward else forward_table_ref
        out_state[...] = jnp.where(keep, state, out_state[...])
        out_table[...] = jnp.where(keep, table, out_table[...])

    for backward in (False, True):

        def run(count, carry, backward=backward):
            level = z.levels - 1 - count if backward else count

            def one(chunk, inner):
                now = chunk >= limits[1] if backward else chunk <= limits[0]

                @pl.when(now & (unpacked(counts[int(backward)], chunk) > 0))
                def _():
                    step(level, chunk, backward)

                return inner

            return lax.fori_loop(span_ref[level], span_ref[z.levels + level], one, carry)

        lax.fori_loop(0, z.levels, run, 0)

    for chunk in range(GROUPS):

        @pl.when(open_ref[chunk] == 1)
        def _(chunk=chunk):
            fetch(chunk).wait()


def start_fetches(fetch, open_ref, pending_ref):
    for chunk in range(GROUPS):
        wanted = True if pending_ref is None else pending_ref[chunk] > 0
        open_ref[chunk] = 0

        @pl.when(wanted)
        def _(chunk=chunk):
            fetch(chunk).start()
            open_ref[chunk] = 1

    if pending_ref is not None:
        for chunk in reversed(range(GROUPS)):

            @pl.when((pending_ref[GROUPS + chunk] > 0) & (open_ref[chunk] == 0))
            def _(chunk=chunk):
                fetch(chunk).start()
                open_ref[chunk] = 1


def send_messages(z, curve, sends_ref, kinds_ref, forward_table_ref, swept_table_ref, message_ref):
    n = z.columns
    row_id = lax.broadcasted_iota(jnp.int32, (z.trace_pad, n), 0)
    messages = []
    still = jnp.zeros((1, n), F32)
    for group in range(3):
        where = sends_ref[0][group : group + 1]
        side = sends_ref[1][group : group + 1]
        kind = kinds_ref[pl.ds(group, 1), :]
        message = jnp.zeros((z.trace_pad, n), F32)
        for face in range(FACES):
            at = pl.ds(face * z.trace_pad, z.trace_pad)
            first = lane_take(forward_table_ref[at, :], where)
            second = lane_take(swept_table_ref[at, :], where)
            picked = jnp.where(kind == 1, first, second)
            message = jnp.where(side == face, picked, message)
        message = jnp.where((kind == 3) & (row_id == z.flag), 2.0, message)
        unsent = (kind > 0) & (message[z.flag : z.flag + 1] < 0.5)
        still = jnp.maximum(still, jnp.where(unsent, 1.0, 0.0))
        messages.append(message)
    still = jnp.broadcast_to(jnp.max(still, axis=1, keepdims=True), (1, n))
    message_ref[...] = jnp.broadcast_to(still[None, None], message_ref.shape)
    for group in range(3):
        message = jnp.where(row_id == z.open, still, messages[group])
        pack(z, message, group, curve, message_ref)


def first_kernel(
    z,
    curve_ref,
    span_ref,
    right_ref,
    level_ref,
    start_table_ref,
    arrived_ref,
    ints_ref,
    floats_ref,
    sends_ref,
    near_ref,
    weights_ref,
    jac_ref,
    pick_ref,
    chunks_in,
    message_ref,
    base_ref,
    right_sorted_ref,
    start_slots_ref,
    kinds_ref,
    urgent_ref,
    pending_out,
    forward_table_ref,
    swept_table_ref,
    forward_ref,
    swept_ref,
    stack_ref,
    part_ref,
    fresh_ref,
    chunks_ref,
    sems,
    open_ref,
):
    n = z.columns
    curve = curve_ref[0]

    def fetch(chunk):
        return pltpu.make_async_copy(chunks_in.at[chunk], chunks_ref.at[chunk], sems.at[chunk])

    start_fetches(fetch, open_ref, None)
    traces = [unpack(z, group, curve, arrived_ref) for group in range(3)]
    for group in range(3):
        start_slots_ref[group] = traces[group]
    send_kinds(z, traces, sends_ref, level_ref, kinds_ref)
    urgent_rows(z, sends_ref, kinds_ref, urgent_ref)
    first_base(
        z, traces, start_table_ref, ints_ref, floats_ref, right_ref, jac_ref, stack_ref, right_sorted_ref, base_ref
    )
    forward_table_ref[...] = jnp.zeros_like(forward_table_ref)
    swept_table_ref[...] = jnp.zeros_like(swept_table_ref)
    forward_ref[...] = jnp.zeros_like(forward_ref)
    swept_ref[...] = jnp.zeros_like(swept_ref)
    missing_forward = jnp.sum(jnp.where(floats_ref[4] > 0, 1.0, 0.0), axis=0, keepdims=True)
    missing_swept = jnp.sum(jnp.where(floats_ref[5] > 0, 1.0, 0.0), axis=0, keepdims=True)
    base_ref[pl.ds(z.block, 1), :] = missing_forward
    right_sorted_ref[pl.ds(z.block, 1), :] = missing_swept
    steps(
        z,
        span_ref,
        missing_forward,
        missing_swept,
        ints_ref,
        floats_ref,
        near_ref,
        weights_ref,
        jac_ref,
        pick_ref,
        chunks_ref,
        forward_table_ref,
        swept_table_ref,
        forward_ref,
        swept_ref,
        base_ref,
        right_sorted_ref,
        stack_ref,
        part_ref,
        fresh_ref,
        fetch,
        open_ref,
        pending_out,
        None,
        urgent_ref,
        False,
    )
    send_messages(z, curve, sends_ref, kinds_ref, forward_table_ref, swept_table_ref, message_ref)


def round_kernel(
    z,
    curve_ref,
    span_ref,
    arrived_ref,
    ints_ref,
    floats_ref,
    sends_ref,
    near_ref,
    weights_ref,
    jac_ref,
    pick_ref,
    chunks_in,
    base_ref,
    right_ref,
    start_slots_ref,
    kinds_ref,
    forward_table_in,
    swept_table_in,
    forward_in,
    swept_in,
    pending_in,
    urgent_ref,
    message_ref,
    more_ref,
    pending_out,
    forward_base_ref,
    swept_base_ref,
    forward_table_ref,
    swept_table_ref,
    forward_ref,
    swept_ref,
    stack_ref,
    part_ref,
    fresh_ref,
    wide_ref,
    chunks_ref,
    sems,
    open_ref,
):
    n = z.columns
    curve = curve_ref[0]

    def fetch(chunk):
        return pltpu.make_async_copy(chunks_in.at[chunk], chunks_ref.at[chunk], sems.at[chunk])

    start_fetches(fetch, open_ref, pending_in)
    forward_table_ref[...] = forward_table_in[...]
    swept_table_ref[...] = swept_table_in[...]
    forward_ref[...] = forward_in[...]
    swept_ref[...] = swept_in[...]
    row_id = lax.broadcasted_iota(jnp.int32, (z.trace_pad, n), 0)
    still = jnp.max(arrived_ref[:, z.tiles - 1, 3:4, :], axis=0)
    still = jnp.where(lane_iota(1) == n - 1, still, 0.0)
    more = jnp.max(still).astype(jnp.int32)
    more_ref[0] = more
    traces = []
    for group in range(3):
        arrived = unpack(z, group, curve, arrived_ref)
        flag = arrived[z.flag : z.flag + 1]
        traces.append(jnp.where((flag > 1.5) & (row_id != z.flag), start_slots_ref[group], arrived))
    missing_forward, missing_swept = later_bases(
        z, traces, ints_ref, floats_ref, base_ref, right_ref, jac_ref, wide_ref, forward_base_ref, swept_base_ref
    )
    steps(
        z,
        span_ref,
        missing_forward,
        missing_swept,
        ints_ref,
        floats_ref,
        near_ref,
        weights_ref,
        jac_ref,
        pick_ref,
        chunks_ref,
        forward_table_ref,
        swept_table_ref,
        forward_ref,
        swept_ref,
        forward_base_ref,
        swept_base_ref,
        stack_ref,
        part_ref,
        fresh_ref,
        fetch,
        open_ref,
        pending_out,
        pending_in,
        urgent_ref,
        more == 0,
    )

    @pl.when(more > 0)
    def _():
        send_messages(z, curve, sends_ref, kinds_ref, forward_table_ref, swept_table_ref, message_ref)


def rest_kernel(
    z,
    span_ref,
    ints_ref,
    floats_ref,
    near_ref,
    weights_ref,
    jac_ref,
    pick_ref,
    chunks_in,
    forward_base_ref,
    swept_base_ref,
    forward_table_in,
    swept_table_in,
    forward_in,
    swept_in,
    pending_in,
    forward_table_ref,
    swept_table_ref,
    forward_ref,
    swept_ref,
    stack_ref,
    part_ref,
    fresh_ref,
    chunks_ref,
    sems,
    open_ref,
    pending_out,
):
    def fetch(chunk):
        return pltpu.make_async_copy(chunks_in.at[chunk], chunks_ref.at[chunk], sems.at[chunk])

    start_fetches(fetch, open_ref, pending_in)
    forward_table_ref[...] = forward_table_in[...]
    swept_table_ref[...] = swept_table_in[...]
    forward_ref[...] = forward_in[...]
    swept_ref[...] = swept_in[...]
    steps(
        z,
        span_ref,
        forward_base_ref[pl.ds(z.block, 1), :],
        swept_base_ref[pl.ds(z.block, 1), :],
        ints_ref,
        floats_ref,
        near_ref,
        weights_ref,
        jac_ref,
        pick_ref,
        chunks_ref,
        forward_table_ref,
        swept_table_ref,
        forward_ref,
        swept_ref,
        forward_base_ref,
        swept_base_ref,
        stack_ref,
        part_ref,
        fresh_ref,
        fetch,
        open_ref,
        pending_out,
        pending_in,
    )


def output_kernel(z, ints_ref, forward_ref, swept_ref, forward_out, swept_out):
    pos = ints_ref[0][0:1]
    for source, target in ((forward_ref, forward_out), (swept_ref, swept_out)):
        for group in range(GROUPS):
            count = min(z.rows, z.block - group * z.rows)
            block = lane_take(source[pl.ds(group * z.rows_pad, z.rows_pad), :], pos)
            target[pl.ds(group * z.rows, count), :] = block[:count]


def call(kernel, outs, inputs, scratch=(), aliases=None, smem_in=(), smem_out=(), hbm_in=(), hbm_out=(), vmem=24):
    whole, smem = pl.BlockSpec(memory_space=pltpu.VMEM), pl.BlockSpec(memory_space=pltpu.SMEM)
    hbm = pl.BlockSpec(memory_space=pltpu.HBM)
    return pl.pallas_call(
        kernel,
        out_shape=outs,
        in_specs=[smem if at in smem_in else hbm if at in hbm_in else whole for at in range(inputs)],
        out_specs=[smem if at in smem_out else hbm if at in hbm_out else whole for at in range(len(outs))],
        scratch_shapes=list(scratch),
        input_output_aliases=aliases or {},
        compiler_params=pltpu.CompilerParams(vmem_limit_bytes=vmem << 20),
    )


def shape(*dims, kind=F32):
    return jax.ShapeDtypeStruct(dims, kind)


def kept(*dims, kind=F32):
    return pltpu.VMEM(dims, kind)


def body(
    start_state,
    right_side,
    block_inverse,
    lifted_flux_jacobian,
    face_weight,
    dep_level,
    face_link,
    send_list,
    recv_list,
):
    curves, slabs = lax.axis_size("curve"), lax.axis_size("slab")
    levels = send_list.shape[0]
    cap = send_list.shape[1] // (curves * slabs)
    slots = levels * cap
    block, n = start_state.shape
    z = Sizes(block, n, levels, slots, curves, slabs)
    own = lax.axis_index("curve").astype(jnp.int32)
    curve = own.reshape(1)

    slot_level = jnp.asarray(
        np.tile(np.repeat(np.arange(levels), cap), slabs).reshape(1, n), jnp.int32
    )
    pick = jnp.asarray(selector(z), BF16)
    ints, floats, sends, span, start_table, message, jac = call(
        functools.partial(prepare_kernel, z),
        [
            kept(5, SUB, n, kind=jnp.int32),
            kept(7, SUB, n),
            kept(3, SUB, n, kind=jnp.int32),
            shape(2 * levels, kind=jnp.int32),
            kept(z.table_rows, n),
            shape(z.devices, z.tiles, 4, n),
            kept(z.jac_rows, 3 * z.table_rows, kind=BF16),
        ],
        10,
        scratch=[pltpu.VMEM((z.state_rows, n), F32), pltpu.VMEM((z.jac_rows, 3 * z.table_rows), F32)],
        smem_in=(0,),
        smem_out=(3,),
        vmem=60,
    )(curve, start_state, dep_level.reshape(1, n), face_link, face_weight, send_list, recv_list, slot_level, pick, lifted_flux_jacobian)

    def exchange(message):
        return lax.all_to_all(message, ("curve", "slab"), 0, 0, tiled=True)

    arrived = exchange(message)
    depth = 6
    chunks, near, weights = call(
        functools.partial(blocks_kernel, z),
        [
            shape(GROUPS, z.rows, z.block_pad, n),
            shape(GROUPS, SUB, n, kind=jnp.int32),
            shape(GROUPS, 3, SUB, n),
        ],
        3,
        scratch=[
            pltpu.VMEM((depth, GROUPS, z.block_pad, n), F32),
            pltpu.VMEM((GROUPS, z.rows, z.block_pad, n), F32),
            pltpu.SemaphoreType.DMA((depth, GROUPS)),
            pltpu.SemaphoreType.DMA((z.rows,)),
        ],
        hbm_in=(0,),
        hbm_out=(0,),
        vmem=48,
    )(block_inverse, ints, floats)
    tables = [
        kept(z.table_rows, n),
        kept(z.table_rows, n),
        kept(z.state_rows, n),
        kept(z.state_rows, n),
    ]
    scratch = [
        pltpu.VMEM((z.table_rows, n), F32),
        pltpu.VMEM((z.rows_pad, n), F32),
        pltpu.VMEM((SUB, n), F32),
    ]
    blocks = [
        pltpu.VMEM((GROUPS, z.rows, z.block_pad, n), F32),
        pltpu.SemaphoreType.DMA((GROUPS,)),
        pltpu.SMEM((GROUPS,), jnp.int32),
    ]
    message, base, right, start_slots, kinds, urgent, pending, *state = call(
        functools.partial(first_kernel, z),
        [
            shape(z.devices, z.tiles, 4, n),
            kept(z.block_pad, n),
            kept(z.block_pad, n),
            kept(3, z.trace_pad, n),
            kept(3, n, kind=jnp.int32),
            kept(SUB, n),
            shape(2 * GROUPS, kind=jnp.int32),
        ]
        + tables,
        14,
        scratch=scratch + blocks,
        smem_in=(0, 1),
        smem_out=(6,),
        hbm_in=(13,),
        vmem=16,
    )(
        curve,
        span,
        right_side,
        slot_level,
        start_table,
        arrived,
        ints,
        floats,
        sends,
        near,
        weights,
        jac,
        pick,
        chunks,
    )

    round_call = call(
        functools.partial(round_kernel, z),
        [
            shape(z.devices, z.tiles, 4, n),
            shape(1, kind=jnp.int32),
            shape(2 * GROUPS, kind=jnp.int32),
            kept(z.block_pad, n),
            kept(z.block_pad, n),
        ]
        + tables,
        21,
        scratch=scratch + [pltpu.VMEM((z.table_rows, 2 * n), F32)] + blocks,
        aliases={15: 5, 16: 6, 17: 7, 18: 8},
        smem_in=(0, 1, 19),
        smem_out=(1, 2),
        hbm_in=(10,),
        vmem=16,
    )

    rest_call = call(
        functools.partial(rest_kernel, z),
        tables,
        15,
        scratch=scratch + blocks + [pltpu.SMEM((2 * GROUPS,), jnp.int32)],
        aliases={10: 0, 11: 1, 12: 2, 13: 3},
        smem_in=(0, 14),
        hbm_in=(7,),
        vmem=16,
    )

    def one_round(carry):
        _, message, pending, bases, state = carry
        arrived = exchange(message)
        state = rest_call(span, ints, floats, near, weights, jac, pick, chunks, *bases, *state, pending)
        message, more, pending, *rest = round_call(
            curve,
            span,
            arrived,
            ints,
            floats,
            sends,
            near,
            weights,
            jac,
            pick,
            chunks,
            base,
            right,
            start_slots,
            kinds,
            *state,
            pending,
            urgent,
        )
        return more[0], message, pending, tuple(rest[:2]), tuple(rest[2:])

    start = (jnp.array(1, jnp.int32), message, pending, (base, right), tuple(state))
    *_, state = lax.while_loop(lambda carry: carry[0] > 0, one_round, start)
    return tuple(
        call(functools.partial(output_kernel, z), [shape(block, n), shape(block, n)], 3)(
            ints, state[2], state[3]
        )
    )


def solution(mesh):
    split = ("curve", "slab")
    return jax.shard_map(
        body,
        mesh=mesh,
        in_specs=(
            P(None, split),
            P(None, split),
            P(None, None, split),
            P(),
            P(None, split),
            P(split),
            P(None, split),
            P(None, split),
            P(None, split),
        ),
        out_specs=(P(None, split), P(None, split)),
        check_vma=False,
    )
```
